32 devices in a mesh: section: 4 (over y, x), ctx: 8 (over z, core).
Axes of the slice: x: 2, y: 2, z: 4, core: 2. Of those that a mesh axis runs over, the one named last changes fastest.
Arguments:
- incoming: bfloat16 [4, 1024, 4096], P('section', 'ctx'), may hold values from -6 to 6
- layer_input: bfloat16 [4, 1024, 4096], P('section', 'ctx'), may hold values from -6 to 6
- pre_gate: bfloat16 [4, 1024, 4096], P('section', 'ctx'), may hold values from -6 to 6
- mid_gate: bfloat16 [4, 1024, 4096], P('section', 'ctx'), may hold values from -6 to 6
- long_gate: bfloat16 [4, 1024, 4096], P('section', 'ctx'), may hold values from -6 to 6
- out_gate: bfloat16 [4, 1024, 4096], P('section', 'ctx'), may hold values from -6 to 6
- long_filter: bfloat16 [4, 4096, 1024], P('section', 'ctx'), may hold values from -0.1875 to 0.1875
- mid_filter: bfloat16 [4, 128, 4096], P('section'), may hold values from -0.5 to 0.5
Outputs:
- input_grad: bfloat16 [4, 1024, 4096], P('section', 'ctx')
- long_grad: bfloat16 [4, 4096, 1024], P('section', 'ctx')
- mid_grad: bfloat16 [4, 128, 4096], P('section', None, 'ctx')
The draws below stay inside these ranges and needn't reach their ends.
All inputs are finite; a program needn't handle non-finite values.
Results may differ from the reference program's by a relative error of at most 0.008.
Values may be sent and summed in bfloat16 or wider, within the bound.
No kernel may reach another device: no remote copies, remote signals or barrier semaphores. Data moves between devices by JAX's collectives and lax.ppermute only.
A program may use at most 192 MiB of HBM per device.

```python
import math
import jax
import jax.numpy as jnp
from jax import lax

D = 4096
KM = 128
SECTIONS = 4
SEQ = 1024


def block_scale(key, shape, cuts, low, high):
    def one(dim, blocks):
        draws = jax.random.uniform(jax.random.fold_in(jax.random.fold_in(key, 6), dim), (blocks,), jnp.float32, low / len(cuts), high / len(cuts))
        return jnp.repeat(jnp.exp(draws), shape[dim] // blocks).reshape((-1,) + (1,) * (len(shape) - dim - 1))

    level = one(*cuts[0])
    for cut in cuts[1:]:
        level = level * one(*cut)
    return level


def centred(stream_key, extent, deviation, reach, split=(), kind=jnp.bfloat16):
    loudness = block_scale(stream_key, extent, split, -0.22, 0.18) if split else 1.0
    array = jax.random.normal(stream_key, extent, jnp.float32) * deviation * loudness
    return jnp.minimum(jnp.maximum(array, -reach), reach).astype(kind)


def setup_inputs(seed: int = 0) -> dict:
    key_list = jax.random.split(jax.random.key(seed), 9)
    incoming = centred(key_list[0], (SECTIONS, SEQ, D), 1.0, 6.0, ((0, 4), (1, 8)))
    layer_input = centred(key_list[1], (SECTIONS, SEQ, D), 1.0, 6.0, ((0, 4), (1, 8)))
    pre_gate = centred(key_list[2], (SECTIONS, SEQ, D), 1.0, 6.0, ((0, 4), (1, 8)))
    mid_gate = centred(key_list[3], (SECTIONS, SEQ, D), 1.0, 6.0, ((0, 4), (1, 8)))
    long_gate = centred(key_list[4], (SECTIONS, SEQ, D), 1.0, 6.0, ((0, 4), (1, 8)))
    out_gate = centred(key_list[5], (SECTIONS, SEQ, D), 1.0, 6.0, ((0, 4), (1, 8)))
    long_filter = centred(key_list[6], (SECTIONS, D, SEQ), SEQ ** -0.5, 0.1875, ((0, 4), (1, 8)))
    mid_filter = centred(key_list[7], (SECTIONS, KM, D), KM ** -0.5, 0.5, ((0, 4),))
    return dict(incoming=incoming, layer_input=layer_input, pre_gate=pre_gate, mid_gate=mid_gate, long_gate=long_gate, out_gate=out_gate, long_filter=long_filter, mid_filter=mid_filter)


def causal_mix(signal, filter_taps):
    padded = jnp.concatenate([jnp.zeros((KM - 1, D), signal.dtype), signal], 0)

    def add_tap(index, total):
        window = lax.dynamic_slice_in_dim(padded, KM - 1 - index, SEQ, 0)
        return total + filter_taps[index].astype(jnp.float32) * window.astype(jnp.float32)

    return lax.fori_loop(0, KM, add_tap, jnp.zeros((SEQ, D), jnp.float32))


def anticausal_mix(signal, filter_taps):
    padded = jnp.concatenate([signal, jnp.zeros((KM - 1, D), signal.dtype)], 0)

    def add_tap(index, total):
        window = lax.dynamic_slice_in_dim(padded, index, SEQ, 0)
        return total + filter_taps[index].astype(jnp.float32) * window.astype(jnp.float32)

    return lax.fori_loop(0, KM, add_tap, jnp.zeros((SEQ, D), jnp.float32))


def tap_sums(grad_b, mixed_in):
    padded = jnp.concatenate([jnp.zeros((KM - 1, D), mixed_in.dtype), mixed_in], 0)

    def one_tap(index):
        window = lax.dynamic_slice_in_dim(padded, KM - 1 - index, SEQ, 0)
        return jnp.sum(grad_b.astype(jnp.float32) * window.astype(jnp.float32), axis=0)

    return lax.map(one_tap, jnp.arange(KM, dtype=jnp.int32))


def long_pass(grad_z, long_in, filt):
    block = math.gcd(D, 256)
    length = 2 * SEQ
    shaped_z = grad_z.T.reshape(D // block, block, SEQ)
    shaped_w = long_in.T.reshape(D // block, block, SEQ)
    shaped_h = filt.reshape(D // block, block, SEQ)

    def one_block(pieces):
        piece_z, piece_w, piece_h = pieces
        spec_z = jnp.fft.rfft(piece_z.astype(jnp.float32), n=length, axis=-1)
        spec_w = jnp.fft.rfft(piece_w.astype(jnp.float32), n=length, axis=-1)
        spec_h = jnp.fft.rfft(piece_h.astype(jnp.float32), n=length, axis=-1)
        lag_grad = jnp.fft.irfft(spec_z * jnp.conj(spec_w), n=length, axis=-1)[:, :SEQ]
        input_part = jnp.fft.irfft(spec_z * jnp.conj(spec_h), n=length, axis=-1)[:, :SEQ]
        return lag_grad, input_part

    lag_grad, input_part = lax.map(one_block, (shaped_z, shaped_w, shaped_h))
    return lag_grad.reshape(D, SEQ), input_part.reshape(D, SEQ).T


def reference(incoming, layer_input, pre_gate, mid_gate, long_gate, out_gate, long_filter, mid_filter):
    beta = (2.0 * SECTIONS) ** -0.5
    scale = float(SEQ) ** -0.5
    input_list, long_list, mid_list = [], [], []
    for section_index in range(SECTIONS):
        adjoint = incoming[(section_index + 1) % SECTIONS].astype(jnp.float32)
        inputs = layer_input[section_index].astype(jnp.float32)
        gate_pre = pre_gate[section_index].astype(jnp.float32)
        gate_mid = mid_gate[section_index].astype(jnp.float32)
        gate_long = long_gate[section_index].astype(jnp.float32)
        gate_out = out_gate[section_index].astype(jnp.float32)
        filter_taps = mid_filter[section_index]
        mixed_in = (inputs * gate_pre).astype(jnp.bfloat16)
        branch = causal_mix(mixed_in, filter_taps)
        resid = inputs + beta * branch * gate_mid
        long_in = (resid * gate_long).astype(jnp.bfloat16)
        grad_z = (beta * adjoint * gate_out).astype(jnp.bfloat16)
        lag_grad, input_part = long_pass(grad_z, long_in, long_filter[section_index])
        long_list.append((lag_grad * scale).astype(jnp.bfloat16))
        grad_w = input_part.astype(jnp.bfloat16)
        grad_u = adjoint + grad_w.astype(jnp.float32) * gate_long
        grad_b = (beta * grad_u * gate_mid).astype(jnp.bfloat16)
        grad_act = anticausal_mix(grad_b, filter_taps)
        input_list.append((grad_u + grad_act * gate_pre).astype(jnp.bfloat16))
        mid_list.append((tap_sums(grad_b, mixed_in) * scale).astype(jnp.bfloat16))
    return (jnp.stack(input_list, 0), jnp.stack(long_list, 0), jnp.stack(mid_list, 0))
```

```python
import functools
import math

import jax
import jax.numpy as jnp
import numpy as np
from jax import lax
from jax.experimental import pallas as pl
from jax.experimental.pallas import tpu as pltpu
from jax.sharding import PartitionSpec as P

BF16 = jnp.bfloat16
F32 = jnp.float32
VMEM_BYTES = 48 * 1024 * 1024


def passed_along(value, axis, steps):
    count = lax.axis_size(axis)
    pairs = [(source, (source + steps) % count) for source in range(count)]
    return lax.ppermute(value, axis, pairs)


def shifted(array, axis, by):
    devices = lax.axis_size(axis)
    pairs = [(i, i + by) for i in range(devices) if 0 <= i + by < devices]
    return lax.ppermute(array, axis, pairs)


def forward_table(period, positions):
    angle = np.pi * np.outer(2 * np.arange(period // 2) + 1, positions) / period
    return np.concatenate([np.cos(angle), -np.sin(angle)], 0).astype(BF16)


def inverse_table(period, positions):
    angle = np.pi * np.outer(positions, 2 * np.arange(period // 2) + 1) / period
    return (np.concatenate([np.cos(angle), -np.sin(angle)], 1) * (2.0 / period)).astype(BF16)


def dot(left, right):
    return jnp.dot(left, right, preferred_element_type=F32)


def dot_nt(left, right):
    return lax.dot_general(left, right, (((1,), (1,)), ((), ())), preferred_element_type=F32)


def times(left, right):
    half = left.shape[0] // 2
    l_re, l_im, r_re, r_im = left[:half], left[half:], right[:half], right[half:]
    return jnp.concatenate(
        [(l_re * r_re - l_im * r_im).astype(BF16), (l_re * r_im + l_im * r_re).astype(BF16)], 0
    )


def times_conj(left, right):
    half = left.shape[0] // 2
    l_re, l_im, r_re, r_im = left[:half], left[half:], right[:half], right[half:]
    return jnp.concatenate(
        [(l_re * r_re + l_im * r_im).astype(BF16), (l_im * r_re - l_re * r_im).astype(BF16)], 0
    )


def put_columns(out_ref, value, start):
    owned = out_ref.shape[2]
    width = value.shape[1]
    if owned >= width:
        out_ref[start // owned, :, start % owned : start % owned + width] = value
    else:
        for j in range(width // owned):
            out_ref[start // owned + j] = value[:, j * owned : (j + 1) * owned]


def get_columns(in_ref, start, width):
    owned = in_ref.shape[2]
    if owned >= width:
        return in_ref[start // owned, :, start % owned : start % owned + width]
    return jnp.concatenate([in_ref[start // owned + j] for j in range(width // owned)], 1)


def mix_kernel(inputs_ref, gate_ref, out_ref):
    out_ref[...] = (inputs_ref[...].astype(F32) * gate_ref[...].astype(F32)).astype(BF16)


def grad_z_kernel(beta, adjoint_ref, gate_ref, out_ref):
    value = beta * adjoint_ref[...].astype(F32) * gate_ref[...].astype(F32)
    put_columns(out_ref, value.astype(BF16), 0)


def branch_kernel(
    beta, step, fwd_ref, inv_ref, earlier_ref, mixed_ref, taps_ref, inputs_ref, mid_ref, long_ref, out_ref
):
    tokens = mixed_ref.shape[0]
    taps = taps_ref.shape[0]
    for start in range(0, mixed_ref.shape[1], step):
        cols = slice(start, start + step)
        signal = dot(fwd_ref[:, :tokens], earlier_ref[:, cols]) + dot(
            fwd_ref[:, tokens:], mixed_ref[:, cols]
        )
        filt = dot(fwd_ref[:, :taps], taps_ref[:, cols])
        branch = dot(inv_ref[...], times(signal, filt))
        resid = inputs_ref[:, cols].astype(F32) + beta * branch * mid_ref[:, cols].astype(F32)
        value = (resid * long_ref[:, cols].astype(F32)).astype(BF16)
        put_columns(out_ref, value, start)


def taps_kernel(
    beta, step, fwd_ref, inv_ref, earlier_ref, mixed_ref, adjoint_ref, grad_w_ref, long_ref, mid_ref,
    grad_b_ref, part_ref,
):
    tokens = mixed_ref.shape[0]
    for start in range(0, mixed_ref.shape[1], step):
        cols = slice(start, start + step)
        grad_w = get_columns(grad_w_ref, start, step).astype(F32)
        grad_u = adjoint_ref[:, cols].astype(F32) + grad_w * long_ref[:, cols].astype(F32)
        grad_b = (beta * grad_u * mid_ref[:, cols].astype(F32)).astype(BF16)
        grad_b_ref[:, cols] = grad_b
        signal = dot(fwd_ref[:, :tokens], earlier_ref[:, cols]) + dot(
            fwd_ref[:, tokens:], mixed_ref[:, cols]
        )
        grad = dot(fwd_ref[:, :tokens], grad_b)
        part = dot(inv_ref[...], times_conj(signal, grad))
        put_columns(part_ref, part.astype(BF16), start)


def input_grad_kernel(
    step, fwd_ref, inv_ref, grad_b_ref, later_ref, taps_ref, adjoint_ref, grad_w_ref, long_ref, pre_ref,
    out_ref,
):
    tokens = grad_b_ref.shape[0]
    taps = taps_ref.shape[0]
    for start in range(0, grad_b_ref.shape[1], step):
        cols = slice(start, start + step)
        grad_w = get_columns(grad_w_ref, start, step).astype(F32)
        grad_u = adjoint_ref[:, cols].astype(F32) + grad_w * long_ref[:, cols].astype(F32)
        signal = dot(fwd_ref[:, :tokens], grad_b_ref[:, cols]) + dot(
            fwd_ref[:, tokens:], later_ref[:, cols]
        )
        filt = dot(fwd_ref[:, :taps], taps_ref[:, cols])
        act = dot(inv_ref[...], times_conj(signal, filt))
        out_ref[:, cols] = (grad_u + act * pre_ref[:, cols].astype(F32)).astype(BF16)


def filter_kernel(blocks, fwd_ref, filt_ref, out_ref):
    size = filt_ref.shape[1] // blocks
    for d in range(blocks):
        piece = dot_nt(fwd_ref[:, size:], filt_ref[:, d * size : (d + 1) * size])
        if d:
            piece += dot_nt(fwd_ref[:, :size], filt_ref[:, (d - 1) * size : d * size])
        out_ref[d] = piece


def correlate(blocks, own_ref, other, joint_ref):
    period, width = joint_ref.shape[1:]
    half = period // 2
    rows, lanes = 16, math.gcd(width, 128) if width % 128 == 0 else width

    def chunk(i, _):
        at = pl.multiple_of(i * rows, rows)
        re, im = pl.ds(at, rows), pl.ds(pl.multiple_of(half + at, rows), rows)
        for start in range(0, width, lanes):
            cols = slice(start, start + lanes)
            own = [(own_ref[q, re, cols], own_ref[q, im, cols]) for q in range(blocks)]
            oth = [(other[d, re, cols], other[d, im, cols]) for d in range(blocks)]
            for p in range(blocks):
                sum_re = sum_im = None
                for q in range(p, blocks):
                    a_re, a_im = own[q]
                    b_re, b_im = oth[q - p]
                    new_re = a_re * b_re + a_im * b_im
                    new_im = a_im * b_re - a_re * b_im
                    sum_re = new_re if sum_re is None else sum_re + new_re
                    sum_im = new_im if sum_im is None else sum_im + new_im
                joint_ref[p, re, cols] = sum_re.astype(BF16)
                joint_ref[p, im, cols] = sum_im.astype(BF16)
        return 0

    lax.fori_loop(0, half // rows, chunk, 0)


def grad_w_kernel(blocks, fwd_ref, inv_ref, grad_ref, filt_ref, out_ref, own_ref, joint_ref):
    size = grad_ref.shape[0] // blocks
    for q in range(blocks):
        own_ref[q] = dot(fwd_ref[:, size:], grad_ref[q * size : (q + 1) * size])
    correlate(blocks, own_ref, filt_ref, joint_ref)
    for p in range(blocks):
        out_ref[p * size : (p + 1) * size] = dot(inv_ref[...], joint_ref[p]).astype(BF16)


def long_grad_kernel(
    blocks, scale, fwd_ref, inv_ref, grad_ref, long_ref, out_ref, own_ref, other_ref, joint_ref
):
    size = grad_ref.shape[0] // blocks
    for q in range(blocks):
        own_ref[q] = dot(fwd_ref[:, size:], grad_ref[q * size : (q + 1) * size])
        other = dot(fwd_ref[:, size:], long_ref[q * size : (q + 1) * size])
        if q:
            other += dot(fwd_ref[:, :size], long_ref[(q - 1) * size : q * size])
        other_ref[q] = other
    correlate(blocks, own_ref, other_ref, joint_ref)
    for p in range(blocks):
        lags = (dot(inv_ref[...], joint_ref[p]) * scale).T
        out_ref[:, p * size : (p + 1) * size] = lags.astype(BF16)


def total_kernel(scale, parts_ref, out_ref):
    total = parts_ref[0].astype(F32)
    for i in range(1, parts_ref.shape[0]):
        total += parts_ref[i].astype(F32)
    out_ref[...] = (total * scale).astype(BF16)


def call(body, grid, ins, outs, args, flops, scratch=(), name=None):
    moved = sum(a.size * a.dtype.itemsize for a in args)
    moved += sum(math.prod(shape) * jnp.dtype(kind).itemsize for shape, kind, _ in outs)
    result = pl.pallas_call(
        body,
        grid=grid,
        in_specs=ins,
        out_specs=[spec for _, _, spec in outs],
        out_shape=[jax.ShapeDtypeStruct(shape, kind) for shape, kind, _ in outs],
        scratch_shapes=list(scratch),
        compiler_params=pltpu.CompilerParams(vmem_limit_bytes=VMEM_BYTES),
        cost_estimate=pl.CostEstimate(flops=flops, bytes_accessed=moved, transcendentals=0),
        name=name,
    )(*args)
    return result[0] if len(result) == 1 else result


def whole_spec(array):
    return pl.BlockSpec(array.shape, lambda i: (0,) * array.ndim)


def per_device(
    incoming, layer_input, pre_gate, mid_gate, long_gate, out_gate, long_filter, mid_filter
):
    sections = lax.axis_size("section")
    devices = lax.axis_size("ctx")
    beta = (2.0 * sections) ** (-0.5)
    tokens, channels = layer_input.shape[1:]
    taps = mid_filter.shape[1]
    seq_len = tokens * devices
    scale = float(seq_len) ** (-0.5)
    owned = channels // devices

    span = tokens + max(tokens, taps)
    fwd = jnp.asarray(forward_table(span, np.arange(span)))
    inv_conv = jnp.asarray(inverse_table(span, tokens + np.arange(tokens)))
    inv_corr = jnp.asarray(inverse_table(span, np.arange(tokens)))
    inv_taps = jnp.asarray(inverse_table(span, tokens - np.arange(taps)))
    size = max(math.gcd(seq_len, 256), seq_len // 8)
    blocks = seq_len // size
    period = 2 * size
    long_fwd = jnp.asarray(forward_table(period, np.arange(-size, size)))
    long_inv = jnp.asarray(inverse_table(period, np.arange(size)))

    wide = max(512, owned)
    step = min(256, wide)
    grid = (channels // wide,)
    rows_spec = pl.BlockSpec((tokens, wide), lambda i: (0, i))
    taps_spec = pl.BlockSpec((taps, wide), lambda i: (0, i))
    major_spec = pl.BlockSpec((wide // owned, tokens, owned), lambda i: (i, 0, 0))
    taps_major = pl.BlockSpec((wide // owned, taps, owned), lambda i: (i, 0, 0))
    rows_shape = (tokens, channels)
    major_shape = (devices, tokens, owned)
    mid_flops = 8 * span * tokens * channels

    tile = math.gcd(owned, 256)
    long_grid = (owned // tile,)
    long_spec = pl.BlockSpec((seq_len, tile), lambda i: (0, i))
    lag_spec = pl.BlockSpec((tile, seq_len), lambda i: (i, 0))
    spectrum_spec = pl.BlockSpec((blocks, period, tile), lambda i: (0, 0, i))
    spectrum = pltpu.VMEM((blocks, period, tile), F32)
    joint = pltpu.VMEM((blocks, period, tile), BF16)
    long_flops = 4 * period * seq_len * owned

    inputs, gate_pre, gate_mid, gate_long, gate_out = (
        array[0] for array in (layer_input, pre_gate, mid_gate, long_gate, out_gate)
    )
    filter_taps = mid_filter[0]

    adjoint = passed_along(incoming[0], "section", -1)
    mixed_in = call(
        mix_kernel, grid, [rows_spec] * 2, [(rows_shape, BF16, rows_spec)], [inputs, gate_pre],
        2 * tokens * channels, name="mix",
    )
    earlier = shifted(mixed_in, "ctx", 1)
    filter_spectrum = call(
        functools.partial(filter_kernel, blocks), long_grid, [whole_spec(long_fwd), lag_spec],
        [((blocks, period, owned), F32, spectrum_spec)], [long_fwd, long_filter[0]], long_flops,
        name="filter",
    )
    grad_z = call(
        functools.partial(grad_z_kernel, beta), grid, [rows_spec] * 2,
        [(major_shape, BF16, major_spec)], [adjoint, gate_out], 2 * tokens * channels, name="gradz",
    )
    long_in = call(
        functools.partial(branch_kernel, beta, step), grid,
        [whole_spec(fwd), whole_spec(inv_conv)] + [rows_spec] * 2 + [taps_spec] + [rows_spec] * 3,
        [(major_shape, BF16, major_spec)],
        [fwd, inv_conv, earlier, mixed_in, filter_taps, inputs, gate_mid, gate_long], mid_flops,
        name="branch",
    )
    channel_z = lax.all_to_all(grad_z, "ctx", split_axis=0, concat_axis=0, tiled=True)
    channel_w = lax.all_to_all(long_in, "ctx", split_axis=0, concat_axis=0, tiled=True)
    channel_z = channel_z.reshape(seq_len, owned)
    channel_w = channel_w.reshape(seq_len, owned)
    grad_w = call(
        functools.partial(grad_w_kernel, blocks), long_grid,
        [whole_spec(long_fwd), whole_spec(long_inv), long_spec, spectrum_spec],
        [((seq_len, owned), BF16, long_spec)], [long_fwd, long_inv, channel_z, filter_spectrum],
        long_flops, [spectrum, joint], name="gradw",
    )
    returned = lax.all_to_all(
        grad_w.reshape(major_shape), "ctx", split_axis=0, concat_axis=0, tiled=True
    )
    long_grad = call(
        functools.partial(long_grad_kernel, blocks, scale), long_grid,
        [whole_spec(long_fwd), whole_spec(long_inv), long_spec, long_spec],
        [((owned, seq_len), BF16, lag_spec)], [long_fwd, long_inv, channel_z, channel_w],
        2 * long_flops, [spectrum, spectrum, joint], name="longgrad",
    )
    grad_b, tap_parts = call(
        functools.partial(taps_kernel, beta, step), grid,
        [whole_spec(fwd), whole_spec(inv_taps)] + [rows_spec] * 3 + [major_spec] + [rows_spec] * 2,
        [(rows_shape, BF16, rows_spec), ((devices, taps, owned), BF16, taps_major)],
        [fwd, inv_taps, earlier, mixed_in, adjoint, returned, gate_long, gate_mid], mid_flops,
        name="taps",
    )
    later = shifted(grad_b, "ctx", -1)
    gathered = lax.all_to_all(tap_parts, "ctx", split_axis=0, concat_axis=0, tiled=True)
    input_grad = call(
        functools.partial(input_grad_kernel, step), grid,
        [whole_spec(fwd), whole_spec(inv_corr)] + [rows_spec] * 2 + [taps_spec, rows_spec, major_spec]
        + [rows_spec] * 2,
        [(rows_shape, BF16, rows_spec)],
        [fwd, inv_corr, grad_b, later, filter_taps, adjoint, returned, gate_long, gate_pre],
        mid_flops, name="inputgrad",
    )
    mid_grad = call(
        functools.partial(total_kernel, scale), (1,), [whole_spec(gathered)],
        [((taps, owned), BF16, pl.BlockSpec((taps, owned), lambda i: (0, 0)))], [gathered],
        devices * taps * owned, name="midgrad",
    )
    return (input_grad[None], long_grad[None], mid_grad[None])


def solution(mesh):
    placed = (
        P("section", "ctx", None),
        P("section", "ctx", None),
        P("section", "ctx", None),
        P("section", "ctx", None),
        P("section", "ctx", None),
        P("section", "ctx", None),
        P("section", "ctx", None),
        P("section", None, None),
    )
    return jax.shard_map(
        per_device,
        mesh=mesh,
        in_specs=placed,
        out_specs=(P("section", "ctx", None), P("section", "ctx", None), P("section", None, "ctx")),
        check_vma=False,
    )
```

```python
import functools
import math

import jax
import jax.numpy as jnp
import numpy as np
from jax import lax
from jax.experimental import pallas as pl
from jax.experimental.pallas import tpu as pltpu
from jax.sharding import PartitionSpec as P

BF16 = jnp.bfloat16
F32 = jnp.float32
VMEM_BYTES = 60 * 1024 * 1024


def passed_along(value, axis, steps):
    count = lax.axis_size(axis)
    pairs = [(source, (source + steps) % count) for source in range(count)]
    return lax.ppermute(value, axis, pairs)


def shifted(array, axis, by):
    devices = lax.axis_size(axis)
    pairs = [(i, i + by) for i in range(devices) if 0 <= i + by < devices]
    return lax.ppermute(array, axis, pairs)


def forward_table(period, positions):
    angle = np.pi * np.outer(2 * np.arange(period // 2) + 1, positions) / period
    return np.concatenate([np.cos(angle), -np.sin(angle)], 0).astype(BF16)


def inverse_table(period, positions):
    angle = np.pi * np.outer(positions, 2 * np.arange(period // 2) + 1) / period
    return (np.concatenate([np.cos(angle), -np.sin(angle)], 1) * (2.0 / period)).astype(BF16)


def dot(left, right):
    return jnp.dot(left, right, preferred_element_type=F32)


def dot_nt(left, right):
    return lax.dot_general(left, right, (((1,), (1,)), ((), ())), preferred_element_type=F32)


def times(left, right):
    half = left.shape[0] // 2
    l_re, l_im, r_re, r_im = left[:half], left[half:], right[:half], right[half:]
    return jnp.concatenate(
        [(l_re * r_re - l_im * r_im).astype(BF16), (l_re * r_im + l_im * r_re).astype(BF16)], 0
    )


def times_conj(left, right):
    half = left.shape[0] // 2
    l_re, l_im, r_re, r_im = left[:half], left[half:], right[:half], right[half:]
    return jnp.concatenate(
        [(l_re * r_re + l_im * r_im).astype(BF16), (l_im * r_re - l_re * r_im).astype(BF16)], 0
    )


def put_columns(out_ref, value, start):
    owned = out_ref.shape[2]
    width = value.shape[1]
    if owned >= width:
        out_ref[start // owned, :, start % owned : start % owned + width] = value
    else:
        for j in range(width // owned):
            out_ref[start // owned + j] = value[:, j * owned : (j + 1) * owned]


def get_columns(in_ref, start, width):
    owned = in_ref.shape[2]
    if owned >= width:
        return in_ref[start // owned, :, start % owned : start % owned + width]
    return jnp.concatenate([in_ref[start // owned + j] for j in range(width // owned)], 1)


def mix_kernel(inputs_ref, gate_ref, out_ref):
    out_ref[...] = (inputs_ref[...].astype(F32) * gate_ref[...].astype(F32)).astype(BF16)


def grad_z_kernel(beta, adjoint_ref, gate_ref, out_ref):
    value = beta * adjoint_ref[...].astype(F32) * gate_ref[...].astype(F32)
    put_columns(out_ref, value.astype(BF16), 0)


def branch_kernel(
    beta, step, fwd_ref, inv_ref, earlier_ref, mixed_ref, taps_ref, inputs_ref, mid_ref, long_ref, out_ref
):
    tokens = mixed_ref.shape[0]
    taps = taps_ref.shape[0]
    for start in range(0, mixed_ref.shape[1], step):
        cols = slice(start, start + step)
        signal = dot(fwd_ref[:, :tokens], earlier_ref[:, cols]) + dot(
            fwd_ref[:, tokens:], mixed_ref[:, cols]
        )
        filt = dot(fwd_ref[:, :taps], taps_ref[:, cols])
        branch = dot(inv_ref[...], times(signal, filt))
        resid = inputs_ref[:, cols].astype(F32) + beta * branch * mid_ref[:, cols].astype(F32)
        value = (resid * long_ref[:, cols].astype(F32)).astype(BF16)
        put_columns(out_ref, value, start)


def taps_kernel(
    beta, step, core_ref, fwd_ref, inv_ref, earlier_ref, mixed_ref, adjoint_ref, grad_w_ref, long_ref,
    mid_ref, grad_b_ref, part_ref,
):
    tokens = mixed_ref.shape[0]
    owned = part_ref.shape[3]
    core = core_ref[0]
    for start in range(0, mixed_ref.shape[1], step):
        cols = slice(start, start + step)
        grad_w = get_columns(grad_w_ref, start, step).astype(F32)
        grad_u = adjoint_ref[:, cols].astype(F32) + grad_w * long_ref[:, cols].astype(F32)
        grad_b = (beta * grad_u * mid_ref[:, cols].astype(F32)).astype(BF16)
        grad_b_ref[:, cols] = grad_b
        signal = dot(fwd_ref[:, :tokens], earlier_ref[:, cols]) + dot(
            fwd_ref[:, tokens:], mixed_ref[:, cols]
        )
        grad = dot(fwd_ref[:, :tokens], grad_b)
        part = dot(inv_ref[...], times_conj(signal, grad)).astype(BF16)
        width = min(owned, step)
        for j in range(0, step, width):
            owner, at = divmod(start + j, owned)
            slot = core if owner % 2 == 0 else 1 - core
            part_ref[slot, owner // 2, :, at : at + width] = part[:, j : j + width]


def input_grad_kernel(
    step, fwd_ref, inv_ref, grad_b_ref, later_ref, taps_ref, adjoint_ref, grad_w_ref, long_ref, pre_ref,
    out_ref,
):
    tokens = grad_b_ref.shape[0]
    taps = taps_ref.shape[0]
    for start in range(0, grad_b_ref.shape[1], step):
        cols = slice(start, start + step)
        grad_w = get_columns(grad_w_ref, start, step).astype(F32)
        grad_u = adjoint_ref[:, cols].astype(F32) + grad_w * long_ref[:, cols].astype(F32)
        signal = dot(fwd_ref[:, :tokens], grad_b_ref[:, cols]) + dot(
            fwd_ref[:, tokens:], later_ref[:, cols]
        )
        filt = dot(fwd_ref[:, :taps], taps_ref[:, cols])
        act = dot(inv_ref[...], times_conj(signal, filt))
        out_ref[:, cols] = (grad_u + act * pre_ref[:, cols].astype(F32)).astype(BF16)


def filter_kernel(blocks, fwd_ref, filt_ref, out_ref):
    size = filt_ref.shape[1] // blocks
    for d in range(blocks):
        piece = dot_nt(fwd_ref[:, size:], filt_ref[:, d * size : (d + 1) * size])
        if d:
            piece += dot_nt(fwd_ref[:, :size], filt_ref[:, (d - 1) * size : d * size])
        out_ref[d] = piece


def correlate(blocks, own_ref, other, joint_ref):
    period, width = joint_ref.shape[1:]
    half = period // 2
    rows, lanes = 16, math.gcd(width, 128) if width % 128 == 0 else width

    def chunk(i, _):
        at = pl.multiple_of(i * rows, rows)
        re, im = pl.ds(at, rows), pl.ds(pl.multiple_of(half + at, rows), rows)
        for start in range(0, width, lanes):
            cols = slice(start, start + lanes)
            own = [(own_ref[q, re, cols], own_ref[q, im, cols]) for q in range(blocks)]
            oth = [(other[d, re, cols], other[d, im, cols]) for d in range(blocks)]
            for p in range(blocks):
                sum_re = sum_im = None
                for q in range(p, blocks):
                    a_re, a_im = own[q]
                    b_re, b_im = oth[q - p]
                    new_re = a_re * b_re + a_im * b_im
                    new_im = a_im * b_re - a_re * b_im
                    sum_re = new_re if sum_re is None else sum_re + new_re
                    sum_im = new_im if sum_im is None else sum_im + new_im
                joint_ref[p, re, cols] = sum_re.astype(BF16)
                joint_ref[p, im, cols] = sum_im.astype(BF16)
        return 0

    lax.fori_loop(0, half // rows, chunk, 0)


def grad_w_kernel(blocks, fwd_ref, inv_ref, grad_ref, filt_ref, out_ref, own_ref, joint_ref):
    size = grad_ref.shape[0] // blocks
    for q in range(blocks):
        own_ref[q] = dot(fwd_ref[:, size:], grad_ref[q * size : (q + 1) * size])
    correlate(blocks, own_ref, filt_ref, joint_ref)
    for p in range(blocks):
        out_ref[p * size : (p + 1) * size] = dot(inv_ref[...], joint_ref[p]).astype(BF16)


def long_grad_kernel(
    blocks, scale, fwd_ref, inv_ref, grad_ref, long_ref, out_ref, own_ref, other_ref, joint_ref
):
    size = grad_ref.shape[0] // blocks
    for q in range(blocks):
        own_ref[q] = dot(fwd_ref[:, size:], grad_ref[q * size : (q + 1) * size])
        other = dot(fwd_ref[:, size:], long_ref[q * size : (q + 1) * size])
        if q:
            other += dot(fwd_ref[:, :size], long_ref[(q - 1) * size : q * size])
        other_ref[q] = other
    correlate(blocks, own_ref, other_ref, joint_ref)
    for p in range(blocks):
        lags = (dot(inv_ref[...], joint_ref[p]) * scale).T
        out_ref[:, p * size : (p + 1) * size] = lags.astype(BF16)


def total_kernel(scale, parts_ref, out_ref):
    total = parts_ref[0].astype(F32)
    for i in range(1, parts_ref.shape[0]):
        total += parts_ref[i].astype(F32)
    out_ref[...] = (total * scale).astype(BF16)


def call(body, grid, ins, outs, args, flops, scratch=(), name=None):
    moved = sum(a.size * a.dtype.itemsize for a in args)
    moved += sum(math.prod(shape) * jnp.dtype(kind).itemsize for shape, kind, _ in outs)
    result = pl.pallas_call(
        body,
        grid=grid,
        in_specs=ins,
        out_specs=[spec for _, _, spec in outs],
        out_shape=[jax.ShapeDtypeStruct(shape, kind) for shape, kind, _ in outs],
        scratch_shapes=list(scratch),
        compiler_params=pltpu.CompilerParams(vmem_limit_bytes=VMEM_BYTES),
        cost_estimate=pl.CostEstimate(flops=flops, bytes_accessed=moved, transcendentals=0),
        name=name,
    )(*args)
    return result[0] if len(result) == 1 else result


def whole_spec(array):
    return pl.BlockSpec(array.shape, lambda i: (0,) * array.ndim)


def per_device(
    incoming, layer_input, pre_gate, mid_gate, long_gate, out_gate, long_filter, mid_filter
):
    sections = lax.axis_size("section")
    devices = lax.axis_size("ctx")
    beta = (2.0 * sections) ** (-0.5)
    tokens, channels = layer_input.shape[1:]
    taps = mid_filter.shape[1]
    seq_len = tokens * devices
    scale = float(seq_len) ** (-0.5)
    owned = channels // devices

    span = tokens + max(tokens, taps)
    fwd = jnp.asarray(forward_table(span, np.arange(span)))
    inv_conv = jnp.asarray(inverse_table(span, tokens + np.arange(tokens)))
    inv_corr = jnp.asarray(inverse_table(span, np.arange(tokens)))
    inv_taps = jnp.asarray(inverse_table(span, tokens - np.arange(taps)))
    size = max(math.gcd(seq_len, 256), seq_len // 8)
    blocks = seq_len // size
    period = 2 * size
    long_fwd = jnp.asarray(forward_table(period, np.arange(-size, size)))
    long_inv = jnp.asarray(inverse_table(period, np.arange(size)))

    wide = max(1024, 2 * owned)
    step = min(256, wide)
    grid = (channels // wide,)
    rows_spec = pl.BlockSpec((tokens, wide), lambda i: (0, i))
    taps_spec = pl.BlockSpec((taps, wide), lambda i: (0, i))
    major_spec = pl.BlockSpec((wide // owned, tokens, owned), lambda i: (i, 0, 0))
    taps_major = pl.BlockSpec((2, wide // owned // 2, taps, owned), lambda i: (0, i, 0, 0))
    rows_shape = (tokens, channels)
    major_shape = (devices, tokens, owned)
    mid_flops = 8 * span * tokens * channels

    tile = math.gcd(owned, 256)
    long_grid = (owned // tile,)
    long_spec = pl.BlockSpec((seq_len, tile), lambda i: (0, i))
    lag_spec = pl.BlockSpec((tile, seq_len), lambda i: (i, 0))
    spectrum_spec = pl.BlockSpec((blocks, period, tile), lambda i: (0, 0, i))
    spectrum = pltpu.VMEM((blocks, period, tile), F32)
    joint = pltpu.VMEM((blocks, period, tile), BF16)
    long_flops = 4 * period * seq_len * owned

    inputs, gate_pre, gate_mid, gate_long, gate_out = (
        array[0] for array in (layer_input, pre_gate, mid_gate, long_gate, out_gate)
    )
    filter_taps = mid_filter[0]

    mixed_in = call(
        mix_kernel, grid, [rows_spec] * 2, [(rows_shape, BF16, rows_spec)], [inputs, gate_pre],
        2 * tokens * channels, name="mix",
    )
    sent, mixed_in = lax.optimization_barrier((incoming[0], mixed_in))
    earlier = shifted(mixed_in, "ctx", 1)
    adjoint = passed_along(sent, "section", -1)
    long_in = call(
        functools.partial(branch_kernel, beta, step), grid,
        [whole_spec(fwd), whole_spec(inv_conv)] + [rows_spec] * 2 + [taps_spec] + [rows_spec] * 3,
        [(major_shape, BF16, major_spec)],
        [fwd, inv_conv, earlier, mixed_in, filter_taps, inputs, gate_mid, gate_long], mid_flops,
        name="branch",
    )
    channel_w = lax.all_to_all(long_in, "ctx", split_axis=0, concat_axis=0, tiled=True)
    adjoint, long_lags, _ = lax.optimization_barrier((adjoint, long_filter[0], long_in))
    grad_z = call(
        functools.partial(grad_z_kernel, beta), grid, [rows_spec] * 2,
        [(major_shape, BF16, major_spec)], [adjoint, gate_out], 2 * tokens * channels, name="gradz",
    )
    filter_spectrum = call(
        functools.partial(filter_kernel, blocks), long_grid, [whole_spec(long_fwd), lag_spec],
        [((blocks, period, owned), F32, spectrum_spec)], [long_fwd, long_lags], long_flops,
        name="filter",
    )
    grad_z, channel_w, filter_spectrum = lax.optimization_barrier((grad_z, channel_w, filter_spectrum))
    channel_z = lax.all_to_all(grad_z, "ctx", split_axis=0, concat_axis=0, tiled=True)
    channel_z = channel_z.reshape(seq_len, owned)
    channel_w = channel_w.reshape(seq_len, owned)
    grad_w = call(
        functools.partial(grad_w_kernel, blocks), long_grid,
        [whole_spec(long_fwd), whole_spec(long_inv), long_spec, spectrum_spec],
        [((seq_len, owned), BF16, long_spec)], [long_fwd, long_inv, channel_z, filter_spectrum],
        long_flops, [spectrum, joint], name="gradw",
    )
    returned = lax.all_to_all(
        grad_w.reshape(major_shape), "ctx", split_axis=0, concat_axis=0, tiled=True
    )
    channel_z, channel_w, _ = lax.optimization_barrier((channel_z, channel_w, grad_w))
    long_grad = call(
        functools.partial(long_grad_kernel, blocks, scale), long_grid,
        [whole_spec(long_fwd), whole_spec(long_inv), long_spec, long_spec],
        [((owned, seq_len), BF16, lag_spec)], [long_fwd, long_inv, channel_z, channel_w],
        2 * long_flops, [spectrum, spectrum, joint], name="longgrad",
    )
    returned, long_grad = lax.optimization_barrier((returned, long_grad))
    core = (lax.axis_index("ctx") % 2).astype(jnp.int32)[None]
    grad_b, tap_parts = call(
        functools.partial(taps_kernel, beta, step), grid,
        [pl.BlockSpec(memory_space=pltpu.SMEM), whole_spec(fwd), whole_spec(inv_taps)]
        + [rows_spec] * 3 + [major_spec] + [rows_spec] * 2,
        [(rows_shape, BF16, rows_spec), ((2, devices // 2, taps, owned), BF16, taps_major)],
        [core, fwd, inv_taps, earlier, mixed_in, adjoint, returned, gate_long, gate_mid], mid_flops,
        name="taps",
    )
    partner = lax.ppermute(tap_parts[1], "ctx", [(i, i ^ 1) for i in range(devices)])
    later = shifted(grad_b, "ctx", -1)
    chip_parts = (tap_parts[0].astype(F32) + partner.astype(F32)).astype(BF16)
    gathered = lax.all_to_all(
        chip_parts, "ctx", split_axis=0, concat_axis=0, tiled=True,
        axis_index_groups=[list(range(c, devices, 2)) for c in range(2)],
    )
    later, _ = lax.optimization_barrier((later, chip_parts))
    input_grad = call(
        functools.partial(input_grad_kernel, step), grid,
        [whole_spec(fwd), whole_spec(inv_corr)] + [rows_spec] * 2 + [taps_spec, rows_spec, major_spec]
        + [rows_spec] * 2,
        [(rows_shape, BF16, rows_spec)],
        [fwd, inv_corr, grad_b, later, filter_taps, adjoint, returned, gate_long, gate_pre],
        mid_flops, name="inputgrad",
    )
    mid_grad = call(
        functools.partial(total_kernel, scale), (1,), [whole_spec(gathered)],
        [((taps, owned), BF16, pl.BlockSpec((taps, owned), lambda i: (0, 0)))], [gathered],
        devices * taps * owned, name="midgrad",
    )
    return (input_grad[None], long_grad[None], mid_grad[None])


def solution(mesh):
    placed = (
        P("section", "ctx", None),
        P("section", "ctx", None),
        P("section", "ctx", None),
        P("section", "ctx", None),
        P("section", "ctx", None),
        P("section", "ctx", None),
        P("section", "ctx", None),
        P("section", None, None),
    )
    return jax.shard_map(
        per_device,
        mesh=mesh,
        in_specs=placed,
        out_specs=(P("section", "ctx", None), P("section", "ctx", None), P("section", None, "ctx")),
        check_vma=False,
    )
```

```python
import functools
import math

import jax
import jax.numpy as jnp
import numpy as np
from jax import lax
from jax.experimental import pallas as pl
from jax.experimental.pallas import tpu as pltpu
from jax.sharding import PartitionSpec as P

BF16 = jnp.bfloat16
F32 = jnp.float32
MIB = 1024 * 1024


def passed_along(value, axis, steps):
    count = lax.axis_size(axis)
    pairs = [(source, (source + steps) % count) for source in range(count)]
    return lax.ppermute(value, axis, pairs)


def shifted(array, axis, by):
    devices = lax.axis_size(axis)
    pairs = [(i, i + by) for i in range(devices) if 0 <= i + by < devices]
    return lax.ppermute(array, axis, pairs)


def forward_table(period, positions):
    angle = np.pi * np.outer(2 * np.arange(period // 2) + 1, positions) / period
    return np.concatenate([np.cos(angle), -np.sin(angle)], 0).astype(BF16)


def inverse_table(period, positions):
    angle = np.pi * np.outer(positions, 2 * np.arange(period // 2) + 1) / period
    return (np.concatenate([np.cos(angle), -np.sin(angle)], 1) * (2.0 / period)).astype(BF16)


def dot(left, right):
    return jnp.dot(left, right, preferred_element_type=F32)


def dot_nt(left, right):
    return lax.dot_general(left, right, (((1,), (1,)), ((), ())), preferred_element_type=F32)


def stacked(*rows):
    return jnp.concatenate(rows, 0)


def times(left, right):
    half = left.shape[0] // 2
    l_re, l_im, r_re, r_im = left[:half], left[half:], right[:half], right[half:]
    return jnp.concatenate(
        [(l_re * r_re - l_im * r_im).astype(BF16), (l_re * r_im + l_im * r_re).astype(BF16)], 0
    )


def times_conj(left, right):
    half = left.shape[0] // 2
    l_re, l_im, r_re, r_im = left[:half], left[half:], right[:half], right[half:]
    return jnp.concatenate(
        [(l_re * r_re + l_im * r_im).astype(BF16), (l_im * r_re - l_re * r_im).astype(BF16)], 0
    )


def put_columns(out_ref, value, start):
    owned = out_ref.shape[2]
    width = value.shape[1]
    if owned >= width:
        out_ref[start // owned, :, start % owned : start % owned + width] = value
    else:
        for j in range(width // owned):
            out_ref[start // owned + j] = value[:, j * owned : (j + 1) * owned]


def get_columns(in_ref, start, width):
    owned = in_ref.shape[2]
    if owned >= width:
        return in_ref[start // owned, :, start % owned : start % owned + width]
    return jnp.concatenate([in_ref[start // owned + j] for j in range(width // owned)], 1)


def mix_kernel(inputs_ref, gate_ref, out_ref):
    out_ref[...] = (inputs_ref[...].astype(F32) * gate_ref[...].astype(F32)).astype(BF16)


def grad_z_kernel(beta, adjoint_ref, gate_ref, out_ref):
    value = beta * adjoint_ref[...].astype(F32) * gate_ref[...].astype(F32)
    put_columns(out_ref, value.astype(BF16), 0)


def branch_kernel(
    beta, step, fwd_ref, inv_ref, earlier_ref, mixed_ref, taps_ref, inputs_ref, mid_ref, long_ref, out_ref
):
    tokens = mixed_ref.shape[0]
    taps = taps_ref.shape[0]
    for start in range(0, mixed_ref.shape[1], step):
        cols = slice(start, start + step)
        signal = dot(fwd_ref[...], stacked(earlier_ref[:, cols], mixed_ref[:, cols]))
        filt = dot(fwd_ref[:, :taps], taps_ref[:, cols])
        branch = dot(inv_ref[...], times(signal, filt))
        resid = inputs_ref[:, cols].astype(F32) + beta * branch * mid_ref[:, cols].astype(F32)
        value = (resid * long_ref[:, cols].astype(F32)).astype(BF16)
        put_columns(out_ref, value, start)


def grad_b_kernel(beta, adjoint_ref, grad_w_ref, long_ref, mid_ref, out_ref):
    grad_w = get_columns(grad_w_ref, 0, out_ref.shape[1]).astype(F32)
    grad_u = adjoint_ref[...].astype(F32) + grad_w * long_ref[...].astype(F32)
    out_ref[...] = (beta * grad_u * mid_ref[...].astype(F32)).astype(BF16)


def taps_kernel(
    step, core_ref, fwd_ref, inv_ref, earlier_ref, mixed_ref, grad_b_ref, keep_ref, send_ref
):
    tokens = mixed_ref.shape[0]
    owned = keep_ref.shape[2]
    width = min(owned, step)

    def put(even_ref, odd_ref, owner, at, value):
        ref = even_ref if owner % 2 == 0 else odd_ref
        ref[owner // 2, :, at : at + width] = value

    for start in range(0, mixed_ref.shape[1], step):
        cols = slice(start, start + step)
        signal = dot(fwd_ref[...], stacked(earlier_ref[:, cols], mixed_ref[:, cols]))
        grad = dot(fwd_ref[:, :tokens], grad_b_ref[:, cols])
        part = dot(inv_ref[...], times_conj(signal, grad)).astype(BF16)
        for j in range(0, step, width):
            owner, at = divmod(start + j, owned)
            value = part[:, j : j + width]
            pl.when(core_ref[0] == 0)(functools.partial(put, keep_ref, send_ref, owner, at, value))
            pl.when(core_ref[0] == 1)(functools.partial(put, send_ref, keep_ref, owner, at, value))


def input_grad_kernel(
    step, fwd_ref, inv_ref, grad_b_ref, later_ref, taps_ref, adjoint_ref, grad_w_ref, long_ref, pre_ref,
    out_ref,
):
    tokens = grad_b_ref.shape[0]
    taps = taps_ref.shape[0]
    for start in range(0, grad_b_ref.shape[1], step):
        cols = slice(start, start + step)
        grad_w = get_columns(grad_w_ref, start, step).astype(F32)
        grad_u = adjoint_ref[:, cols].astype(F32) + grad_w * long_ref[:, cols].astype(F32)
        signal = dot(fwd_ref[...], stacked(grad_b_ref[:, cols], later_ref[:, cols]))
        filt = dot(fwd_ref[:, :taps], taps_ref[:, cols])
        act = dot(inv_ref[...], times_conj(signal, filt))
        out_ref[:, cols] = (grad_u + act * pre_ref[:, cols].astype(F32)).astype(BF16)


def correlate(blocks, own_ref, other, joint_ref):
    period, width = joint_ref.shape[1:]
    half = period // 2
    rows, lanes = 16, math.gcd(width, 128) if width % 128 == 0 else width

    def chunk(i, _):
        at = pl.multiple_of(i * rows, rows)
        re, im = pl.ds(at, rows), pl.ds(pl.multiple_of(half + at, rows), rows)
        for start in range(0, width, lanes):
            cols = slice(start, start + lanes)
            own = [(own_ref[q, re, cols], own_ref[q, im, cols]) for q in range(blocks)]
            oth = [(other[d, re, cols], other[d, im, cols]) for d in range(blocks)]
            for p in range(blocks):
                sum_re = sum_im = None
                for q in range(p, blocks):
                    a_re, a_im = own[q]
                    b_re, b_im = oth[q - p]
                    new_re = a_re * b_re + a_im * b_im
                    new_im = a_im * b_re - a_re * b_im
                    sum_re = new_re if sum_re is None else sum_re + new_re
                    sum_im = new_im if sum_im is None else sum_im + new_im
                joint_ref[p, re, cols] = sum_re.astype(BF16)
                joint_ref[p, im, cols] = sum_im.astype(BF16)
        return 0

    lax.fori_loop(0, half // rows, chunk, 0)


def grad_w_kernel(
    blocks, fwd_ref, inv_ref, grad_ref, filt_ref, out_ref, own_ref, other_ref, joint_ref
):
    size = grad_ref.shape[0] // blocks
    for q in range(blocks):
        own_ref[q] = dot(fwd_ref[:, size:], grad_ref[q * size : (q + 1) * size])
        other = dot_nt(fwd_ref[:, size:], filt_ref[:, q * size : (q + 1) * size])
        if q:
            other += dot_nt(fwd_ref[:, :size], filt_ref[:, (q - 1) * size : q * size])
        other_ref[q] = other
    correlate(blocks, own_ref, other_ref, joint_ref)
    for p in range(blocks):
        out_ref[p * size : (p + 1) * size] = dot(inv_ref[...], joint_ref[p]).astype(BF16)


def long_grad_kernel(
    blocks, scale, fwd_ref, inv_ref, grad_ref, long_ref, out_ref, own_ref, other_ref, joint_ref
):
    size = grad_ref.shape[0] // blocks
    for q in range(blocks):
        own_ref[q] = dot(fwd_ref[:, size:], grad_ref[q * size : (q + 1) * size])
        other = dot(fwd_ref[:, size:], long_ref[q * size : (q + 1) * size])
        if q:
            other += dot(fwd_ref[:, :size], long_ref[(q - 1) * size : q * size])
        other_ref[q] = other
    correlate(blocks, own_ref, other_ref, joint_ref)
    for p in range(blocks):
        lags = (dot(inv_ref[...], joint_ref[p]) * scale).T
        out_ref[:, p * size : (p + 1) * size] = lags.astype(BF16)


def total_kernel(scale, parts_ref, out_ref):
    total = parts_ref[0].astype(F32)
    for i in range(1, parts_ref.shape[0]):
        total += parts_ref[i].astype(F32)
    out_ref[...] = (total * scale).astype(BF16)


def call(body, grid, ins, outs, args, flops, scratch=(), vmem=16, name=None):
    moved = sum(a.size * a.dtype.itemsize for a in args)
    moved += sum(math.prod(shape) * jnp.dtype(kind).itemsize for shape, kind, _ in outs)
    result = pl.pallas_call(
        body,
        grid=grid,
        in_specs=ins,
        out_specs=[spec for _, _, spec in outs],
        out_shape=[jax.ShapeDtypeStruct(shape, kind) for shape, kind, _ in outs],
        scratch_shapes=list(scratch),
        compiler_params=pltpu.CompilerParams(vmem_limit_bytes=vmem * MIB),
        cost_estimate=pl.CostEstimate(flops=flops, bytes_accessed=moved, transcendentals=0),
        name=name,
    )(*args)
    return result[0] if len(result) == 1 else result


def whole_spec(array):
    return pl.BlockSpec(array.shape, lambda i: (0,) * array.ndim)


def per_device(
    incoming, layer_input, pre_gate, mid_gate, long_gate, out_gate, long_filter, mid_filter
):
    sections = lax.axis_size("section")
    devices = lax.axis_size("ctx")
    beta = (2.0 * sections) ** (-0.5)
    tokens, channels = layer_input.shape[1:]
    taps = mid_filter.shape[1]
    seq_len = tokens * devices
    scale = float(seq_len) ** (-0.5)
    owned = channels // devices

    span = tokens + max(tokens, taps)
    fwd = jnp.asarray(forward_table(span, np.arange(span)))
    inv_conv = jnp.asarray(inverse_table(span, tokens + np.arange(tokens)))
    inv_corr = jnp.asarray(inverse_table(span, np.arange(tokens)))
    inv_taps = jnp.asarray(inverse_table(span, tokens - np.arange(taps)))
    size = max(math.gcd(seq_len, 256), seq_len // 8)
    blocks = seq_len // size
    period = 2 * size
    long_fwd = jnp.asarray(forward_table(period, np.arange(-size, size)))
    long_inv = jnp.asarray(inverse_table(period, np.arange(size)))

    wide = max(1024, 2 * owned)
    step = min(256, wide)
    grid = (channels // wide,)
    rows_spec = pl.BlockSpec((tokens, wide), lambda i: (0, i))
    taps_spec = pl.BlockSpec((taps, wide), lambda i: (0, i))
    major_spec = pl.BlockSpec((wide // owned, tokens, owned), lambda i: (i, 0, 0))
    half_major = pl.BlockSpec((wide // owned // 2, taps, owned), lambda i: (i, 0, 0))
    half_shape = (devices // 2, taps, owned)
    rows_shape = (tokens, channels)
    major_shape = (devices, tokens, owned)
    mid_flops = 8 * span * tokens * channels

    tile = math.gcd(owned, 256)
    long_grid = (owned // tile,)
    long_spec = pl.BlockSpec((seq_len, tile), lambda i: (0, i))
    lag_spec = pl.BlockSpec((tile, seq_len), lambda i: (i, 0))
    spectrum = pltpu.VMEM((blocks, period, tile), F32)
    joint = pltpu.VMEM((blocks, period, tile), BF16)
    lanes = -(-tile // 128) * 128
    long_vmem = 2 * (long_fwd.size + long_inv.size) * 2 + 20 * blocks * period * lanes
    long_vmem = -(-long_vmem // MIB) + 6
    long_flops = 4 * period * seq_len * owned

    inputs, gate_pre, gate_mid, gate_long, gate_out = (
        array[0] for array in (layer_input, pre_gate, mid_gate, long_gate, out_gate)
    )
    filter_taps = mid_filter[0]

    adjoint = passed_along(incoming[0], "section", -1)
    mixed_in = call(
        mix_kernel, grid, [rows_spec] * 2, [(rows_shape, BF16, rows_spec)], [inputs, gate_pre],
        2 * tokens * channels, name="mix",
    )
    earlier = shifted(mixed_in, "ctx", 1)
    adjoint, earlier = lax.optimization_barrier((adjoint, earlier))
    grad_z = call(
        functools.partial(grad_z_kernel, beta), grid, [rows_spec] * 2,
        [(major_shape, BF16, major_spec)], [adjoint, gate_out], 2 * tokens * channels, name="gradz",
    )
    grad_z, earlier = lax.optimization_barrier((grad_z, earlier))
    channel_z = lax.all_to_all(grad_z, "ctx", split_axis=0, concat_axis=0, tiled=True)
    long_in = call(
        functools.partial(branch_kernel, beta, step), grid,
        [whole_spec(fwd), whole_spec(inv_conv)] + [rows_spec] * 2 + [taps_spec] + [rows_spec] * 3,
        [(major_shape, BF16, major_spec)],
        [fwd, inv_conv, earlier, mixed_in, filter_taps, inputs, gate_mid, gate_long], mid_flops,
        name="branch",
    )
    channel_z, long_in = lax.optimization_barrier((channel_z, long_in))
    channel_w = lax.all_to_all(long_in, "ctx", split_axis=0, concat_axis=0, tiled=True)
    channel_z = channel_z.reshape(seq_len, owned)
    grad_w = call(
        functools.partial(grad_w_kernel, blocks), long_grid,
        [whole_spec(long_fwd), whole_spec(long_inv), long_spec, lag_spec],
        [((seq_len, owned), BF16, long_spec)], [long_fwd, long_inv, channel_z, long_filter[0]],
        2 * long_flops, [spectrum, spectrum, joint], long_vmem, "gradw",
    )
    grad_w, channel_w = lax.optimization_barrier((grad_w, channel_w))
    returned = lax.all_to_all(
        grad_w.reshape(major_shape), "ctx", split_axis=0, concat_axis=0, tiled=True
    )
    channel_w = channel_w.reshape(seq_len, owned)
    long_grad = call(
        functools.partial(long_grad_kernel, blocks, scale), long_grid,
        [whole_spec(long_fwd), whole_spec(long_inv), long_spec, long_spec],
        [((owned, seq_len), BF16, lag_spec)], [long_fwd, long_inv, channel_z, channel_w],
        2 * long_flops, [spectrum, spectrum, joint], long_vmem, "longgrad",
    )
    returned, long_grad = lax.optimization_barrier((returned, long_grad))
    grad_b = call(
        functools.partial(grad_b_kernel, beta), grid,
        [rows_spec, major_spec] + [rows_spec] * 2, [(rows_shape, BF16, rows_spec)],
        [adjoint, returned, gate_long, gate_mid], 4 * tokens * channels, name="gradb",
    )
    later = shifted(grad_b, "ctx", -1)
    core = (lax.axis_index("ctx") % 2).astype(jnp.int32)[None]
    keep, send = call(
        functools.partial(taps_kernel, step), grid,
        [pl.BlockSpec(memory_space=pltpu.SMEM), whole_spec(fwd), whole_spec(inv_taps)]
        + [rows_spec] * 3,
        [(half_shape, BF16, half_major)] * 2,
        [core, fwd, inv_taps, earlier, mixed_in, grad_b], mid_flops, name="taps",
    )
    partner = lax.ppermute(send, "ctx", [(i, i ^ 1) for i in range(devices)])
    chip_parts = (keep.astype(F32) + partner.astype(F32)).astype(BF16)
    gathered = lax.all_to_all(
        chip_parts, "ctx", split_axis=0, concat_axis=0, tiled=True,
        axis_index_groups=[list(range(c, devices, 2)) for c in range(2)],
    )
    later, _ = lax.optimization_barrier((later, chip_parts))
    input_grad = call(
        functools.partial(input_grad_kernel, step), grid,
        [whole_spec(fwd), whole_spec(inv_corr)] + [rows_spec] * 2 + [taps_spec, rows_spec, major_spec]
        + [rows_spec] * 2,
        [(rows_shape, BF16, rows_spec)],
        [fwd, inv_corr, grad_b, later, filter_taps, adjoint, returned, gate_long, gate_pre],
        mid_flops, name="inputgrad",
    )
    mid_grad = call(
        functools.partial(total_kernel, scale), (1,), [whole_spec(gathered)],
        [((taps, owned), BF16, pl.BlockSpec((taps, owned), lambda i: (0, 0)))], [gathered],
        devices * taps * owned, name="midgrad",
    )
    return (input_grad[None], long_grad[None], mid_grad[None])


def solution(mesh):
    placed = (
        P("section", "ctx", None),
        P("section", "ctx", None),
        P("section", "ctx", None),
        P("section", "ctx", None),
        P("section", "ctx", None),
        P("section", "ctx", None),
        P("section", "ctx", None),
        P("section", None, None),
    )
    return jax.shard_map(
        per_device,
        mesh=mesh,
        in_specs=placed,
        out_specs=(P("section", "ctx", None), P("section", "ctx", None), P("section", None, "ctx")),
        check_vma=False,
    )
```

```python
import functools
import math

import jax
import jax.numpy as jnp
import numpy as np
from jax import lax
from jax.experimental import pallas as pl
from jax.experimental.pallas import tpu as pltpu
from jax.sharding import PartitionSpec as P

BF16 = jnp.bfloat16
F32 = jnp.float32
MIB = 1024 * 1024


def passed_along(value, axis, steps):
    count = lax.axis_size(axis)
    pairs = [(source, (source + steps) % count) for source in range(count)]
    return lax.ppermute(value, axis, pairs)


def shifted(array, axis, by):
    devices = lax.axis_size(axis)
    pairs = [(i, i + by) for i in range(devices) if 0 <= i + by < devices]
    return lax.ppermute(array, axis, pairs)


def forward_table(period, positions):
    angle = np.pi * np.outer(2 * np.arange(period // 2) + 1, positions) / period
    return np.concatenate([np.cos(angle), -np.sin(angle)], 0).astype(BF16)


def inverse_table(period, positions):
    angle = np.pi * np.outer(positions, 2 * np.arange(period // 2) + 1) / period
    return (np.concatenate([np.cos(angle), -np.sin(angle)], 1) * (2.0 / period)).astype(BF16)


def dot(left, right):
    return jnp.dot(left, right, preferred_element_type=F32)


def dot_nt(left, right):
    return lax.dot_general(left, right, (((1,), (1,)), ((), ())), preferred_element_type=F32)


def stacked(*rows):
    return jnp.concatenate(rows, 0)


def times(left, right):
    half = left.shape[0] // 2
    l_re, l_im, r_re, r_im = left[:half], left[half:], right[:half], right[half:]
    return jnp.concatenate(
        [(l_re * r_re - l_im * r_im).astype(BF16), (l_re * r_im + l_im * r_re).astype(BF16)], 0
    )


def times_conj(left, right):
    half = left.shape[0] // 2
    l_re, l_im, r_re, r_im = left[:half], left[half:], right[:half], right[half:]
    return jnp.concatenate(
        [(l_re * r_re + l_im * r_im).astype(BF16), (l_im * r_re - l_re * r_im).astype(BF16)], 0
    )


def put_columns(out_ref, value, start):
    owned = out_ref.shape[2]
    width = value.shape[1]
    if owned >= width:
        out_ref[start // owned, :, start % owned : start % owned + width] = value
    else:
        for j in range(width // owned):
            out_ref[start // owned + j] = value[:, j * owned : (j + 1) * owned]


def get_columns(in_ref, start, width):
    owned = in_ref.shape[2]
    if owned >= width:
        return in_ref[start // owned, :, start % owned : start % owned + width]
    return jnp.concatenate([in_ref[start // owned + j] for j in range(width // owned)], 1)


def mix_kernel(inputs_ref, gate_ref, out_ref):
    out_ref[...] = (inputs_ref[...].astype(F32) * gate_ref[...].astype(F32)).astype(BF16)


def grad_z_kernel(beta, adjoint_ref, gate_ref, out_ref):
    value = beta * adjoint_ref[...].astype(F32) * gate_ref[...].astype(F32)
    put_columns(out_ref, value.astype(BF16), 0)


def branch_kernel(
    beta, step, fwd_ref, inv_ref, earlier_ref, mixed_ref, taps_ref, inputs_ref, mid_ref, long_ref, out_ref
):
    tokens = mixed_ref.shape[0]
    taps = taps_ref.shape[0]
    for start in range(0, mixed_ref.shape[1], step):
        cols = slice(start, start + step)
        signal = dot(fwd_ref[...], stacked(earlier_ref[:, cols], mixed_ref[:, cols]))
        filt = dot(fwd_ref[:, :taps], taps_ref[:, cols])
        branch = dot(inv_ref[...], times(signal, filt))
        resid = inputs_ref[:, cols].astype(F32) + beta * branch * mid_ref[:, cols].astype(F32)
        value = (resid * long_ref[:, cols].astype(F32)).astype(BF16)
        put_columns(out_ref, value, start)


def grad_b_kernel(beta, adjoint_ref, grad_w_ref, long_ref, mid_ref, out_ref):
    grad_w = get_columns(grad_w_ref, 0, out_ref.shape[1]).astype(F32)
    grad_u = adjoint_ref[...].astype(F32) + grad_w * long_ref[...].astype(F32)
    out_ref[...] = (beta * grad_u * mid_ref[...].astype(F32)).astype(BF16)


def taps_kernel(
    step, core_ref, fwd_ref, inv_ref, earlier_ref, mixed_ref, grad_b_ref, keep_ref, send_ref
):
    tokens = mixed_ref.shape[0]
    owned = keep_ref.shape[2]
    width = min(owned, step)

    def put(even_ref, odd_ref, owner, at, value):
        ref = even_ref if owner % 2 == 0 else odd_ref
        ref[owner // 2, :, at : at + width] = value

    for start in range(0, mixed_ref.shape[1], step):
        cols = slice(start, start + step)
        signal = dot(fwd_ref[...], stacked(earlier_ref[:, cols], mixed_ref[:, cols]))
        grad = dot(fwd_ref[:, :tokens], grad_b_ref[:, cols])
        part = dot(inv_ref[...], times_conj(signal, grad)).astype(BF16)
        for j in range(0, step, width):
            owner, at = divmod(start + j, owned)
            value = part[:, j : j + width]
            pl.when(core_ref[0] == 0)(functools.partial(put, keep_ref, send_ref, owner, at, value))
            pl.when(core_ref[0] == 1)(functools.partial(put, send_ref, keep_ref, owner, at, value))


def input_grad_kernel(
    step, fwd_ref, inv_ref, grad_b_ref, later_ref, taps_ref, adjoint_ref, grad_w_ref, long_ref, pre_ref,
    out_ref,
):
    tokens = grad_b_ref.shape[0]
    taps = taps_ref.shape[0]
    for start in range(0, grad_b_ref.shape[1], step):
        cols = slice(start, start + step)
        grad_w = get_columns(grad_w_ref, start, step).astype(F32)
        grad_u = adjoint_ref[:, cols].astype(F32) + grad_w * long_ref[:, cols].astype(F32)
        signal = dot(fwd_ref[...], stacked(grad_b_ref[:, cols], later_ref[:, cols]))
        filt = dot(fwd_ref[:, :taps], taps_ref[:, cols])
        act = dot(inv_ref[...], times_conj(signal, filt))
        out_ref[:, cols] = (grad_u + act * pre_ref[:, cols].astype(F32)).astype(BF16)


def correlate(blocks, own_ref, other, joint_ref):
    period, width = joint_ref.shape[1:]
    half = period // 2
    rows, lanes = 16, math.gcd(width, 128) if width % 128 == 0 else width

    def chunk(i, _):
        at = pl.multiple_of(i * rows, rows)
        re, im = pl.ds(at, rows), pl.ds(pl.multiple_of(half + at, rows), rows)
        for start in range(0, width, lanes):
            cols = slice(start, start + lanes)
            own = [(own_ref[q, re, cols], own_ref[q, im, cols]) for q in range(blocks)]
            oth = [(other[d, re, cols], other[d, im, cols]) for d in range(blocks)]
            for p in range(blocks):
                sum_re = sum_im = None
                for q in range(p, blocks):
                    a_re, a_im = own[q]
                    b_re, b_im = oth[q - p]
                    new_re = a_re * b_re + a_im * b_im
                    new_im = a_im * b_re - a_re * b_im
                    sum_re = new_re if sum_re is None else sum_re + new_re
                    sum_im = new_im if sum_im is None else sum_im + new_im
                joint_ref[p, re, cols] = sum_re.astype(BF16)
                joint_ref[p, im, cols] = sum_im.astype(BF16)
        return 0

    lax.fori_loop(0, half // rows, chunk, 0)


def grad_w_kernel(
    blocks, fwd_ref, inv_ref, grad_ref, filt_ref, out_ref, own_ref, other_ref, joint_ref
):
    size = grad_ref.shape[0] // blocks
    for q in range(blocks):
        own_ref[q] = dot(fwd_ref[:, size:], grad_ref[q * size : (q + 1) * size])
        other = dot_nt(fwd_ref[:, size:], filt_ref[:, q * size : (q + 1) * size])
        if q:
            other += dot_nt(fwd_ref[:, :size], filt_ref[:, (q - 1) * size : q * size])
        other_ref[q] = other
    correlate(blocks, own_ref, other_ref, joint_ref)
    for p in range(blocks):
        out_ref[p * size : (p + 1) * size] = dot(inv_ref[...], joint_ref[p]).astype(BF16)


def long_grad_kernel(
    blocks, scale, fwd_ref, inv_ref, grad_ref, long_ref, out_ref, own_ref, other_ref, joint_ref
):
    size = grad_ref.shape[0] // blocks
    for q in range(blocks):
        own_ref[q] = dot(fwd_ref[:, size:], grad_ref[q * size : (q + 1) * size])
        other = dot(fwd_ref[:, size:], long_ref[q * size : (q + 1) * size])
        if q:
            other += dot(fwd_ref[:, :size], long_ref[(q - 1) * size : q * size])
        other_ref[q] = other
    correlate(blocks, own_ref, other_ref, joint_ref)
    for p in range(blocks):
        lags = (dot(inv_ref[...], joint_ref[p]) * scale).T
        out_ref[:, p * size : (p + 1) * size] = lags.astype(BF16)


def total_kernel(scale, parts_ref, out_ref):
    total = parts_ref[0].astype(F32)
    for i in range(1, parts_ref.shape[0]):
        total += parts_ref[i].astype(F32)
    out_ref[...] = (total * scale).astype(BF16)


def call(body, grid, ins, outs, args, flops, scratch=(), vmem=16, name=None):
    moved = sum(a.size * a.dtype.itemsize for a in args)
    moved += sum(math.prod(shape) * jnp.dtype(kind).itemsize for shape, kind, _ in outs)
    result = pl.pallas_call(
        body,
        grid=grid,
        in_specs=ins,
        out_specs=[spec for _, _, spec in outs],
        out_shape=[jax.ShapeDtypeStruct(shape, kind) for shape, kind, _ in outs],
        scratch_shapes=list(scratch),
        compiler_params=pltpu.CompilerParams(vmem_limit_bytes=vmem * MIB),
        cost_estimate=pl.CostEstimate(flops=flops, bytes_accessed=moved, transcendentals=0),
        name=name,
    )(*args)
    return result[0] if len(result) == 1 else result


def whole_spec(array):
    return pl.BlockSpec(array.shape, lambda i: (0,) * array.ndim)


def by_all_to_all(
    incoming, layer_input, pre_gate, mid_gate, long_gate, out_gate, long_filter, mid_filter
):
    sections = lax.axis_size("section")
    devices = lax.axis_size("ctx")
    beta = (2.0 * sections) ** (-0.5)
    tokens, channels = layer_input.shape[1:]
    taps = mid_filter.shape[1]
    seq_len = tokens * devices
    scale = float(seq_len) ** (-0.5)
    owned = channels // devices

    span = tokens + max(tokens, taps)
    fwd = jnp.asarray(forward_table(span, np.arange(span)))
    inv_conv = jnp.asarray(inverse_table(span, tokens + np.arange(tokens)))
    inv_corr = jnp.asarray(inverse_table(span, np.arange(tokens)))
    inv_taps = jnp.asarray(inverse_table(span, tokens - np.arange(taps)))
    size = max(math.gcd(seq_len, 256), seq_len // 8)
    blocks = seq_len // size
    period = 2 * size
    long_fwd = jnp.asarray(forward_table(period, np.arange(-size, size)))
    long_inv = jnp.asarray(inverse_table(period, np.arange(size)))

    wide = max(1024, 2 * owned)
    step = min(256, wide)
    grid = (channels // wide,)
    rows_spec = pl.BlockSpec((tokens, wide), lambda i: (0, i))
    taps_spec = pl.BlockSpec((taps, wide), lambda i: (0, i))
    major_spec = pl.BlockSpec((wide // owned, tokens, owned), lambda i: (i, 0, 0))
    half_major = pl.BlockSpec((wide // owned // 2, taps, owned), lambda i: (i, 0, 0))
    half_shape = (devices // 2, taps, owned)
    rows_shape = (tokens, channels)
    major_shape = (devices, tokens, owned)
    mid_flops = 8 * span * tokens * channels

    tile = math.gcd(owned, 256)
    long_grid = (owned // tile,)
    long_spec = pl.BlockSpec((seq_len, tile), lambda i: (0, i))
    lag_spec = pl.BlockSpec((tile, seq_len), lambda i: (i, 0))
    spectrum = pltpu.VMEM((blocks, period, tile), F32)
    joint = pltpu.VMEM((blocks, period, tile), BF16)
    lanes = -(-tile // 128) * 128
    long_vmem = 2 * (long_fwd.size + long_inv.size) * 2 + 20 * blocks * period * lanes
    long_vmem = -(-long_vmem // MIB) + 6
    long_flops = 4 * period * seq_len * owned

    inputs, gate_pre, gate_mid, gate_long, gate_out = (
        array[0] for array in (layer_input, pre_gate, mid_gate, long_gate, out_gate)
    )
    filter_taps = mid_filter[0]

    adjoint = passed_along(incoming[0], "section", -1)
    mixed_in = call(
        mix_kernel, grid, [rows_spec] * 2, [(rows_shape, BF16, rows_spec)], [inputs, gate_pre],
        2 * tokens * channels, name="mix",
    )
    earlier = shifted(mixed_in, "ctx", 1)
    adjoint, earlier = lax.optimization_barrier((adjoint, earlier))
    grad_z = call(
        functools.partial(grad_z_kernel, beta), grid, [rows_spec] * 2,
        [(major_shape, BF16, major_spec)], [adjoint, gate_out], 2 * tokens * channels, name="gradz",
    )
    grad_z, earlier = lax.optimization_barrier((grad_z, earlier))
    channel_z = lax.all_to_all(grad_z, "ctx", split_axis=0, concat_axis=0, tiled=True)
    long_in = call(
        functools.partial(branch_kernel, beta, step), grid,
        [whole_spec(fwd), whole_spec(inv_conv)] + [rows_spec] * 2 + [taps_spec] + [rows_spec] * 3,
        [(major_shape, BF16, major_spec)],
        [fwd, inv_conv, earlier, mixed_in, filter_taps, inputs, gate_mid, gate_long], mid_flops,
        name="branch",
    )
    channel_z, long_in = lax.optimization_barrier((channel_z, long_in))
    channel_w = lax.all_to_all(long_in, "ctx", split_axis=0, concat_axis=0, tiled=True)
    channel_z = channel_z.reshape(seq_len, owned)
    grad_w = call(
        functools.partial(grad_w_kernel, blocks), long_grid,
        [whole_spec(long_fwd), whole_spec(long_inv), long_spec, lag_spec],
        [((seq_len, owned), BF16, long_spec)], [long_fwd, long_inv, channel_z, long_filter[0]],
        2 * long_flops, [spectrum, spectrum, joint], long_vmem, "gradw",
    )
    grad_w, channel_w = lax.optimization_barrier((grad_w, channel_w))
    returned = lax.all_to_all(
        grad_w.reshape(major_shape), "ctx", split_axis=0, concat_axis=0, tiled=True
    )
    channel_w = channel_w.reshape(seq_len, owned)
    long_grad = call(
        functools.partial(long_grad_kernel, blocks, scale), long_grid,
        [whole_spec(long_fwd), whole_spec(long_inv), long_spec, long_spec],
        [((owned, seq_len), BF16, lag_spec)], [long_fwd, long_inv, channel_z, channel_w],
        2 * long_flops, [spectrum, spectrum, joint], long_vmem, "longgrad",
    )
    returned, long_grad = lax.optimization_barrier((returned, long_grad))
    grad_b = call(
        functools.partial(grad_b_kernel, beta), grid,
        [rows_spec, major_spec] + [rows_spec] * 2, [(rows_shape, BF16, rows_spec)],
        [adjoint, returned, gate_long, gate_mid], 4 * tokens * channels, name="gradb",
    )
    later = shifted(grad_b, "ctx", -1)
    core = (lax.axis_index("ctx") % 2).astype(jnp.int32)[None]
    keep, send = call(
        functools.partial(taps_kernel, step), grid,
        [pl.BlockSpec(memory_space=pltpu.SMEM), whole_spec(fwd), whole_spec(inv_taps)]
        + [rows_spec] * 3,
        [(half_shape, BF16, half_major)] * 2,
        [core, fwd, inv_taps, earlier, mixed_in, grad_b], mid_flops, name="taps",
    )
    partner = lax.ppermute(send, "ctx", [(i, i ^ 1) for i in range(devices)])
    chip_parts = (keep.astype(F32) + partner.astype(F32)).astype(BF16)
    gathered = lax.all_to_all(
        chip_parts, "ctx", split_axis=0, concat_axis=0, tiled=True,
        axis_index_groups=[list(range(c, devices, 2)) for c in range(2)],
    )
    later, _ = lax.optimization_barrier((later, chip_parts))
    input_grad = call(
        functools.partial(input_grad_kernel, step), grid,
        [whole_spec(fwd), whole_spec(inv_corr)] + [rows_spec] * 2 + [taps_spec, rows_spec, major_spec]
        + [rows_spec] * 2,
        [(rows_shape, BF16, rows_spec)],
        [fwd, inv_corr, grad_b, later, filter_taps, adjoint, returned, gate_long, gate_pre],
        mid_flops, name="inputgrad",
    )
    mid_grad = call(
        functools.partial(total_kernel, scale), (1,), [whole_spec(gathered)],
        [((taps, owned), BF16, pl.BlockSpec((taps, owned), lambda i: (0, 0)))], [gathered],
        devices * taps * owned, name="midgrad",
    )
    return (input_grad[None], long_grad[None], mid_grad[None])


def columns(index, width):
    return pl.ds(pl.multiple_of(index * width, width), width)


def pick_kernel(me_ref, in_ref, near_ref, far_ref):
    half, width = me_ref[1], near_ref.shape[1]
    near_ref[...] = in_ref[:, columns(half, width)]
    far_ref[...] = in_ref[:, columns(1 - half, width)]


def pieces_z_kernel(beta, first, me_ref, adjoint_ref, gate_ref, *out_refs):
    count = len(out_refs)
    width = out_refs[0].shape[1]
    me = me_ref[0]
    for k in range(count):
        owner = me ^ (first + k)
        part = adjoint_ref[:, columns(owner & (count - 1), width)].astype(F32)
        gate = gate_ref[:, columns(owner, width)].astype(F32)
        out_refs[k][...] = (beta * part * gate).astype(BF16)


def pieces_branch_kernel(
    beta, me_ref, fwd_ref, inv_ref, earlier_ref, mixed_ref, taps_ref, inputs_ref, mid_ref, long_ref,
    signal_ref, filt_ref, *out_refs,
):
    taps = taps_ref.shape[0]
    width = out_refs[0].shape[1]
    me = me_ref[0]
    count = len(out_refs)
    for k in list(range(count // 2, count)) + list(range(count // 2)):
        cols = columns(me ^ k, width)
        signal = dot(fwd_ref[...], stacked(earlier_ref[:, cols], mixed_ref[:, cols]))
        filt = dot(fwd_ref[:, :taps], taps_ref[:, cols])
        signal_ref[:, cols] = signal.astype(BF16)
        filt_ref[:, cols] = filt.astype(BF16)
        branch = dot(inv_ref[...], times(signal, filt))
        resid = inputs_ref[:, cols].astype(F32) + beta * branch * mid_ref[:, cols].astype(F32)
        out_refs[k][...] = (resid * long_ref[:, cols].astype(F32)).astype(BF16)


def spectra(blocks, fwd_ref, array_ref, cols, out_ref):
    size = array_ref.shape[0] // blocks
    for q in range(blocks):
        out_ref[q] = dot(fwd_ref[:, size:], array_ref[q * size : (q + 1) * size, cols])


def extended_spectra(blocks, fwd_ref, array_ref, cols, out_ref):
    size = array_ref.shape[0] // blocks
    out_ref[0] = dot(fwd_ref[:, size:], array_ref[:size, cols])
    for q in range(1, blocks):
        out_ref[q] = dot(fwd_ref[...], array_ref[(q - 1) * size : (q + 1) * size, cols])


def pieces_grad_w_kernel(blocks, count, me_ref, fwd_ref, inv_ref, filt_ref, *refs):
    piece_refs, out_refs = refs[:count], refs[count : 2 * count]
    whole_ref, own_ref, other_ref, joint_ref, result_ref = refs[2 * count :]
    rows = piece_refs[0].shape[0]
    size = whole_ref.shape[0] // blocks
    tile = joint_ref.shape[2]
    me = me_ref[0]
    for k in range(count):
        whole_ref[columns(me ^ k, rows), :] = piece_refs[k][...]
    for start in range(0, whole_ref.shape[1], tile):
        cols = slice(start, start + tile)
        spectra(blocks, fwd_ref, whole_ref, cols, own_ref)
        other_ref[0] = dot_nt(fwd_ref[:, size:], filt_ref[cols, :size])
        for q in range(1, blocks):
            other_ref[q] = dot_nt(fwd_ref[...], filt_ref[cols, (q - 1) * size : (q + 1) * size])
        correlate(blocks, own_ref, other_ref, joint_ref)
        for p in range(blocks):
            result_ref[p * size : (p + 1) * size, cols] = dot(inv_ref[...], joint_ref[p]).astype(BF16)
    for k in range(count):
        out_refs[k][...] = result_ref[columns(me ^ k, rows), :]


def pieces_long_grad_kernel(blocks, scale, count, me_ref, fwd_ref, inv_ref, grad_ref, *refs):
    piece_refs, out_ref = refs[:count], refs[count]
    own_ref, other_ref, joint_ref, whole_ref = refs[count + 1 :]
    rows = piece_refs[0].shape[0]
    size = whole_ref.shape[0] // blocks
    tile = joint_ref.shape[2]
    me = me_ref[0]
    for k in range(count):
        whole_ref[columns(me ^ k, rows), :] = piece_refs[k][...]
    for start in range(0, whole_ref.shape[1], tile):
        cols = slice(start, start + tile)
        spectra(blocks, fwd_ref, grad_ref, cols, own_ref)
        extended_spectra(blocks, fwd_ref, whole_ref, cols, other_ref)
        correlate(blocks, own_ref, other_ref, joint_ref)
        for p in range(blocks):
            lags = (dot(inv_ref[...], joint_ref[p]) * scale).T
            out_ref[cols, p * size : (p + 1) * size] = lags.astype(BF16)


def pieces_grad_b_kernel(beta, count, me_ref, near_ref, far_ref, long_ref, mid_ref, *refs):
    piece_refs, (grad_u_ref, grad_b_ref) = refs[:count], refs[count:]
    width = piece_refs[0].shape[1]
    half = count // 2
    me = me_ref[0]
    for k in range(count):
        owner = me ^ k
        cols = columns(owner, width)
        adjoint_ref = near_ref if k < half else far_ref
        adjoint = adjoint_ref[:, columns(owner & (half - 1), width)].astype(F32)
        grad_u = adjoint + piece_refs[k][...].astype(F32) * long_ref[:, cols].astype(F32)
        grad_u_ref[:, cols] = grad_u
        grad_b_ref[:, cols] = (beta * grad_u * mid_ref[:, cols].astype(F32)).astype(BF16)


def pieces_taps_kernel(me_ref, fwd_ref, inv_ref, signal_ref, grad_b_ref, keep_ref, send_ref):
    tokens = grad_b_ref.shape[0]
    width = keep_ref.shape[2]
    me = me_ref[0]
    for k in range(2 * keep_ref.shape[0]):
        cols = columns(me ^ k, width)
        grad = dot(fwd_ref[:, :tokens], grad_b_ref[:, cols])
        part = dot(inv_ref[...], times_conj(signal_ref[:, cols].astype(F32), grad)).astype(BF16)
        (send_ref if k % 2 else keep_ref)[k // 2] = part


def pair_kernel(keep_ref, came_ref, *out_refs):
    for m, out_ref in enumerate(out_refs):
        out_ref[...] = (keep_ref[m].astype(F32) + came_ref[m].astype(F32)).astype(BF16)


def pieces_total_kernel(scale, *refs):
    total = refs[0][...].astype(F32)
    for ref in refs[1:-1]:
        total += ref[...].astype(F32)
    refs[-1][...] = (total * scale).astype(BF16)


def pieces_input_grad_kernel(
    step, fwd_ref, inv_ref, grad_b_ref, later_ref, filt_ref, grad_u_ref, pre_ref, out_ref
):
    for start in range(0, grad_b_ref.shape[1], step):
        cols = slice(start, start + step)
        signal = dot(fwd_ref[...], stacked(grad_b_ref[:, cols], later_ref[:, cols]))
        act = dot(inv_ref[...], times_conj(signal, filt_ref[:, cols].astype(F32)))
        value = grad_u_ref[:, cols] + act * pre_ref[:, cols].astype(F32)
        out_ref[:, cols] = value.astype(BF16)


def local(body, outs, args, flops, scratch=(), vmem=24, name=None):
    moved = sum(a.size * a.dtype.itemsize for a in args)
    moved += sum(math.prod(shape) * jnp.dtype(kind).itemsize for shape, kind in outs)
    specs = [
        pl.BlockSpec(memory_space=pltpu.SMEM if a.dtype == jnp.int32 else pltpu.VMEM) for a in args
    ]
    result = pl.pallas_call(
        body,
        in_specs=specs,
        out_specs=[pl.BlockSpec(memory_space=pltpu.VMEM) for _ in outs],
        out_shape=[jax.ShapeDtypeStruct(shape, kind) for shape, kind in outs],
        scratch_shapes=list(scratch),
        compiler_params=pltpu.CompilerParams(vmem_limit_bytes=vmem * MIB),
        cost_estimate=pl.CostEstimate(flops=flops, bytes_accessed=moved, transcendentals=0),
        name=name,
    )(*args)
    return result[0] if len(result) == 1 else result


def swapped(array, k):
    count = lax.axis_size("ctx")
    return lax.ppermute(array, "ctx", [(i, i ^ k) for i in range(count)])


def exchanged(pieces, step=1):
    came = [pieces[0]] + [None] * (len(pieces) - 1)
    for k in range(len(pieces) - 1, 0, -1):
        came[k] = swapped(pieces[k], k * step)
    return came


def by_permutes(
    incoming, layer_input, pre_gate, mid_gate, long_gate, out_gate, long_filter, mid_filter
):
    sections = lax.axis_size("section")
    devices = lax.axis_size("ctx")
    half = devices // 2
    beta = (2.0 * sections) ** (-0.5)
    tokens, channels = layer_input.shape[1:]
    taps = mid_filter.shape[1]
    seq_len = tokens * devices
    scale = float(seq_len) ** (-0.5)
    owned = channels // devices

    span = tokens + max(tokens, taps)
    fwd = jnp.asarray(forward_table(span, np.arange(span)))
    inv_conv = jnp.asarray(inverse_table(span, tokens + np.arange(tokens)))
    inv_corr = jnp.asarray(inverse_table(span, np.arange(tokens)))
    inv_taps = jnp.asarray(inverse_table(span, tokens - np.arange(taps)))
    size = max(math.gcd(seq_len, 256), seq_len // 8)
    blocks = seq_len // size
    period = 2 * size
    long_fwd = jnp.asarray(forward_table(period, np.arange(-size, size)))
    long_inv = jnp.asarray(inverse_table(period, np.arange(size)))
    tile = math.gcd(owned, 256)
    spectrum = pltpu.VMEM((blocks, period, tile), F32)
    joint = pltpu.VMEM((blocks, period, tile), BF16)
    staged = pltpu.VMEM((seq_len, owned), BF16)

    rows_shape = ((tokens, channels), BF16)
    half_shape = ((tokens, channels // 2), BF16)
    piece = ((tokens, owned), BF16)
    tap_piece = ((taps, owned), BF16)
    mid_flops = 8 * span * tokens * channels
    long_flops = 12 * period * seq_len * owned
    few = 4 * tokens * channels

    index = lax.axis_index("ctx")
    me = jnp.stack([index, index // half]).astype(jnp.int32)
    inputs, gate_pre, gate_mid, gate_long, gate_out = (
        array[0] for array in (layer_input, pre_gate, mid_gate, long_gate, out_gate)
    )
    filter_taps = mid_filter[0]

    near, far = local(pick_kernel, [half_shape] * 2, [me, incoming[0]], few, name="pick")
    far = passed_along(far, "section", -1)
    near = passed_along(near, "section", -1)
    mixed_in = local(mix_kernel, [rows_shape], [inputs, gate_pre], few, name="mix")
    earlier = shifted(mixed_in, "ctx", 1)
    far_z = local(
        functools.partial(pieces_z_kernel, beta, half), [piece] * half, [me, far, gate_out], few, name="farz"
    )
    near_z = local(
        functools.partial(pieces_z_kernel, beta, 0), [piece] * half, [me, near, gate_out], few, name="nearz"
    )
    signal, filt, *pieces_w = local(
        functools.partial(pieces_branch_kernel, beta),
        [((span, channels), BF16)] * 2 + [piece] * devices,
        [me, fwd, inv_conv, earlier, mixed_in, filter_taps, inputs, gate_mid, gate_long], mid_flops,
        name="branch",
    )
    pieces_z = exchanged(list(near_z) + list(far_z))
    pieces_w = exchanged(pieces_w)
    *pieces_g, channel_z = local(
        functools.partial(pieces_grad_w_kernel, blocks, devices),
        [piece] * devices + [((seq_len, owned), BF16)],
        [me, long_fwd, long_inv, long_filter[0], *pieces_z], long_flops,
        [spectrum, spectrum, joint, staged], name="gradw",
    )
    pieces_g = exchanged(pieces_g)
    long_grad = local(
        functools.partial(pieces_long_grad_kernel, blocks, scale, devices), [((owned, seq_len), BF16)],
        [me, long_fwd, long_inv, channel_z, *pieces_w], long_flops,
        [spectrum, spectrum, joint, staged], name="longgrad",
    )
    pieces_g, long_grad = lax.optimization_barrier((pieces_g, long_grad))
    grad_u, grad_b = local(
        functools.partial(pieces_grad_b_kernel, beta, devices), [((tokens, channels), F32), rows_shape],
        [me, near, far, gate_long, gate_mid, *pieces_g], few, name="gradb",
    )
    later = shifted(grad_b, "ctx", -1)
    keep, send = local(
        pieces_taps_kernel, [((half, taps, owned), BF16)] * 2, [me, fwd, inv_taps, signal, grad_b],
        mid_flops, name="taps",
    )
    sums = local(pair_kernel, [tap_piece] * half, [keep, swapped(send, 1)], few, name="pair")
    sums = exchanged(list(sums), 2)
    later, _ = lax.optimization_barrier((later, sums[0]))
    input_grad = local(
        functools.partial(pieces_input_grad_kernel, 512), [rows_shape],
        [fwd, inv_corr, grad_b, later, filt, grad_u, gate_pre], mid_flops, name="inputgrad",
    )
    mid_grad = local(functools.partial(pieces_total_kernel, scale), [tap_piece], sums, few, name="midgrad")
    return (input_grad[None], long_grad[None], mid_grad[None])


def per_device(*arrays):
    devices = lax.axis_size("ctx")
    owned = arrays[0].shape[2] // devices
    if owned % 128 == 0 and devices in (2, 4, 8, 16):
        return by_permutes(*arrays)
    return by_all_to_all(*arrays)


def solution(mesh):
    placed = (
        P("section", "ctx", None),
        P("section", "ctx", None),
        P("section", "ctx", None),
        P("section", "ctx", None),
        P("section", "ctx", None),
        P("section", "ctx", None),
        P("section", "ctx", None),
        P("section", None, None),
    )
    return jax.shard_map(
        per_device,
        mesh=mesh,
        in_specs=placed,
        out_specs=(P("section", "ctx", None), P("section", "ctx", None), P("section", None, "ctx")),
        check_vma=False,
    )
```

```python
import functools
import math

import jax
import jax.numpy as jnp
import numpy as np
from jax import lax
from jax.experimental import pallas as pl
from jax.experimental.pallas import tpu as pltpu
from jax.sharding import PartitionSpec as P

BF16 = jnp.bfloat16
F32 = jnp.float32
MIB = 1024 * 1024


def passed_along(value, axis, steps):
    count = lax.axis_size(axis)
    pairs = [(source, (source + steps) % count) for source in range(count)]
    return lax.ppermute(value, axis, pairs)


def shifted(array, axis, by):
    devices = lax.axis_size(axis)
    pairs = [(i, i + by) for i in range(devices) if 0 <= i + by < devices]
    return lax.ppermute(array, axis, pairs)


def forward_table(period, positions):
    angle = np.pi * np.outer(2 * np.arange(period // 2) + 1, positions) / period
    return np.concatenate([np.cos(angle), -np.sin(angle)], 0).astype(BF16)


def inverse_table(period, positions):
    angle = np.pi * np.outer(positions, 2 * np.arange(period // 2) + 1) / period
    return (np.concatenate([np.cos(angle), -np.sin(angle)], 1) * (2.0 / period)).astype(BF16)


def dot(left, right):
    return jnp.dot(left, right, preferred_element_type=F32)


def dot_nt(left, right):
    return lax.dot_general(left, right, (((1,), (1,)), ((), ())), preferred_element_type=F32)


def stacked(*rows):
    return jnp.concatenate(rows, 0)


def times(left, right):
    half = left.shape[0] // 2
    l_re, l_im, r_re, r_im = left[:half], left[half:], right[:half], right[half:]
    return jnp.concatenate(
        [(l_re * r_re - l_im * r_im).astype(BF16), (l_re * r_im + l_im * r_re).astype(BF16)], 0
    )


def times_conj(left, right):
    half = left.shape[0] // 2
    l_re, l_im, r_re, r_im = left[:half], left[half:], right[:half], right[half:]
    return jnp.concatenate(
        [(l_re * r_re + l_im * r_im).astype(BF16), (l_im * r_re - l_re * r_im).astype(BF16)], 0
    )


def put_columns(out_ref, value, start):
    owned = out_ref.shape[2]
    width = value.shape[1]
    if owned >= width:
        out_ref[start // owned, :, start % owned : start % owned + width] = value
    else:
        for j in range(width // owned):
            out_ref[start // owned + j] = value[:, j * owned : (j + 1) * owned]


def get_columns(in_ref, start, width):
    owned = in_ref.shape[2]
    if owned >= width:
        return in_ref[start // owned, :, start % owned : start % owned + width]
    return jnp.concatenate([in_ref[start // owned + j] for j in range(width // owned)], 1)


def mix_kernel(inputs_ref, gate_ref, out_ref):
    out_ref[...] = (inputs_ref[...].astype(F32) * gate_ref[...].astype(F32)).astype(BF16)


def grad_z_kernel(beta, adjoint_ref, gate_ref, out_ref):
    value = beta * adjoint_ref[...].astype(F32) * gate_ref[...].astype(F32)
    put_columns(out_ref, value.astype(BF16), 0)


def branch_kernel(
    beta, step, fwd_ref, inv_ref, earlier_ref, mixed_ref, taps_ref, inputs_ref, mid_ref, long_ref, out_ref
):
    tokens = mixed_ref.shape[0]
    taps = taps_ref.shape[0]
    for start in range(0, mixed_ref.shape[1], step):
        cols = slice(start, start + step)
        signal = dot(fwd_ref[...], stacked(earlier_ref[:, cols], mixed_ref[:, cols]))
        filt = dot(fwd_ref[:, :taps], taps_ref[:, cols])
        branch = dot(inv_ref[...], times(signal, filt))
        resid = inputs_ref[:, cols].astype(F32) + beta * branch * mid_ref[:, cols].astype(F32)
        value = (resid * long_ref[:, cols].astype(F32)).astype(BF16)
        put_columns(out_ref, value, start)


def grad_b_kernel(beta, adjoint_ref, grad_w_ref, long_ref, mid_ref, out_ref):
    grad_w = get_columns(grad_w_ref, 0, out_ref.shape[1]).astype(F32)
    grad_u = adjoint_ref[...].astype(F32) + grad_w * long_ref[...].astype(F32)
    out_ref[...] = (beta * grad_u * mid_ref[...].astype(F32)).astype(BF16)


def taps_kernel(
    step, core_ref, fwd_ref, inv_ref, earlier_ref, mixed_ref, grad_b_ref, keep_ref, send_ref
):
    tokens = mixed_ref.shape[0]
    owned = keep_ref.shape[2]
    width = min(owned, step)

    def put(even_ref, odd_ref, owner, at, value):
        ref = even_ref if owner % 2 == 0 else odd_ref
        ref[owner // 2, :, at : at + width] = value

    for start in range(0, mixed_ref.shape[1], step):
        cols = slice(start, start + step)
        signal = dot(fwd_ref[...], stacked(earlier_ref[:, cols], mixed_ref[:, cols]))
        grad = dot(fwd_ref[:, :tokens], grad_b_ref[:, cols])
        part = dot(inv_ref[...], times_conj(signal, grad)).astype(BF16)
        for j in range(0, step, width):
            owner, at = divmod(start + j, owned)
            value = part[:, j : j + width]
            pl.when(core_ref[0] == 0)(functools.partial(put, keep_ref, send_ref, owner, at, value))
            pl.when(core_ref[0] == 1)(functools.partial(put, send_ref, keep_ref, owner, at, value))


def input_grad_kernel(
    step, fwd_ref, inv_ref, grad_b_ref, later_ref, taps_ref, adjoint_ref, grad_w_ref, long_ref, pre_ref,
    out_ref,
):
    tokens = grad_b_ref.shape[0]
    taps = taps_ref.shape[0]
    for start in range(0, grad_b_ref.shape[1], step):
        cols = slice(start, start + step)
        grad_w = get_columns(grad_w_ref, start, step).astype(F32)
        grad_u = adjoint_ref[:, cols].astype(F32) + grad_w * long_ref[:, cols].astype(F32)
        signal = dot(fwd_ref[...], stacked(grad_b_ref[:, cols], later_ref[:, cols]))
        filt = dot(fwd_ref[:, :taps], taps_ref[:, cols])
        act = dot(inv_ref[...], times_conj(signal, filt))
        out_ref[:, cols] = (grad_u + act * pre_ref[:, cols].astype(F32)).astype(BF16)


def correlate(blocks, own_ref, other, joint_ref):
    period, width = joint_ref.shape[1:]
    half = period // 2
    rows, lanes = 16, math.gcd(width, 128) if width % 128 == 0 else width

    def chunk(i, _):
        at = pl.multiple_of(i * rows, rows)
        re, im = pl.ds(at, rows), pl.ds(pl.multiple_of(half + at, rows), rows)
        for start in range(0, width, lanes):
            cols = slice(start, start + lanes)
            own = [(own_ref[q, re, cols], own_ref[q, im, cols]) for q in range(blocks)]
            oth = [(other[d, re, cols], other[d, im, cols]) for d in range(blocks)]
            for p in range(blocks):
                sum_re = sum_im = None
                for q in range(p, blocks):
                    a_re, a_im = own[q]
                    b_re, b_im = oth[q - p]
                    new_re = a_re * b_re + a_im * b_im
                    new_im = a_im * b_re - a_re * b_im
                    sum_re = new_re if sum_re is None else sum_re + new_re
                    sum_im = new_im if sum_im is None else sum_im + new_im
                joint_ref[p, re, cols] = sum_re.astype(BF16)
                joint_ref[p, im, cols] = sum_im.astype(BF16)
        return 0

    lax.fori_loop(0, half // rows, chunk, 0)


def grad_w_kernel(
    blocks, fwd_ref, inv_ref, grad_ref, filt_ref, out_ref, own_ref, other_ref, joint_ref
):
    size = grad_ref.shape[0] // blocks
    for q in range(blocks):
        own_ref[q] = dot(fwd_ref[:, size:], grad_ref[q * size : (q + 1) * size])
        other = dot_nt(fwd_ref[:, size:], filt_ref[:, q * size : (q + 1) * size])
        if q:
            other += dot_nt(fwd_ref[:, :size], filt_ref[:, (q - 1) * size : q * size])
        other_ref[q] = other
    correlate(blocks, own_ref, other_ref, joint_ref)
    for p in range(blocks):
        out_ref[p * size : (p + 1) * size] = dot(inv_ref[...], joint_ref[p]).astype(BF16)


def long_grad_kernel(
    blocks, scale, fwd_ref, inv_ref, grad_ref, long_ref, out_ref, own_ref, other_ref, joint_ref
):
    size = grad_ref.shape[0] // blocks
    for q in range(blocks):
        own_ref[q] = dot(fwd_ref[:, size:], grad_ref[q * size : (q + 1) * size])
        other = dot(fwd_ref[:, size:], long_ref[q * size : (q + 1) * size])
        if q:
            other += dot(fwd_ref[:, :size], long_ref[(q - 1) * size : q * size])
        other_ref[q] = other
    correlate(blocks, own_ref, other_ref, joint_ref)
    for p in range(blocks):
        lags = (dot(inv_ref[...], joint_ref[p]) * scale).T
        out_ref[:, p * size : (p + 1) * size] = lags.astype(BF16)


def total_kernel(scale, parts_ref, out_ref):
    total = parts_ref[0].astype(F32)
    for i in range(1, parts_ref.shape[0]):
        total += parts_ref[i].astype(F32)
    out_ref[...] = (total * scale).astype(BF16)


def call(body, grid, ins, outs, args, flops, scratch=(), vmem=16, name=None):
    moved = sum(a.size * a.dtype.itemsize for a in args)
    moved += sum(math.prod(shape) * jnp.dtype(kind).itemsize for shape, kind, _ in outs)
    result = pl.pallas_call(
        body,
        grid=grid,
        in_specs=ins,
        out_specs=[spec for _, _, spec in outs],
        out_shape=[jax.ShapeDtypeStruct(shape, kind) for shape, kind, _ in outs],
        scratch_shapes=list(scratch),
        compiler_params=pltpu.CompilerParams(vmem_limit_bytes=vmem * MIB),
        cost_estimate=pl.CostEstimate(flops=flops, bytes_accessed=moved, transcendentals=0),
        name=name,
    )(*args)
    return result[0] if len(result) == 1 else result


def whole_spec(array):
    return pl.BlockSpec(array.shape, lambda i: (0,) * array.ndim)


def by_all_to_all(
    incoming, layer_input, pre_gate, mid_gate, long_gate, out_gate, long_filter, mid_filter
):
    sections = lax.axis_size("section")
    devices = lax.axis_size("ctx")
    beta = (2.0 * sections) ** (-0.5)
    tokens, channels = layer_input.shape[1:]
    taps = mid_filter.shape[1]
    seq_len = tokens * devices
    scale = float(seq_len) ** (-0.5)
    owned = channels // devices

    span = tokens + max(tokens, taps)
    fwd = jnp.asarray(forward_table(span, np.arange(span)))
    inv_conv = jnp.asarray(inverse_table(span, tokens + np.arange(tokens)))
    inv_corr = jnp.asarray(inverse_table(span, np.arange(tokens)))
    inv_taps = jnp.asarray(inverse_table(span, tokens - np.arange(taps)))
    size = max(math.gcd(seq_len, 256), seq_len // 8)
    blocks = seq_len // size
    period = 2 * size
    long_fwd = jnp.asarray(forward_table(period, np.arange(-size, size)))
    long_inv = jnp.asarray(inverse_table(period, np.arange(size)))

    wide = max(1024, 2 * owned)
    step = min(256, wide)
    grid = (channels // wide,)
    rows_spec = pl.BlockSpec((tokens, wide), lambda i: (0, i))
    taps_spec = pl.BlockSpec((taps, wide), lambda i: (0, i))
    major_spec = pl.BlockSpec((wide // owned, tokens, owned), lambda i: (i, 0, 0))
    half_major = pl.BlockSpec((wide // owned // 2, taps, owned), lambda i: (i, 0, 0))
    half_shape = (devices // 2, taps, owned)
    rows_shape = (tokens, channels)
    major_shape = (devices, tokens, owned)
    mid_flops = 8 * span * tokens * channels

    tile = math.gcd(owned, 256)
    long_grid = (owned // tile,)
    long_spec = pl.BlockSpec((seq_len, tile), lambda i: (0, i))
    lag_spec = pl.BlockSpec((tile, seq_len), lambda i: (i, 0))
    spectrum = pltpu.VMEM((blocks, period, tile), F32)
    joint = pltpu.VMEM((blocks, period, tile), BF16)
    lanes = -(-tile // 128) * 128
    long_vmem = 2 * (long_fwd.size + long_inv.size) * 2 + 20 * blocks * period * lanes
    long_vmem = -(-long_vmem // MIB) + 6
    long_flops = 4 * period * seq_len * owned

    inputs, gate_pre, gate_mid, gate_long, gate_out = (
        array[0] for array in (layer_input, pre_gate, mid_gate, long_gate, out_gate)
    )
    filter_taps = mid_filter[0]

    adjoint = passed_along(incoming[0], "section", -1)
    mixed_in = call(
        mix_kernel, grid, [rows_spec] * 2, [(rows_shape, BF16, rows_spec)], [inputs, gate_pre],
        2 * tokens * channels, name="mix",
    )
    earlier = shifted(mixed_in, "ctx", 1)
    adjoint, earlier = lax.optimization_barrier((adjoint, earlier))
    grad_z = call(
        functools.partial(grad_z_kernel, beta), grid, [rows_spec] * 2,
        [(major_shape, BF16, major_spec)], [adjoint, gate_out], 2 * tokens * channels, name="gradz",
    )
    grad_z, earlier = lax.optimization_barrier((grad_z, earlier))
    channel_z = lax.all_to_all(grad_z, "ctx", split_axis=0, concat_axis=0, tiled=True)
    long_in = call(
        functools.partial(branch_kernel, beta, step), grid,
        [whole_spec(fwd), whole_spec(inv_conv)] + [rows_spec] * 2 + [taps_spec] + [rows_spec] * 3,
        [(major_shape, BF16, major_spec)],
        [fwd, inv_conv, earlier, mixed_in, filter_taps, inputs, gate_mid, gate_long], mid_flops,
        name="branch",
    )
    channel_z, long_in = lax.optimization_barrier((channel_z, long_in))
    channel_w = lax.all_to_all(long_in, "ctx", split_axis=0, concat_axis=0, tiled=True)
    channel_z = channel_z.reshape(seq_len, owned)
    grad_w = call(
        functools.partial(grad_w_kernel, blocks), long_grid,
        [whole_spec(long_fwd), whole_spec(long_inv), long_spec, lag_spec],
        [((seq_len, owned), BF16, long_spec)], [long_fwd, long_inv, channel_z, long_filter[0]],
        2 * long_flops, [spectrum, spectrum, joint], long_vmem, "gradw",
    )
    grad_w, channel_w = lax.optimization_barrier((grad_w, channel_w))
    returned = lax.all_to_all(
        grad_w.reshape(major_shape), "ctx", split_axis=0, concat_axis=0, tiled=True
    )
    channel_w = channel_w.reshape(seq_len, owned)
    long_grad = call(
        functools.partial(long_grad_kernel, blocks, scale), long_grid,
        [whole_spec(long_fwd), whole_spec(long_inv), long_spec, long_spec],
        [((owned, seq_len), BF16, lag_spec)], [long_fwd, long_inv, channel_z, channel_w],
        2 * long_flops, [spectrum, spectrum, joint], long_vmem, "longgrad",
    )
    returned, long_grad = lax.optimization_barrier((returned, long_grad))
    grad_b = call(
        functools.partial(grad_b_kernel, beta), grid,
        [rows_spec, major_spec] + [rows_spec] * 2, [(rows_shape, BF16, rows_spec)],
        [adjoint, returned, gate_long, gate_mid], 4 * tokens * channels, name="gradb",
    )
    later = shifted(grad_b, "ctx", -1)
    core = (lax.axis_index("ctx") % 2).astype(jnp.int32)[None]
    keep, send = call(
        functools.partial(taps_kernel, step), grid,
        [pl.BlockSpec(memory_space=pltpu.SMEM), whole_spec(fwd), whole_spec(inv_taps)]
        + [rows_spec] * 3,
        [(half_shape, BF16, half_major)] * 2,
        [core, fwd, inv_taps, earlier, mixed_in, grad_b], mid_flops, name="taps",
    )
    partner = lax.ppermute(send, "ctx", [(i, i ^ 1) for i in range(devices)])
    chip_parts = (keep.astype(F32) + partner.astype(F32)).astype(BF16)
    gathered = lax.all_to_all(
        chip_parts, "ctx", split_axis=0, concat_axis=0, tiled=True,
        axis_index_groups=[list(range(c, devices, 2)) for c in range(2)],
    )
    later, _ = lax.optimization_barrier((later, chip_parts))
    input_grad = call(
        functools.partial(input_grad_kernel, step), grid,
        [whole_spec(fwd), whole_spec(inv_corr)] + [rows_spec] * 2 + [taps_spec, rows_spec, major_spec]
        + [rows_spec] * 2,
        [(rows_shape, BF16, rows_spec)],
        [fwd, inv_corr, grad_b, later, filter_taps, adjoint, returned, gate_long, gate_pre],
        mid_flops, name="inputgrad",
    )
    mid_grad = call(
        functools.partial(total_kernel, scale), (1,), [whole_spec(gathered)],
        [((taps, owned), BF16, pl.BlockSpec((taps, owned), lambda i: (0, 0)))], [gathered],
        devices * taps * owned, name="midgrad",
    )
    return (input_grad[None], long_grad[None], mid_grad[None])


def columns(index, width):
    return pl.ds(pl.multiple_of(index * width, width), width)


def pick_kernel(slot, me_ref, in_ref, out_ref):
    out_ref[...] = in_ref[:, columns(me_ref[slot], out_ref.shape[1])]


def pieces_z_kernel(beta, first, me_ref, adjoint_ref, gate_ref, *out_refs):
    count = len(out_refs)
    width = out_refs[0].shape[1]
    me = me_ref[0]
    for k in range(count):
        owner = me ^ (first + k)
        part = adjoint_ref[:, columns(owner & (count - 1), width)].astype(F32)
        gate = gate_ref[:, columns(owner, width)].astype(F32)
        out_refs[k][...] = (beta * part * gate).astype(BF16)


def pieces_branch_kernel(
    beta, me_ref, fwd_ref, inv_ref, earlier_ref, mixed_ref, taps_ref, inputs_ref, mid_ref, long_ref,
    signal_ref, filt_ref, *out_refs,
):
    taps = taps_ref.shape[0]
    width = out_refs[0].shape[1]
    me = me_ref[0]
    count = len(out_refs)
    for k in list(range(count // 2, count)) + list(range(count // 2)):
        cols = columns(me ^ k, width)
        signal = dot(fwd_ref[...], stacked(earlier_ref[:, cols], mixed_ref[:, cols]))
        filt = dot(fwd_ref[:, :taps], taps_ref[:, cols])
        signal_ref[:, cols] = signal.astype(BF16)
        filt_ref[:, cols] = filt.astype(BF16)
        branch = dot(inv_ref[...], times(signal, filt))
        resid = inputs_ref[:, cols].astype(F32) + beta * branch * mid_ref[:, cols].astype(F32)
        out_refs[k][...] = (resid * long_ref[:, cols].astype(F32)).astype(BF16)


def spectra(blocks, fwd_ref, array_ref, cols, out_ref):
    size = array_ref.shape[0] // blocks
    for q in range(blocks):
        out_ref[q] = dot(fwd_ref[:, size:], array_ref[q * size : (q + 1) * size, cols])


def extended_spectra(blocks, fwd_ref, array_ref, cols, out_ref):
    size = array_ref.shape[0] // blocks
    out_ref[0] = dot(fwd_ref[:, size:], array_ref[:size, cols])
    for q in range(1, blocks):
        out_ref[q] = dot(fwd_ref[...], array_ref[(q - 1) * size : (q + 1) * size, cols])


def pieces_grad_w_kernel(blocks, count, me_ref, fwd_ref, inv_ref, filt_ref, *refs):
    piece_refs, out_refs = refs[:count][::-1], refs[count : 2 * count]
    whole_ref, own_ref, other_ref, joint_ref, result_ref = refs[2 * count :]
    rows = piece_refs[0].shape[0]
    size = whole_ref.shape[0] // blocks
    tile = joint_ref.shape[2]
    me = me_ref[0]
    for k in range(count):
        whole_ref[columns(me ^ k, rows), :] = piece_refs[k][...]
    for start in range(0, whole_ref.shape[1], tile):
        cols = slice(start, start + tile)
        spectra(blocks, fwd_ref, whole_ref, cols, own_ref)
        other_ref[0] = dot_nt(fwd_ref[:, size:], filt_ref[cols, :size])
        for q in range(1, blocks):
            other_ref[q] = dot_nt(fwd_ref[...], filt_ref[cols, (q - 1) * size : (q + 1) * size])
        correlate(blocks, own_ref, other_ref, joint_ref)
        for p in range(blocks):
            result_ref[p * size : (p + 1) * size, cols] = dot(inv_ref[...], joint_ref[p]).astype(BF16)
    for k in range(count):
        out_refs[k][...] = result_ref[columns(me ^ k, rows), :]


def pieces_long_grad_kernel(blocks, scale, count, me_ref, fwd_ref, inv_ref, grad_ref, *refs):
    piece_refs, out_ref = refs[:count][::-1], refs[count]
    own_ref, other_ref, joint_ref, whole_ref = refs[count + 1 :]
    rows = piece_refs[0].shape[0]
    size = whole_ref.shape[0] // blocks
    tile = joint_ref.shape[2]
    me = me_ref[0]
    for k in range(count):
        whole_ref[columns(me ^ k, rows), :] = piece_refs[k][...]
    for start in range(0, whole_ref.shape[1], tile):
        cols = slice(start, start + tile)
        spectra(blocks, fwd_ref, grad_ref, cols, own_ref)
        extended_spectra(blocks, fwd_ref, whole_ref, cols, other_ref)
        correlate(blocks, own_ref, other_ref, joint_ref)
        for p in range(blocks):
            lags = (dot(inv_ref[...], joint_ref[p]) * scale).T
            out_ref[cols, p * size : (p + 1) * size] = lags.astype(BF16)


def pieces_grad_b_kernel(beta, count, me_ref, near_ref, far_ref, long_ref, mid_ref, *refs):
    piece_refs, (grad_u_ref, grad_b_ref) = refs[:count][::-1], refs[count:]
    width = piece_refs[0].shape[1]
    half = count // 2
    me = me_ref[0]
    for k in range(count):
        owner = me ^ k
        cols = columns(owner, width)
        adjoint_ref = near_ref if k < half else far_ref
        adjoint = adjoint_ref[:, columns(owner & (half - 1), width)].astype(F32)
        grad_u = adjoint + piece_refs[k][...].astype(F32) * long_ref[:, cols].astype(F32)
        grad_u_ref[:, cols] = grad_u
        grad_b_ref[:, cols] = (beta * grad_u * mid_ref[:, cols].astype(F32)).astype(BF16)


def pieces_taps_kernel(me_ref, fwd_ref, inv_ref, signal_ref, grad_b_ref, keep_ref, send_ref):
    tokens = grad_b_ref.shape[0]
    width = keep_ref.shape[2]
    me = me_ref[0]
    for k in range(2 * keep_ref.shape[0]):
        cols = columns(me ^ k, width)
        grad = dot(fwd_ref[:, :tokens], grad_b_ref[:, cols])
        part = dot(inv_ref[...], times_conj(signal_ref[:, cols].astype(F32), grad)).astype(BF16)
        (send_ref if k % 2 else keep_ref)[k // 2] = part


def pair_kernel(keep_ref, came_ref, *out_refs):
    for m, out_ref in enumerate(out_refs):
        out_ref[...] = (keep_ref[m].astype(F32) + came_ref[m].astype(F32)).astype(BF16)


def pieces_total_kernel(scale, *refs):
    total = refs[0][...].astype(F32)
    for ref in refs[1:-1]:
        total += ref[...].astype(F32)
    refs[-1][...] = (total * scale).astype(BF16)


def pieces_input_grad_kernel(
    step, fwd_ref, inv_ref, grad_b_ref, later_ref, filt_ref, grad_u_ref, pre_ref, out_ref
):
    for start in range(0, grad_b_ref.shape[1], step):
        cols = slice(start, start + step)
        signal = dot(fwd_ref[...], stacked(grad_b_ref[:, cols], later_ref[:, cols]))
        act = dot(inv_ref[...], times_conj(signal, filt_ref[:, cols].astype(F32)))
        value = grad_u_ref[:, cols] + act * pre_ref[:, cols].astype(F32)
        out_ref[:, cols] = value.astype(BF16)


def local(body, outs, args, flops, scratch=(), vmem=24, name=None):
    moved = sum(a.size * a.dtype.itemsize for a in args)
    moved += sum(math.prod(shape) * jnp.dtype(kind).itemsize for shape, kind in outs)
    specs = [
        pl.BlockSpec(memory_space=pltpu.SMEM if a.dtype == jnp.int32 else pltpu.VMEM) for a in args
    ]
    result = pl.pallas_call(
        body,
        in_specs=specs,
        out_specs=[pl.BlockSpec(memory_space=pltpu.VMEM) for _ in outs],
        out_shape=[jax.ShapeDtypeStruct(shape, kind) for shape, kind in outs],
        scratch_shapes=list(scratch),
        compiler_params=pltpu.CompilerParams(vmem_limit_bytes=vmem * MIB),
        cost_estimate=pl.CostEstimate(flops=flops, bytes_accessed=moved, transcendentals=0),
        name=name,
    )(*args)
    return result[0] if len(result) == 1 else result


def swapped(array, k):
    count = lax.axis_size("ctx")
    return lax.ppermute(array, "ctx", [(i, i ^ k) for i in range(count)])


def exchanged(pieces, step=1, first=0):
    came = list(pieces)
    for k in range(len(pieces) - 1, -1, -1):
        if first + k:
            came[k] = swapped(pieces[k], (first + k) * step)
    return came


def by_permutes(
    incoming, layer_input, pre_gate, mid_gate, long_gate, out_gate, long_filter, mid_filter
):
    sections = lax.axis_size("section")
    devices = lax.axis_size("ctx")
    half = devices // 2
    beta = (2.0 * sections) ** (-0.5)
    tokens, channels = layer_input.shape[1:]
    taps = mid_filter.shape[1]
    seq_len = tokens * devices
    scale = float(seq_len) ** (-0.5)
    owned = channels // devices

    span = tokens + max(tokens, taps)
    fwd = jnp.asarray(forward_table(span, np.arange(span)))
    inv_conv = jnp.asarray(inverse_table(span, tokens + np.arange(tokens)))
    inv_corr = jnp.asarray(inverse_table(span, np.arange(tokens)))
    inv_taps = jnp.asarray(inverse_table(span, tokens - np.arange(taps)))
    size = max(math.gcd(seq_len, 256), seq_len // 8)
    blocks = seq_len // size
    period = 2 * size
    long_fwd = jnp.asarray(forward_table(period, np.arange(-size, size)))
    long_inv = jnp.asarray(inverse_table(period, np.arange(size)))
    tile = math.gcd(owned, 256)
    spectrum = pltpu.VMEM((blocks, period, tile), F32)
    joint = pltpu.VMEM((blocks, period, tile), BF16)
    staged = pltpu.VMEM((seq_len, owned), BF16)

    rows_shape = ((tokens, channels), BF16)
    half_shape = ((tokens, channels // 2), BF16)
    piece = ((tokens, owned), BF16)
    tap_piece = ((taps, owned), BF16)
    mid_flops = 8 * span * tokens * channels
    long_flops = 12 * period * seq_len * owned
    few = 4 * tokens * channels

    index = lax.axis_index("ctx")
    me = jnp.stack([index, index // half, 1 - index // half]).astype(jnp.int32)
    inputs, gate_pre, gate_mid, gate_long, gate_out = (
        array[0] for array in (layer_input, pre_gate, mid_gate, long_gate, out_gate)
    )
    filter_taps = mid_filter[0]

    far = local(functools.partial(pick_kernel, 2), [half_shape], [me, incoming[0]], few, name="far")
    far, inputs, gate_pre = lax.optimization_barrier((far, inputs, gate_pre))
    mixed_in = local(mix_kernel, [rows_shape], [inputs, gate_pre], few, name="mix")
    far = passed_along(far, "section", -1)
    earlier = shifted(mixed_in, "ctx", 1)
    far, sent = lax.optimization_barrier((far, incoming[0]))
    near = local(functools.partial(pick_kernel, 1), [half_shape], [me, sent], few, name="near")
    near = passed_along(near, "section", -1)
    far_z = local(
        functools.partial(pieces_z_kernel, beta, half), [piece] * half, [me, far, gate_out], few, name="farz"
    )
    far_z, earlier = lax.optimization_barrier((far_z, earlier))
    signal, filt, *pieces_w = local(
        functools.partial(pieces_branch_kernel, beta),
        [((span, channels), BF16)] * 2 + [piece] * devices,
        [me, fwd, inv_conv, earlier, mixed_in, filter_taps, inputs, gate_mid, gate_long], mid_flops,
        name="branch",
    )
    far_z = exchanged(far_z, first=half)
    far_z, near, pieces_w = lax.optimization_barrier((far_z, near, pieces_w))
    near_z = local(
        functools.partial(pieces_z_kernel, beta, 0), [piece] * half, [me, near, gate_out], few, name="nearz"
    )
    far_w = exchanged(pieces_w[half:], first=half)
    near_z = exchanged(near_z)
    pieces_z = near_z + far_z
    *pieces_g, channel_z = local(
        functools.partial(pieces_grad_w_kernel, blocks, devices),
        [piece] * devices + [((seq_len, owned), BF16)],
        [me, long_fwd, long_inv, long_filter[0], *pieces_z[::-1]], long_flops,
        [spectrum, spectrum, joint, staged], name="gradw",
    )
    far_w, near_w, pieces_g = lax.optimization_barrier((far_w, pieces_w[:half], pieces_g))
    pieces_w = exchanged(near_w) + far_w
    pieces_g = exchanged(pieces_g)[::-1]
    long_grad = local(
        functools.partial(pieces_long_grad_kernel, blocks, scale, devices), [((owned, seq_len), BF16)],
        [me, long_fwd, long_inv, channel_z, *pieces_w[::-1]], long_flops,
        [spectrum, spectrum, joint, staged], name="longgrad",
    )
    pieces_g, long_grad = lax.optimization_barrier((pieces_g, long_grad))
    grad_u, grad_b = local(
        functools.partial(pieces_grad_b_kernel, beta, devices), [((tokens, channels), F32), rows_shape],
        [me, near, far, gate_long, gate_mid, *pieces_g], few, name="gradb",
    )
    later = shifted(grad_b, "ctx", -1)
    keep, send = local(
        pieces_taps_kernel, [((half, taps, owned), BF16)] * 2, [me, fwd, inv_taps, signal, grad_b],
        mid_flops, name="taps",
    )
    sums = local(pair_kernel, [tap_piece] * half, [keep, swapped(send, 1)], few, name="pair")
    sums = exchanged(list(sums), 2)[::-1]
    later, _ = lax.optimization_barrier((later, sums[-1]))
    input_grad = local(
        functools.partial(pieces_input_grad_kernel, 512), [rows_shape],
        [fwd, inv_corr, grad_b, later, filt, grad_u, gate_pre], mid_flops, name="inputgrad",
    )
    sums, input_grad = lax.optimization_barrier((sums, input_grad))
    mid_grad = local(functools.partial(pieces_total_kernel, scale), [tap_piece], sums, few, name="midgrad")
    return (input_grad[None], long_grad[None], mid_grad[None])


def per_device(*arrays):
    devices = lax.axis_size("ctx")
    owned = arrays[0].shape[2] // devices
    if owned % 128 == 0 and devices in (2, 4, 8, 16):
        return by_permutes(*arrays)
    return by_all_to_all(*arrays)


def solution(mesh):
    placed = (
        P("section", "ctx", None),
        P("section", "ctx", None),
        P("section", "ctx", None),
        P("section", "ctx", None),
        P("section", "ctx", None),
        P("section", "ctx", None),
        P("section", "ctx", None),
        P("section", None, None),
    )
    return jax.shard_map(
        per_device,
        mesh=mesh,
        in_specs=placed,
        out_specs=(P("section", "ctx", None), P("section", "ctx", None), P("section", None, "ctx")),
        check_vma=False,
    )
```

```python
import functools
import math

import jax
import jax.numpy as jnp
import numpy as np
from jax import lax
from jax.experimental import pallas as pl
from jax.experimental.pallas import tpu as pltpu
from jax.sharding import PartitionSpec as P

BF16 = jnp.bfloat16
F32 = jnp.float32
MIB = 1024 * 1024


def passed_along(value, axis, steps):
    count = lax.axis_size(axis)
    pairs = [(source, (source + steps) % count) for source in range(count)]
    return lax.ppermute(value, axis, pairs)


def shifted(array, axis, by):
    devices = lax.axis_size(axis)
    pairs = [(i, i + by) for i in range(devices) if 0 <= i + by < devices]
    return lax.ppermute(array, axis, pairs)


def forward_table(period, positions):
    angle = np.pi * np.outer(2 * np.arange(period // 2) + 1, positions) / period
    return np.concatenate([np.cos(angle), -np.sin(angle)], 0).astype(BF16)


def inverse_table(period, positions):
    angle = np.pi * np.outer(positions, 2 * np.arange(period // 2) + 1) / period
    return (np.concatenate([np.cos(angle), -np.sin(angle)], 1) * (2.0 / period)).astype(BF16)


def dot(left, right):
    return jnp.dot(left, right, preferred_element_type=F32)


def dot_nt(left, right):
    return lax.dot_general(left, right, (((1,), (1,)), ((), ())), preferred_element_type=F32)


def stacked(*rows):
    return jnp.concatenate(rows, 0)


def times(left, right):
    half = left.shape[0] // 2
    l_re, l_im, r_re, r_im = left[:half], left[half:], right[:half], right[half:]
    return jnp.concatenate(
        [(l_re * r_re - l_im * r_im).astype(BF16), (l_re * r_im + l_im * r_re).astype(BF16)], 0
    )


def times_conj(left, right):
    half = left.shape[0] // 2
    l_re, l_im, r_re, r_im = left[:half], left[half:], right[:half], right[half:]
    return jnp.concatenate(
        [(l_re * r_re + l_im * r_im).astype(BF16), (l_im * r_re - l_re * r_im).astype(BF16)], 0
    )


def put_columns(out_ref, value, start):
    owned = out_ref.shape[2]
    width = value.shape[1]
    if owned >= width:
        out_ref[start // owned, :, start % owned : start % owned + width] = value
    else:
        for j in range(width // owned):
            out_ref[start // owned + j] = value[:, j * owned : (j + 1) * owned]


def get_columns(in_ref, start, width):
    owned = in_ref.shape[2]
    if owned >= width:
        return in_ref[start // owned, :, start % owned : start % owned + width]
    return jnp.concatenate([in_ref[start // owned + j] for j in range(width // owned)], 1)


def mix_kernel(inputs_ref, gate_ref, out_ref):
    out_ref[...] = (inputs_ref[...].astype(F32) * gate_ref[...].astype(F32)).astype(BF16)


def grad_z_kernel(beta, adjoint_ref, gate_ref, out_ref):
    value = beta * adjoint_ref[...].astype(F32) * gate_ref[...].astype(F32)
    put_columns(out_ref, value.astype(BF16), 0)


def branch_kernel(
    beta, step, fwd_ref, inv_ref, earlier_ref, mixed_ref, taps_ref, inputs_ref, mid_ref, long_ref, out_ref
):
    tokens = mixed_ref.shape[0]
    taps = taps_ref.shape[0]
    for start in range(0, mixed_ref.shape[1], step):
        cols = slice(start, start + step)
        signal = dot(fwd_ref[...], stacked(earlier_ref[:, cols], mixed_ref[:, cols]))
        filt = dot(fwd_ref[:, :taps], taps_ref[:, cols])
        branch = dot(inv_ref[...], times(signal, filt))
        resid = inputs_ref[:, cols].astype(F32) + beta * branch * mid_ref[:, cols].astype(F32)
        value = (resid * long_ref[:, cols].astype(F32)).astype(BF16)
        put_columns(out_ref, value, start)


def grad_b_kernel(beta, adjoint_ref, grad_w_ref, long_ref, mid_ref, out_ref):
    grad_w = get_columns(grad_w_ref, 0, out_ref.shape[1]).astype(F32)
    grad_u = adjoint_ref[...].astype(F32) + grad_w * long_ref[...].astype(F32)
    out_ref[...] = (beta * grad_u * mid_ref[...].astype(F32)).astype(BF16)


def taps_kernel(
    step, core_ref, fwd_ref, inv_ref, earlier_ref, mixed_ref, grad_b_ref, keep_ref, send_ref
):
    tokens = mixed_ref.shape[0]
    owned = keep_ref.shape[2]
    width = min(owned, step)

    def put(even_ref, odd_ref, owner, at, value):
        ref = even_ref if owner % 2 == 0 else odd_ref
        ref[owner // 2, :, at : at + width] = value

    for start in range(0, mixed_ref.shape[1], step):
        cols = slice(start, start + step)
        signal = dot(fwd_ref[...], stacked(earlier_ref[:, cols], mixed_ref[:, cols]))
        grad = dot(fwd_ref[:, :tokens], grad_b_ref[:, cols])
        part = dot(inv_ref[...], times_conj(signal, grad)).astype(BF16)
        for j in range(0, step, width):
            owner, at = divmod(start + j, owned)
            value = part[:, j : j + width]
            pl.when(core_ref[0] == 0)(functools.partial(put, keep_ref, send_ref, owner, at, value))
            pl.when(core_ref[0] == 1)(functools.partial(put, send_ref, keep_ref, owner, at, value))


def input_grad_kernel(
    step, fwd_ref, inv_ref, grad_b_ref, later_ref, taps_ref, adjoint_ref, grad_w_ref, long_ref, pre_ref,
    out_ref,
):
    tokens = grad_b_ref.shape[0]
    taps = taps_ref.shape[0]
    for start in range(0, grad_b_ref.shape[1], step):
        cols = slice(start, start + step)
        grad_w = get_columns(grad_w_ref, start, step).astype(F32)
        grad_u = adjoint_ref[:, cols].astype(F32) + grad_w * long_ref[:, cols].astype(F32)
        signal = dot(fwd_ref[...], stacked(grad_b_ref[:, cols], later_ref[:, cols]))
        filt = dot(fwd_ref[:, :taps], taps_ref[:, cols])
        act = dot(inv_ref[...], times_conj(signal, filt))
        out_ref[:, cols] = (grad_u + act * pre_ref[:, cols].astype(F32)).astype(BF16)


def correlate(blocks, own_ref, other, joint_ref):
    period, width = joint_ref.shape[1:]
    half = period // 2
    rows, lanes = 16, math.gcd(width, 128) if width % 128 == 0 else width

    def chunk(i, _):
        at = pl.multiple_of(i * rows, rows)
        re, im = pl.ds(at, rows), pl.ds(pl.multiple_of(half + at, rows), rows)
        for start in range(0, width, lanes):
            cols = slice(start, start + lanes)
            own = [(own_ref[q, re, cols], own_ref[q, im, cols]) for q in range(blocks)]
            oth = [(other[d, re, cols], other[d, im, cols]) for d in range(blocks)]
            for p in range(blocks):
                sum_re = sum_im = None
                for q in range(p, blocks):
                    a_re, a_im = own[q]
                    b_re, b_im = oth[q - p]
                    new_re = a_re * b_re + a_im * b_im
                    new_im = a_im * b_re - a_re * b_im
                    sum_re = new_re if sum_re is None else sum_re + new_re
                    sum_im = new_im if sum_im is None else sum_im + new_im
                joint_ref[p, re, cols] = sum_re.astype(BF16)
                joint_ref[p, im, cols] = sum_im.astype(BF16)
        return 0

    lax.fori_loop(0, half // rows, chunk, 0)


def grad_w_kernel(
    blocks, fwd_ref, inv_ref, grad_ref, filt_ref, out_ref, own_ref, other_ref, joint_ref
):
    size = grad_ref.shape[0] // blocks
    for q in range(blocks):
        own_ref[q] = dot(fwd_ref[:, size:], grad_ref[q * size : (q + 1) * size])
        other = dot_nt(fwd_ref[:, size:], filt_ref[:, q * size : (q + 1) * size])
        if q:
            other += dot_nt(fwd_ref[:, :size], filt_ref[:, (q - 1) * size : q * size])
        other_ref[q] = other
    correlate(blocks, own_ref, other_ref, joint_ref)
    for p in range(blocks):
        out_ref[p * size : (p + 1) * size] = dot(inv_ref[...], joint_ref[p]).astype(BF16)


def long_grad_kernel(
    blocks, scale, fwd_ref, inv_ref, grad_ref, long_ref, out_ref, own_ref, other_ref, joint_ref
):
    size = grad_ref.shape[0] // blocks
    for q in range(blocks):
        own_ref[q] = dot(fwd_ref[:, size:], grad_ref[q * size : (q + 1) * size])
        other = dot(fwd_ref[:, size:], long_ref[q * size : (q + 1) * size])
        if q:
            other += dot(fwd_ref[:, :size], long_ref[(q - 1) * size : q * size])
        other_ref[q] = other
    correlate(blocks, own_ref, other_ref, joint_ref)
    for p in range(blocks):
        lags = (dot(inv_ref[...], joint_ref[p]) * scale).T
        out_ref[:, p * size : (p + 1) * size] = lags.astype(BF16)


def total_kernel(scale, parts_ref, out_ref):
    total = parts_ref[0].astype(F32)
    for i in range(1, parts_ref.shape[0]):
        total += parts_ref[i].astype(F32)
    out_ref[...] = (total * scale).astype(BF16)


def call(body, grid, ins, outs, args, flops, scratch=(), vmem=16, name=None):
    moved = sum(a.size * a.dtype.itemsize for a in args)
    moved += sum(math.prod(shape) * jnp.dtype(kind).itemsize for shape, kind, _ in outs)
    result = pl.pallas_call(
        body,
        grid=grid,
        in_specs=ins,
        out_specs=[spec for _, _, spec in outs],
        out_shape=[jax.ShapeDtypeStruct(shape, kind) for shape, kind, _ in outs],
        scratch_shapes=list(scratch),
        compiler_params=pltpu.CompilerParams(vmem_limit_bytes=vmem * MIB),
        cost_estimate=pl.CostEstimate(flops=flops, bytes_accessed=moved, transcendentals=0),
        name=name,
    )(*args)
    return result[0] if len(result) == 1 else result


def whole_spec(array):
    return pl.BlockSpec(array.shape, lambda i: (0,) * array.ndim)


def by_all_to_all(
    incoming, layer_input, pre_gate, mid_gate, long_gate, out_gate, long_filter, mid_filter
):
    sections = lax.axis_size("section")
    devices = lax.axis_size("ctx")
    beta = (2.0 * sections) ** (-0.5)
    tokens, channels = layer_input.shape[1:]
    taps = mid_filter.shape[1]
    seq_len = tokens * devices
    scale = float(seq_len) ** (-0.5)
    owned = channels // devices

    span = tokens + max(tokens, taps)
    fwd = jnp.asarray(forward_table(span, np.arange(span)))
    inv_conv = jnp.asarray(inverse_table(span, tokens + np.arange(tokens)))
    inv_corr = jnp.asarray(inverse_table(span, np.arange(tokens)))
    inv_taps = jnp.asarray(inverse_table(span, tokens - np.arange(taps)))
    size = max(math.gcd(seq_len, 256), seq_len // 8)
    blocks = seq_len // size
    period = 2 * size
    long_fwd = jnp.asarray(forward_table(period, np.arange(-size, size)))
    long_inv = jnp.asarray(inverse_table(period, np.arange(size)))

    wide = max(1024, 2 * owned)
    step = min(256, wide)
    grid = (channels // wide,)
    rows_spec = pl.BlockSpec((tokens, wide), lambda i: (0, i))
    taps_spec = pl.BlockSpec((taps, wide), lambda i: (0, i))
    major_spec = pl.BlockSpec((wide // owned, tokens, owned), lambda i: (i, 0, 0))
    half_major = pl.BlockSpec((wide // owned // 2, taps, owned), lambda i: (i, 0, 0))
    half_shape = (devices // 2, taps, owned)
    rows_shape = (tokens, channels)
    major_shape = (devices, tokens, owned)
    mid_flops = 8 * span * tokens * channels

    tile = math.gcd(owned, 256)
    long_grid = (owned // tile,)
    long_spec = pl.BlockSpec((seq_len, tile), lambda i: (0, i))
    lag_spec = pl.BlockSpec((tile, seq_len), lambda i: (i, 0))
    spectrum = pltpu.VMEM((blocks, period, tile), F32)
    joint = pltpu.VMEM((blocks, period, tile), BF16)
    lanes = -(-tile // 128) * 128
    long_vmem = 2 * (long_fwd.size + long_inv.size) * 2 + 20 * blocks * period * lanes
    long_vmem = -(-long_vmem // MIB) + 6
    long_flops = 4 * period * seq_len * owned

    inputs, gate_pre, gate_mid, gate_long, gate_out = (
        array[0] for array in (layer_input, pre_gate, mid_gate, long_gate, out_gate)
    )
    filter_taps = mid_filter[0]

    adjoint = passed_along(incoming[0], "section", -1)
    mixed_in = call(
        mix_kernel, grid, [rows_spec] * 2, [(rows_shape, BF16, rows_spec)], [inputs, gate_pre],
        2 * tokens * channels, name="mix",
    )
    earlier = shifted(mixed_in, "ctx", 1)
    adjoint, earlier = lax.optimization_barrier((adjoint, earlier))
    grad_z = call(
        functools.partial(grad_z_kernel, beta), grid, [rows_spec] * 2,
        [(major_shape, BF16, major_spec)], [adjoint, gate_out], 2 * tokens * channels, name="gradz",
    )
    grad_z, earlier = lax.optimization_barrier((grad_z, earlier))
    channel_z = lax.all_to_all(grad_z, "ctx", split_axis=0, concat_axis=0, tiled=True)
    long_in = call(
        functools.partial(branch_kernel, beta, step), grid,
        [whole_spec(fwd), whole_spec(inv_conv)] + [rows_spec] * 2 + [taps_spec] + [rows_spec] * 3,
        [(major_shape, BF16, major_spec)],
        [fwd, inv_conv, earlier, mixed_in, filter_taps, inputs, gate_mid, gate_long], mid_flops,
        name="branch",
    )
    channel_z, long_in = lax.optimization_barrier((channel_z, long_in))
    channel_w = lax.all_to_all(long_in, "ctx", split_axis=0, concat_axis=0, tiled=True)
    channel_z = channel_z.reshape(seq_len, owned)
    grad_w = call(
        functools.partial(grad_w_kernel, blocks), long_grid,
        [whole_spec(long_fwd), whole_spec(long_inv), long_spec, lag_spec],
        [((seq_len, owned), BF16, long_spec)], [long_fwd, long_inv, channel_z, long_filter[0]],
        2 * long_flops, [spectrum, spectrum, joint], long_vmem, "gradw",
    )
    grad_w, channel_w = lax.optimization_barrier((grad_w, channel_w))
    returned = lax.all_to_all(
        grad_w.reshape(major_shape), "ctx", split_axis=0, concat_axis=0, tiled=True
    )
    channel_w = channel_w.reshape(seq_len, owned)
    long_grad = call(
        functools.partial(long_grad_kernel, blocks, scale), long_grid,
        [whole_spec(long_fwd), whole_spec(long_inv), long_spec, long_spec],
        [((owned, seq_len), BF16, lag_spec)], [long_fwd, long_inv, channel_z, channel_w],
        2 * long_flops, [spectrum, spectrum, joint], long_vmem, "longgrad",
    )
    returned, long_grad = lax.optimization_barrier((returned, long_grad))
    grad_b = call(
        functools.partial(grad_b_kernel, beta), grid,
        [rows_spec, major_spec] + [rows_spec] * 2, [(rows_shape, BF16, rows_spec)],
        [adjoint, returned, gate_long, gate_mid], 4 * tokens * channels, name="gradb",
    )
    later = shifted(grad_b, "ctx", -1)
    core = (lax.axis_index("ctx") % 2).astype(jnp.int32)[None]
    keep, send = call(
        functools.partial(taps_kernel, step), grid,
        [pl.BlockSpec(memory_space=pltpu.SMEM), whole_spec(fwd), whole_spec(inv_taps)]
        + [rows_spec] * 3,
        [(half_shape, BF16, half_major)] * 2,
        [core, fwd, inv_taps, earlier, mixed_in, grad_b], mid_flops, name="taps",
    )
    partner = lax.ppermute(send, "ctx", [(i, i ^ 1) for i in range(devices)])
    chip_parts = (keep.astype(F32) + partner.astype(F32)).astype(BF16)
    gathered = lax.all_to_all(
        chip_parts, "ctx", split_axis=0, concat_axis=0, tiled=True,
        axis_index_groups=[list(range(c, devices, 2)) for c in range(2)],
    )
    later, _ = lax.optimization_barrier((later, chip_parts))
    input_grad = call(
        functools.partial(input_grad_kernel, step), grid,
        [whole_spec(fwd), whole_spec(inv_corr)] + [rows_spec] * 2 + [taps_spec, rows_spec, major_spec]
        + [rows_spec] * 2,
        [(rows_shape, BF16, rows_spec)],
        [fwd, inv_corr, grad_b, later, filter_taps, adjoint, returned, gate_long, gate_pre],
        mid_flops, name="inputgrad",
    )
    mid_grad = call(
        functools.partial(total_kernel, scale), (1,), [whole_spec(gathered)],
        [((taps, owned), BF16, pl.BlockSpec((taps, owned), lambda i: (0, 0)))], [gathered],
        devices * taps * owned, name="midgrad",
    )
    return (input_grad[None], long_grad[None], mid_grad[None])


def columns(index, width):
    return pl.ds(pl.multiple_of(index * width, width), width)


def pick_kernel(firsts, me_ref, in_ref, *out_refs):
    for first, out_ref in zip(firsts, out_refs):
        width = out_ref.shape[1]
        owned = in_ref.shape[1] // 8
        out_ref[...] = in_ref[:, columns((me_ref[0] ^ first) // (width // owned), width)]


def pieces_z_kernel(beta, first, me_ref, adjoint_ref, gate_ref, *out_refs):
    count = len(out_refs)
    width = out_refs[0].shape[1]
    me = me_ref[0]
    for k in range(count):
        owner = me ^ (first + k)
        part = adjoint_ref[:, columns(owner & (count - 1), width)].astype(F32)
        gate = gate_ref[:, columns(owner, width)].astype(F32)
        out_refs[k][...] = (beta * part * gate).astype(BF16)


def pieces_branch_kernel(
    beta, me_ref, fwd_ref, inv_ref, earlier_ref, mixed_ref, taps_ref, inputs_ref, mid_ref, long_ref,
    signal_ref, filt_ref, *out_refs,
):
    taps = taps_ref.shape[0]
    width = out_refs[0].shape[1]
    me = me_ref[0]
    count = len(out_refs)
    for k in list(range(count // 2, count)) + list(range(count // 2)):
        cols = columns(me ^ k, width)
        signal = dot(fwd_ref[...], stacked(earlier_ref[:, cols], mixed_ref[:, cols]))
        filt = dot(fwd_ref[:, :taps], taps_ref[:, cols])
        signal_ref[:, cols] = signal.astype(BF16)
        filt_ref[:, cols] = filt.astype(BF16)
        branch = dot(inv_ref[...], times(signal, filt))
        resid = inputs_ref[:, cols].astype(F32) + beta * branch * mid_ref[:, cols].astype(F32)
        out_refs[k][...] = (resid * long_ref[:, cols].astype(F32)).astype(BF16)


def spectra(blocks, fwd_ref, array_ref, cols, out_ref):
    size = array_ref.shape[0] // blocks
    for q in range(blocks):
        out_ref[q] = dot(fwd_ref[:, size:], array_ref[q * size : (q + 1) * size, cols])


def extended_spectra(blocks, fwd_ref, array_ref, cols, out_ref):
    size = array_ref.shape[0] // blocks
    out_ref[0] = dot(fwd_ref[:, size:], array_ref[:size, cols])
    for q in range(1, blocks):
        out_ref[q] = dot(fwd_ref[...], array_ref[(q - 1) * size : (q + 1) * size, cols])


def pieces_grad_w_kernel(blocks, count, me_ref, fwd_ref, inv_ref, filt_ref, *refs):
    piece_refs, out_refs = refs[:count][::-1], refs[count : 2 * count]
    whole_ref, own_ref, other_ref, joint_ref, result_ref = refs[2 * count :]
    rows = piece_refs[0].shape[0]
    size = whole_ref.shape[0] // blocks
    tile = joint_ref.shape[2]
    me = me_ref[0]
    for k in range(count):
        whole_ref[columns(me ^ k, rows), :] = piece_refs[k][...]
    for start in range(0, whole_ref.shape[1], tile):
        cols = slice(start, start + tile)
        spectra(blocks, fwd_ref, whole_ref, cols, own_ref)
        other_ref[0] = dot_nt(fwd_ref[:, size:], filt_ref[cols, :size])
        for q in range(1, blocks):
            other_ref[q] = dot_nt(fwd_ref[...], filt_ref[cols, (q - 1) * size : (q + 1) * size])
        correlate(blocks, own_ref, other_ref, joint_ref)
        for p in range(blocks):
            result_ref[p * size : (p + 1) * size, cols] = dot(inv_ref[...], joint_ref[p]).astype(BF16)
    for k in range(count):
        out_refs[k][...] = result_ref[columns(me ^ k, rows), :]


def pieces_long_grad_kernel(blocks, scale, count, me_ref, fwd_ref, inv_ref, grad_ref, *refs):
    piece_refs, out_ref = refs[:count][::-1], refs[count]
    own_ref, other_ref, joint_ref, whole_ref = refs[count + 1 :]
    rows = piece_refs[0].shape[0]
    size = whole_ref.shape[0] // blocks
    tile = joint_ref.shape[2]
    me = me_ref[0]
    for k in range(count):
        whole_ref[columns(me ^ k, rows), :] = piece_refs[k][...]
    for start in range(0, whole_ref.shape[1], tile):
        cols = slice(start, start + tile)
        spectra(blocks, fwd_ref, grad_ref, cols, own_ref)
        extended_spectra(blocks, fwd_ref, whole_ref, cols, other_ref)
        correlate(blocks, own_ref, other_ref, joint_ref)
        for p in range(blocks):
            lags = (dot(inv_ref[...], joint_ref[p]) * scale).T
            out_ref[cols, p * size : (p + 1) * size] = lags.astype(BF16)


def pieces_grad_b_kernel(beta, count, me_ref, near_ref, mid_ref, far_ref, long_ref, gate_ref, *refs):
    piece_refs, (grad_u_ref, grad_b_ref) = refs[:count][::-1], refs[count:]
    width = piece_refs[0].shape[1]
    me = me_ref[0]
    for k in range(count):
        owner = me ^ k
        cols = columns(owner, width)
        adjoint_ref = near_ref if k < 4 else mid_ref if k < 6 else far_ref
        adjoint = adjoint_ref[:, columns(owner & (adjoint_ref.shape[1] // width - 1), width)].astype(F32)
        grad_u = adjoint + piece_refs[k][...].astype(F32) * long_ref[:, cols].astype(F32)
        grad_u_ref[:, cols] = grad_u
        grad_b_ref[:, cols] = (beta * grad_u * gate_ref[:, cols].astype(F32)).astype(BF16)


def pieces_taps_kernel(me_ref, fwd_ref, inv_ref, signal_ref, grad_b_ref, keep_ref, send_ref):
    tokens = grad_b_ref.shape[0]
    width = keep_ref.shape[2]
    me = me_ref[0]
    for k in range(2 * keep_ref.shape[0]):
        cols = columns(me ^ k, width)
        grad = dot(fwd_ref[:, :tokens], grad_b_ref[:, cols])
        part = dot(inv_ref[...], times_conj(signal_ref[:, cols].astype(F32), grad)).astype(BF16)
        (send_ref if k % 2 else keep_ref)[k // 2] = part


def pair_kernel(keep_ref, came_ref, kept_ref, sent_ref):
    for m in range(4):
        total = keep_ref[m].astype(F32) + came_ref[m].astype(F32)
        if m % 2:
            sent_ref[m // 2] = total.astype(BF16)
        else:
            kept_ref[m // 2] = total


def four_kernel(kept_ref, came_ref, own_ref, sent_ref):
    own_ref[...] = kept_ref[0] + came_ref[0].astype(F32)
    sent_ref[...] = (kept_ref[1] + came_ref[1].astype(F32)).astype(BF16)


def last_kernel(scale, own_ref, came_ref, out_ref):
    out_ref[...] = ((own_ref[...] + came_ref[...].astype(F32)) * scale).astype(BF16)


def pieces_input_grad_kernel(
    step, fwd_ref, inv_ref, grad_b_ref, later_ref, filt_ref, grad_u_ref, pre_ref, out_ref
):
    for start in range(0, grad_b_ref.shape[1], step):
        cols = slice(start, start + step)
        signal = dot(fwd_ref[...], stacked(grad_b_ref[:, cols], later_ref[:, cols]))
        act = dot(inv_ref[...], times_conj(signal, filt_ref[:, cols].astype(F32)))
        value = grad_u_ref[:, cols] + act * pre_ref[:, cols].astype(F32)
        out_ref[:, cols] = value.astype(BF16)


def local(body, outs, args, flops, scratch=(), vmem=24, name=None):
    moved = sum(a.size * a.dtype.itemsize for a in args)
    moved += sum(math.prod(shape) * jnp.dtype(kind).itemsize for shape, kind in outs)
    specs = [
        pl.BlockSpec(memory_space=pltpu.SMEM if a.dtype == jnp.int32 else pltpu.VMEM) for a in args
    ]
    result = pl.pallas_call(
        body,
        in_specs=specs,
        out_specs=[pl.BlockSpec(memory_space=pltpu.VMEM) for _ in outs],
        out_shape=[jax.ShapeDtypeStruct(shape, kind) for shape, kind in outs],
        scratch_shapes=list(scratch),
        compiler_params=pltpu.CompilerParams(vmem_limit_bytes=vmem * MIB),
        cost_estimate=pl.CostEstimate(flops=flops, bytes_accessed=moved, transcendentals=0),
        name=name,
    )(*args)
    return result[0] if len(result) == 1 else result


def swapped(array, k):
    count = lax.axis_size("ctx")
    return lax.ppermute(array, "ctx", [(i, i ^ k) for i in range(count)])


def after(value, *others):
    return lax.optimization_barrier((value, others))[0]


def exchanged(pieces, first=0):
    return [swapped(piece, first + k) if first + k else piece for k, piece in enumerate(pieces)]


def by_permutes(
    incoming, layer_input, pre_gate, mid_gate, long_gate, out_gate, long_filter, mid_filter
):
    sections = lax.axis_size("section")
    devices = lax.axis_size("ctx")
    half = devices // 2
    beta = (2.0 * sections) ** (-0.5)
    tokens, channels = layer_input.shape[1:]
    taps = mid_filter.shape[1]
    seq_len = tokens * devices
    scale = float(seq_len) ** (-0.5)
    owned = channels // devices

    span = tokens + max(tokens, taps)
    fwd = jnp.asarray(forward_table(span, np.arange(span)))
    inv_conv = jnp.asarray(inverse_table(span, tokens + np.arange(tokens)))
    inv_corr = jnp.asarray(inverse_table(span, np.arange(tokens)))
    inv_taps = jnp.asarray(inverse_table(span, tokens - np.arange(taps)))
    size = max(math.gcd(seq_len, 256), seq_len // 8)
    blocks = seq_len // size
    period = 2 * size
    long_fwd = jnp.asarray(forward_table(period, np.arange(-size, size)))
    long_inv = jnp.asarray(inverse_table(period, np.arange(size)))
    tile = math.gcd(owned, 256)
    spectrum = pltpu.VMEM((blocks, period, tile), F32)
    joint = pltpu.VMEM((blocks, period, tile), BF16)
    staged = pltpu.VMEM((seq_len, owned), BF16)

    rows_shape = ((tokens, channels), BF16)
    half_shape = ((tokens, channels // 2), BF16)
    quarter_shape = ((tokens, channels // 4), BF16)
    piece = ((tokens, owned), BF16)
    tap_piece = ((taps, owned), BF16)
    mid_flops = 8 * span * tokens * channels
    long_flops = 12 * period * seq_len * owned
    few = 4 * tokens * channels

    me = lax.axis_index("ctx").astype(jnp.int32)[None]
    inputs, gate_pre, gate_mid, gate_long, gate_out = (
        array[0] for array in (layer_input, pre_gate, mid_gate, long_gate, out_gate)
    )
    filter_taps = mid_filter[0]

    far = local(functools.partial(pick_kernel, (6,)), [quarter_shape], [me, incoming[0]], few, name="far")
    far = passed_along(far, "section", -1)
    mixed_in = local(mix_kernel, [rows_shape], [inputs, gate_pre], few, name="mix")
    earlier = shifted(mixed_in, "ctx", 1)
    sent = after(incoming[0], far)
    mid, near = local(
        functools.partial(pick_kernel, (4, 0)), [quarter_shape, half_shape], [me, sent], few, name="near"
    )
    mid = passed_along(mid, "section", -1)
    near = passed_along(near, "section", -1)
    far_z = local(
        functools.partial(pieces_z_kernel, beta, 6), [piece] * 2, [me, far, gate_out], few, name="farz"
    )
    mid = after(mid, far_z)
    mid_z = local(
        functools.partial(pieces_z_kernel, beta, 4), [piece] * 2, [me, mid, gate_out], few, name="midz"
    )
    signal, filt, *pieces_w = local(
        functools.partial(pieces_branch_kernel, beta),
        [((span, channels), BF16)] * 2 + [piece] * devices,
        [me, fwd, inv_conv, after(earlier, far_z), mixed_in, filter_taps, inputs, gate_mid, gate_long],
        mid_flops, name="branch",
    )
    far_z = exchanged(far_z, 6)
    near = after(near, mid_z, pieces_w)
    mid_z = exchanged(mid_z, 4)
    near_z = local(
        functools.partial(pieces_z_kernel, beta, 0), [piece] * half, [me, near, gate_out], few, name="nearz"
    )
    near_z = exchanged(near_z)
    far_w = exchanged(after(pieces_w[half:], far_z, mid_z, near_z), half)
    pieces_z = near_z + mid_z + far_z
    *pieces_g, channel_z = local(
        functools.partial(pieces_grad_w_kernel, blocks, devices),
        [piece] * devices + [((seq_len, owned), BF16)],
        [me, long_fwd, long_inv, long_filter[0], *pieces_z[::-1]], long_flops,
        [spectrum, spectrum, joint, staged], name="gradw",
    )
    far_w, near_w, pieces_g = lax.optimization_barrier((far_w, pieces_w[:half], pieces_g))
    pieces_w = exchanged(near_w) + far_w
    pieces_g = exchanged(pieces_g)[::-1]
    long_grad = local(
        functools.partial(pieces_long_grad_kernel, blocks, scale, devices), [((owned, seq_len), BF16)],
        [me, long_fwd, long_inv, channel_z, *pieces_w[::-1]], long_flops,
        [spectrum, spectrum, joint, staged], name="longgrad",
    )
    pieces_g, long_grad = lax.optimization_barrier((pieces_g, long_grad))
    grad_u, grad_b = local(
        functools.partial(pieces_grad_b_kernel, beta, devices), [((tokens, channels), F32), rows_shape],
        [me, near, mid, far, gate_long, gate_mid, *pieces_g], few, name="gradb",
    )
    later = shifted(grad_b, "ctx", -1)
    keep, send = local(
        pieces_taps_kernel, [((half, taps, owned), BF16)] * 2, [me, fwd, inv_taps, signal, grad_b],
        mid_flops, name="taps",
    )
    kept, sums = local(
        pair_kernel, [((2, taps, owned), F32), ((2, taps, owned), BF16)], [keep, swapped(send, 1)], few,
        name="pair",
    )
    own, sums = local(
        four_kernel, [((taps, owned), F32), tap_piece], [kept, swapped(sums, 2)], few, name="four"
    )
    last = swapped(sums, 4)
    later, _ = lax.optimization_barrier((later, sums))
    input_grad = local(
        functools.partial(pieces_input_grad_kernel, 512), [rows_shape],
        [fwd, inv_corr, grad_b, later, filt, grad_u, gate_pre], mid_flops, name="inputgrad",
    )
    last, input_grad = lax.optimization_barrier((last, input_grad))
    mid_grad = local(functools.partial(last_kernel, scale), [tap_piece], [own, last], few, name="midgrad")
    return (input_grad[None], long_grad[None], mid_grad[None])


def per_device(*arrays):
    devices = lax.axis_size("ctx")
    owned = arrays[0].shape[2] // devices
    if owned % 128 == 0 and devices == 8:
        return by_permutes(*arrays)
    return by_all_to_all(*arrays)


def solution(mesh):
    placed = (
        P("section", "ctx", None),
        P("section", "ctx", None),
        P("section", "ctx", None),
        P("section", "ctx", None),
        P("section", "ctx", None),
        P("section", "ctx", None),
        P("section", "ctx", None),
        P("section", None, None),
    )
    return jax.shard_map(
        per_device,
        mesh=mesh,
        in_specs=placed,
        out_specs=(P("section", "ctx", None), P("section", "ctx", None), P("section", None, "ctx")),
        check_vma=False,
    )
```

```python
import functools
import math

import jax
import jax.numpy as jnp
import numpy as np
from jax import lax
from jax.experimental import pallas as pl
from jax.experimental.pallas import tpu as pltpu
from jax.sharding import PartitionSpec as P

BF16 = jnp.bfloat16
F32 = jnp.float32
MIB = 1024 * 1024


def passed_along(value, axis, steps):
    count = lax.axis_size(axis)
    pairs = [(source, (source + steps) % count) for source in range(count)]
    return lax.ppermute(value, axis, pairs)


def shifted(array, axis, by):
    devices = lax.axis_size(axis)
    pairs = [(i, i + by) for i in range(devices) if 0 <= i + by < devices]
    return lax.ppermute(array, axis, pairs)


def forward_table(period, positions):
    angle = np.pi * np.outer(2 * np.arange(period // 2) + 1, positions) / period
    return np.concatenate([np.cos(angle), -np.sin(angle)], 0).astype(BF16)


def inverse_table(period, positions):
    angle = np.pi * np.outer(positions, 2 * np.arange(period // 2) + 1) / period
    return (np.concatenate([np.cos(angle), -np.sin(angle)], 1) * (2.0 / period)).astype(BF16)


def dot(left, right):
    return jnp.dot(left, right, preferred_element_type=F32)


def dot_nt(left, right):
    return lax.dot_general(left, right, (((1,), (1,)), ((), ())), preferred_element_type=F32)


def stacked(*rows):
    return jnp.concatenate(rows, 0)


def times(left, right):
    half = left.shape[0] // 2
    l_re, l_im, r_re, r_im = left[:half], left[half:], right[:half], right[half:]
    return jnp.concatenate(
        [(l_re * r_re - l_im * r_im).astype(BF16), (l_re * r_im + l_im * r_re).astype(BF16)], 0
    )


def times_conj(left, right):
    half = left.shape[0] // 2
    l_re, l_im, r_re, r_im = left[:half], left[half:], right[:half], right[half:]
    return jnp.concatenate(
        [(l_re * r_re + l_im * r_im).astype(BF16), (l_im * r_re - l_re * r_im).astype(BF16)], 0
    )


def put_columns(out_ref, value, start):
    owned = out_ref.shape[2]
    width = value.shape[1]
    if owned >= width:
        out_ref[start // owned, :, start % owned : start % owned + width] = value
    else:
        for j in range(width // owned):
            out_ref[start // owned + j] = value[:, j * owned : (j + 1) * owned]


def get_columns(in_ref, start, width):
    owned = in_ref.shape[2]
    if owned >= width:
        return in_ref[start // owned, :, start % owned : start % owned + width]
    return jnp.concatenate([in_ref[start // owned + j] for j in range(width // owned)], 1)


def mix_kernel(inputs_ref, gate_ref, out_ref):
    out_ref[...] = (inputs_ref[...].astype(F32) * gate_ref[...].astype(F32)).astype(BF16)


def grad_z_kernel(beta, adjoint_ref, gate_ref, out_ref):
    value = beta * adjoint_ref[...].astype(F32) * gate_ref[...].astype(F32)
    put_columns(out_ref, value.astype(BF16), 0)


def branch_kernel(
    beta, step, fwd_ref, inv_ref, earlier_ref, mixed_ref, taps_ref, inputs_ref, mid_ref, long_ref, out_ref
):
    tokens = mixed_ref.shape[0]
    taps = taps_ref.shape[0]
    for start in range(0, mixed_ref.shape[1], step):
        cols = slice(start, start + step)
        signal = dot(fwd_ref[...], stacked(earlier_ref[:, cols], mixed_ref[:, cols]))
        filt = dot(fwd_ref[:, :taps], taps_ref[:, cols])
        branch = dot(inv_ref[...], times(signal, filt))
        resid = inputs_ref[:, cols].astype(F32) + beta * branch * mid_ref[:, cols].astype(F32)
        value = (resid * long_ref[:, cols].astype(F32)).astype(BF16)
        put_columns(out_ref, value, start)


def grad_b_kernel(beta, adjoint_ref, grad_w_ref, long_ref, mid_ref, out_ref):
    grad_w = get_columns(grad_w_ref, 0, out_ref.shape[1]).astype(F32)
    grad_u = adjoint_ref[...].astype(F32) + grad_w * long_ref[...].astype(F32)
    out_ref[...] = (beta * grad_u * mid_ref[...].astype(F32)).astype(BF16)


def taps_kernel(
    step, core_ref, fwd_ref, inv_ref, earlier_ref, mixed_ref, grad_b_ref, keep_ref, send_ref
):
    tokens = mixed_ref.shape[0]
    owned = keep_ref.shape[2]
    width = min(owned, step)

    def put(even_ref, odd_ref, owner, at, value):
        ref = even_ref if owner % 2 == 0 else odd_ref
        ref[owner // 2, :, at : at + width] = value

    for start in range(0, mixed_ref.shape[1], step):
        cols = slice(start, start + step)
        signal = dot(fwd_ref[...], stacked(earlier_ref[:, cols], mixed_ref[:, cols]))
        grad = dot(fwd_ref[:, :tokens], grad_b_ref[:, cols])
        part = dot(inv_ref[...], times_conj(signal, grad)).astype(BF16)
        for j in range(0, step, width):
            owner, at = divmod(start + j, owned)
            value = part[:, j : j + width]
            pl.when(core_ref[0] == 0)(functools.partial(put, keep_ref, send_ref, owner, at, value))
            pl.when(core_ref[0] == 1)(functools.partial(put, send_ref, keep_ref, owner, at, value))


def input_grad_kernel(
    step, fwd_ref, inv_ref, grad_b_ref, later_ref, taps_ref, adjoint_ref, grad_w_ref, long_ref, pre_ref,
    out_ref,
):
    tokens = grad_b_ref.shape[0]
    taps = taps_ref.shape[0]
    for start in range(0, grad_b_ref.shape[1], step):
        cols = slice(start, start + step)
        grad_w = get_columns(grad_w_ref, start, step).astype(F32)
        grad_u = adjoint_ref[:, cols].astype(F32) + grad_w * long_ref[:, cols].astype(F32)
        signal = dot(fwd_ref[...], stacked(grad_b_ref[:, cols], later_ref[:, cols]))
        filt = dot(fwd_ref[:, :taps], taps_ref[:, cols])
        act = dot(inv_ref[...], times_conj(signal, filt))
        out_ref[:, cols] = (grad_u + act * pre_ref[:, cols].astype(F32)).astype(BF16)


def correlate(blocks, own_ref, other, joint_ref):
    period, width = joint_ref.shape[1:]
    half = period // 2
    rows, lanes = 16, math.gcd(width, 128) if width % 128 == 0 else width

    def chunk(i, _):
        at = pl.multiple_of(i * rows, rows)
        re, im = pl.ds(at, rows), pl.ds(pl.multiple_of(half + at, rows), rows)
        for start in range(0, width, lanes):
            cols = slice(start, start + lanes)
            own = [(own_ref[q, re, cols], own_ref[q, im, cols]) for q in range(blocks)]
            oth = [(other[d, re, cols], other[d, im, cols]) for d in range(blocks)]
            for p in range(blocks):
                sum_re = sum_im = None
                for q in range(p, blocks):
                    a_re, a_im = own[q]
                    b_re, b_im = oth[q - p]
                    new_re = a_re * b_re + a_im * b_im
                    new_im = a_im * b_re - a_re * b_im
                    sum_re = new_re if sum_re is None else sum_re + new_re
                    sum_im = new_im if sum_im is None else sum_im + new_im
                joint_ref[p, re, cols] = sum_re.astype(BF16)
                joint_ref[p, im, cols] = sum_im.astype(BF16)
        return 0

    lax.fori_loop(0, half // rows, chunk, 0)


def grad_w_kernel(
    blocks, fwd_ref, inv_ref, grad_ref, filt_ref, out_ref, own_ref, other_ref, joint_ref
):
    size = grad_ref.shape[0] // blocks
    for q in range(blocks):
        own_ref[q] = dot(fwd_ref[:, size:], grad_ref[q * size : (q + 1) * size])
        other = dot_nt(fwd_ref[:, size:], filt_ref[:, q * size : (q + 1) * size])
        if q:
            other += dot_nt(fwd_ref[:, :size], filt_ref[:, (q - 1) * size : q * size])
        other_ref[q] = other
    correlate(blocks, own_ref, other_ref, joint_ref)
    for p in range(blocks):
        out_ref[p * size : (p + 1) * size] = dot(inv_ref[...], joint_ref[p]).astype(BF16)


def long_grad_kernel(
    blocks, scale, fwd_ref, inv_ref, grad_ref, long_ref, out_ref, own_ref, other_ref, joint_ref
):
    size = grad_ref.shape[0] // blocks
    for q in range(blocks):
        own_ref[q] = dot(fwd_ref[:, size:], grad_ref[q * size : (q + 1) * size])
        other = dot(fwd_ref[:, size:], long_ref[q * size : (q + 1) * size])
        if q:
            other += dot(fwd_ref[:, :size], long_ref[(q - 1) * size : q * size])
        other_ref[q] = other
    correlate(blocks, own_ref, other_ref, joint_ref)
    for p in range(blocks):
        lags = (dot(inv_ref[...], joint_ref[p]) * scale).T
        out_ref[:, p * size : (p + 1) * size] = lags.astype(BF16)


def total_kernel(scale, parts_ref, out_ref):
    total = parts_ref[0].astype(F32)
    for i in range(1, parts_ref.shape[0]):
        total += parts_ref[i].astype(F32)
    out_ref[...] = (total * scale).astype(BF16)


def call(body, grid, ins, outs, args, flops, scratch=(), vmem=16, name=None):
    moved = sum(a.size * a.dtype.itemsize for a in args)
    moved += sum(math.prod(shape) * jnp.dtype(kind).itemsize for shape, kind, _ in outs)
    result = pl.pallas_call(
        body,
        grid=grid,
        in_specs=ins,
        out_specs=[spec for _, _, spec in outs],
        out_shape=[jax.ShapeDtypeStruct(shape, kind) for shape, kind, _ in outs],
        scratch_shapes=list(scratch),
        compiler_params=pltpu.CompilerParams(vmem_limit_bytes=vmem * MIB),
        cost_estimate=pl.CostEstimate(flops=flops, bytes_accessed=moved, transcendentals=0),
        name=name,
    )(*args)
    return result[0] if len(result) == 1 else result


def whole_spec(array):
    return pl.BlockSpec(array.shape, lambda i: (0,) * array.ndim)


def by_all_to_all(
    incoming, layer_input, pre_gate, mid_gate, long_gate, out_gate, long_filter, mid_filter
):
    sections = lax.axis_size("section")
    devices = lax.axis_size("ctx")
    beta = (2.0 * sections) ** (-0.5)
    tokens, channels = layer_input.shape[1:]
    taps = mid_filter.shape[1]
    seq_len = tokens * devices
    scale = float(seq_len) ** (-0.5)
    owned = channels // devices

    span = tokens + max(tokens, taps)
    fwd = jnp.asarray(forward_table(span, np.arange(span)))
    inv_conv = jnp.asarray(inverse_table(span, tokens + np.arange(tokens)))
    inv_corr = jnp.asarray(inverse_table(span, np.arange(tokens)))
    inv_taps = jnp.asarray(inverse_table(span, tokens - np.arange(taps)))
    size = max(math.gcd(seq_len, 256), seq_len // 8)
    blocks = seq_len // size
    period = 2 * size
    long_fwd = jnp.asarray(forward_table(period, np.arange(-size, size)))
    long_inv = jnp.asarray(inverse_table(period, np.arange(size)))

    wide = max(1024, 2 * owned)
    step = min(256, wide)
    grid = (channels // wide,)
    rows_spec = pl.BlockSpec((tokens, wide), lambda i: (0, i))
    taps_spec = pl.BlockSpec((taps, wide), lambda i: (0, i))
    major_spec = pl.BlockSpec((wide // owned, tokens, owned), lambda i: (i, 0, 0))
    half_major = pl.BlockSpec((wide // owned // 2, taps, owned), lambda i: (i, 0, 0))
    half_shape = (devices // 2, taps, owned)
    rows_shape = (tokens, channels)
    major_shape = (devices, tokens, owned)
    mid_flops = 8 * span * tokens * channels

    tile = math.gcd(owned, 256)
    long_grid = (owned // tile,)
    long_spec = pl.BlockSpec((seq_len, tile), lambda i: (0, i))
    lag_spec = pl.BlockSpec((tile, seq_len), lambda i: (i, 0))
    spectrum = pltpu.VMEM((blocks, period, tile), F32)
    joint = pltpu.VMEM((blocks, period, tile), BF16)
    lanes = -(-tile // 128) * 128
    long_vmem = 2 * (long_fwd.size + long_inv.size) * 2 + 20 * blocks * period * lanes
    long_vmem = -(-long_vmem // MIB) + 6
    long_flops = 4 * period * seq_len * owned

    inputs, gate_pre, gate_mid, gate_long, gate_out = (
        array[0] for array in (layer_input, pre_gate, mid_gate, long_gate, out_gate)
    )
    filter_taps = mid_filter[0]

    adjoint = passed_along(incoming[0], "section", -1)
    mixed_in = call(
        mix_kernel, grid, [rows_spec] * 2, [(rows_shape, BF16, rows_spec)], [inputs, gate_pre],
        2 * tokens * channels, name="mix",
    )
    earlier = shifted(mixed_in, "ctx", 1)
    adjoint, earlier = lax.optimization_barrier((adjoint, earlier))
    grad_z = call(
        functools.partial(grad_z_kernel, beta), grid, [rows_spec] * 2,
        [(major_shape, BF16, major_spec)], [adjoint, gate_out], 2 * tokens * channels, name="gradz",
    )
    grad_z, earlier = lax.optimization_barrier((grad_z, earlier))
    channel_z = lax.all_to_all(grad_z, "ctx", split_axis=0, concat_axis=0, tiled=True)
    long_in = call(
        functools.partial(branch_kernel, beta, step), grid,
        [whole_spec(fwd), whole_spec(inv_conv)] + [rows_spec] * 2 + [taps_spec] + [rows_spec] * 3,
        [(major_shape, BF16, major_spec)],
        [fwd, inv_conv, earlier, mixed_in, filter_taps, inputs, gate_mid, gate_long], mid_flops,
        name="branch",
    )
    channel_z, long_in = lax.optimization_barrier((channel_z, long_in))
    channel_w = lax.all_to_all(long_in, "ctx", split_axis=0, concat_axis=0, tiled=True)
    channel_z = channel_z.reshape(seq_len, owned)
    grad_w = call(
        functools.partial(grad_w_kernel, blocks), long_grid,
        [whole_spec(long_fwd), whole_spec(long_inv), long_spec, lag_spec],
        [((seq_len, owned), BF16, long_spec)], [long_fwd, long_inv, channel_z, long_filter[0]],
        2 * long_flops, [spectrum, spectrum, joint], long_vmem, "gradw",
    )
    grad_w, channel_w = lax.optimization_barrier((grad_w, channel_w))
    returned = lax.all_to_all(
        grad_w.reshape(major_shape), "ctx", split_axis=0, concat_axis=0, tiled=True
    )
    channel_w = channel_w.reshape(seq_len, owned)
    long_grad = call(
        functools.partial(long_grad_kernel, blocks, scale), long_grid,
        [whole_spec(long_fwd), whole_spec(long_inv), long_spec, long_spec],
        [((owned, seq_len), BF16, lag_spec)], [long_fwd, long_inv, channel_z, channel_w],
        2 * long_flops, [spectrum, spectrum, joint], long_vmem, "longgrad",
    )
    returned, long_grad = lax.optimization_barrier((returned, long_grad))
    grad_b = call(
        functools.partial(grad_b_kernel, beta), grid,
        [rows_spec, major_spec] + [rows_spec] * 2, [(rows_shape, BF16, rows_spec)],
        [adjoint, returned, gate_long, gate_mid], 4 * tokens * channels, name="gradb",
    )
    later = shifted(grad_b, "ctx", -1)
    core = (lax.axis_index("ctx") % 2).astype(jnp.int32)[None]
    keep, send = call(
        functools.partial(taps_kernel, step), grid,
        [pl.BlockSpec(memory_space=pltpu.SMEM), whole_spec(fwd), whole_spec(inv_taps)]
        + [rows_spec] * 3,
        [(half_shape, BF16, half_major)] * 2,
        [core, fwd, inv_taps, earlier, mixed_in, grad_b], mid_flops, name="taps",
    )
    partner = lax.ppermute(send, "ctx", [(i, i ^ 1) for i in range(devices)])
    chip_parts = (keep.astype(F32) + partner.astype(F32)).astype(BF16)
    gathered = lax.all_to_all(
        chip_parts, "ctx", split_axis=0, concat_axis=0, tiled=True,
        axis_index_groups=[list(range(c, devices, 2)) for c in range(2)],
    )
    later, _ = lax.optimization_barrier((later, chip_parts))
    input_grad = call(
        functools.partial(input_grad_kernel, step), grid,
        [whole_spec(fwd), whole_spec(inv_corr)] + [rows_spec] * 2 + [taps_spec, rows_spec, major_spec]
        + [rows_spec] * 2,
        [(rows_shape, BF16, rows_spec)],
        [fwd, inv_corr, grad_b, later, filter_taps, adjoint, returned, gate_long, gate_pre],
        mid_flops, name="inputgrad",
    )
    mid_grad = call(
        functools.partial(total_kernel, scale), (1,), [whole_spec(gathered)],
        [((taps, owned), BF16, pl.BlockSpec((taps, owned), lambda i: (0, 0)))], [gathered],
        devices * taps * owned, name="midgrad",
    )
    return (input_grad[None], long_grad[None], mid_grad[None])


def columns(index, width):
    return pl.ds(pl.multiple_of(index * width, width), width)


def pick_kernel(firsts, me_ref, in_ref, *out_refs):
    for first, out_ref in zip(firsts, out_refs):
        width = out_ref.shape[1]
        owned = in_ref.shape[1] // 8
        out_ref[...] = in_ref[:, columns((me_ref[0] ^ first) // (width // owned), width)]


def pieces_z_kernel(beta, first, me_ref, adjoint_ref, gate_ref, *out_refs):
    count = len(out_refs)
    width = out_refs[0].shape[1]
    me = me_ref[0]
    for k in range(count):
        owner = me ^ (first + k)
        part = adjoint_ref[:, columns(owner & (count - 1), width)].astype(F32)
        gate = gate_ref[:, columns(owner, width)].astype(F32)
        out_refs[k][...] = (beta * part * gate).astype(BF16)


def pieces_branch_kernel(
    beta, me_ref, fwd_ref, inv_ref, earlier_ref, mixed_ref, taps_ref, inputs_ref, mid_ref, long_ref,
    signal_ref, filt_ref, *out_refs,
):
    taps = taps_ref.shape[0]
    width = out_refs[0].shape[1]
    me = me_ref[0]
    count = len(out_refs)
    for k in list(range(count // 2, count)) + list(range(count // 2)):
        cols = columns(me ^ k, width)
        signal = dot(fwd_ref[...], stacked(earlier_ref[:, cols], mixed_ref[:, cols]))
        filt = dot(fwd_ref[:, :taps], taps_ref[:, cols])
        signal_ref[:, cols] = signal.astype(BF16)
        filt_ref[:, cols] = filt.astype(BF16)
        branch = dot(inv_ref[...], times(signal, filt))
        resid = inputs_ref[:, cols].astype(F32) + beta * branch * mid_ref[:, cols].astype(F32)
        out_refs[k][...] = (resid * long_ref[:, cols].astype(F32)).astype(BF16)


def spectra(blocks, fwd_ref, array_ref, cols, out_ref):
    size = array_ref.shape[0] // blocks
    for q in range(blocks):
        out_ref[q] = dot(fwd_ref[:, size:], array_ref[q * size : (q + 1) * size, cols])


def extended_spectra(blocks, fwd_ref, array_ref, cols, out_ref):
    size = array_ref.shape[0] // blocks
    out_ref[0] = dot(fwd_ref[:, size:], array_ref[:size, cols])
    for q in range(1, blocks):
        out_ref[q] = dot(fwd_ref[...], array_ref[(q - 1) * size : (q + 1) * size, cols])


def pieces_grad_w_kernel(blocks, count, me_ref, fwd_ref, inv_ref, filt_ref, *refs):
    piece_refs, out_refs = refs[:count][::-1], refs[count : 2 * count]
    whole_ref, own_ref, other_ref, joint_ref, result_ref = refs[2 * count :]
    rows = piece_refs[0].shape[0]
    size = whole_ref.shape[0] // blocks
    tile = joint_ref.shape[2]
    me = me_ref[0]
    for k in range(count):
        whole_ref[columns(me ^ k, rows), :] = piece_refs[k][...]
    for start in range(0, whole_ref.shape[1], tile):
        cols = slice(start, start + tile)
        spectra(blocks, fwd_ref, whole_ref, cols, own_ref)
        other_ref[0] = dot_nt(fwd_ref[:, size:], filt_ref[cols, :size])
        for q in range(1, blocks):
            other_ref[q] = dot_nt(fwd_ref[...], filt_ref[cols, (q - 1) * size : (q + 1) * size])
        correlate(blocks, own_ref, other_ref, joint_ref)
        for p in range(blocks):
            result_ref[p * size : (p + 1) * size, cols] = dot(inv_ref[...], joint_ref[p]).astype(BF16)
    for k in range(count):
        out_refs[k][...] = result_ref[columns(me ^ k, rows), :]


def pieces_long_grad_kernel(blocks, scale, count, me_ref, fwd_ref, inv_ref, grad_ref, *refs):
    piece_refs, out_ref = refs[:count][::-1], refs[count]
    own_ref, other_ref, joint_ref, whole_ref = refs[count + 1 :]
    rows = piece_refs[0].shape[0]
    size = whole_ref.shape[0] // blocks
    tile = joint_ref.shape[2]
    me = me_ref[0]
    for k in range(count):
        whole_ref[columns(me ^ k, rows), :] = piece_refs[k][...]
    for start in range(0, whole_ref.shape[1], tile):
        cols = slice(start, start + tile)
        spectra(blocks, fwd_ref, grad_ref, cols, own_ref)
        extended_spectra(blocks, fwd_ref, whole_ref, cols, other_ref)
        correlate(blocks, own_ref, other_ref, joint_ref)
        for p in range(blocks):
            lags = (dot(inv_ref[...], joint_ref[p]) * scale).T
            out_ref[cols, p * size : (p + 1) * size] = lags.astype(BF16)


def pieces_grad_b_kernel(beta, count, me_ref, near_ref, far_ref, long_ref, gate_ref, *refs):
    piece_refs, (grad_u_ref, grad_b_ref) = refs[:count][::-1], refs[count:]
    width = piece_refs[0].shape[1]
    me = me_ref[0]
    for k in range(count):
        owner = me ^ k
        cols = columns(owner, width)
        adjoint_ref = near_ref if k < count // 2 else far_ref
        adjoint = adjoint_ref[:, columns(owner & (adjoint_ref.shape[1] // width - 1), width)].astype(F32)
        grad_u = adjoint + piece_refs[k][...].astype(F32) * long_ref[:, cols].astype(F32)
        grad_u_ref[:, cols] = grad_u
        grad_b_ref[:, cols] = (beta * grad_u * gate_ref[:, cols].astype(F32)).astype(BF16)


def pieces_taps_kernel(me_ref, fwd_ref, inv_ref, signal_ref, grad_b_ref, keep_ref, send_ref):
    tokens = grad_b_ref.shape[0]
    width = keep_ref.shape[2]
    me = me_ref[0]
    for k in range(2 * keep_ref.shape[0]):
        cols = columns(me ^ k, width)
        grad = dot(fwd_ref[:, :tokens], grad_b_ref[:, cols])
        part = dot(inv_ref[...], times_conj(signal_ref[:, cols].astype(F32), grad)).astype(BF16)
        (send_ref if k % 2 else keep_ref)[k // 2] = part


def pair_kernel(keep_ref, came_ref, *out_refs):
    for m, out_ref in enumerate(out_refs):
        out_ref[...] = (keep_ref[m].astype(F32) + came_ref[m].astype(F32)).astype(BF16)


def pieces_total_kernel(scale, *refs):
    total = refs[0][...].astype(F32)
    for ref in refs[1:-1]:
        total += ref[...].astype(F32)
    refs[-1][...] = (total * scale).astype(BF16)


def pieces_input_grad_kernel(
    step, fwd_ref, inv_ref, grad_b_ref, later_ref, filt_ref, grad_u_ref, pre_ref, out_ref
):
    for start in range(0, grad_b_ref.shape[1], step):
        cols = slice(start, start + step)
        signal = dot(fwd_ref[...], stacked(grad_b_ref[:, cols], later_ref[:, cols]))
        act = dot(inv_ref[...], times_conj(signal, filt_ref[:, cols].astype(F32)))
        value = grad_u_ref[:, cols] + act * pre_ref[:, cols].astype(F32)
        out_ref[:, cols] = value.astype(BF16)


def local(body, outs, args, flops, scratch=(), vmem=24, name=None):
    moved = sum(a.size * a.dtype.itemsize for a in args)
    moved += sum(math.prod(shape) * jnp.dtype(kind).itemsize for shape, kind in outs)
    specs = [
        pl.BlockSpec(memory_space=pltpu.SMEM if a.dtype == jnp.int32 else pltpu.VMEM) for a in args
    ]
    result = pl.pallas_call(
        body,
        in_specs=specs,
        out_specs=[pl.BlockSpec(memory_space=pltpu.VMEM) for _ in outs],
        out_shape=[jax.ShapeDtypeStruct(shape, kind) for shape, kind in outs],
        scratch_shapes=list(scratch),
        compiler_params=pltpu.CompilerParams(vmem_limit_bytes=vmem * MIB),
        cost_estimate=pl.CostEstimate(flops=flops, bytes_accessed=moved, transcendentals=0),
        name=name,
    )(*args)
    return result[0] if len(result) == 1 else result


def swapped(array, k):
    count = lax.axis_size("ctx")
    return lax.ppermute(array, "ctx", [(i, i ^ k) for i in range(count)])


def after(value, *others):
    return lax.optimization_barrier((value, others))[0]


def exchanged(pieces, first=0):
    return [swapped(piece, first + k) if first + k else piece for k, piece in enumerate(pieces)]


def in_turn(pieces, *before):
    came_7 = swapped(after(pieces[3], before[1]), 7)
    came_6 = swapped(after(pieces[2], before[0]), 6)
    came_5 = swapped(after(pieces[1], came_7), 5)
    came_4 = swapped(after(pieces[0], came_6), 4)
    return [came_4, came_5, came_6, came_7]


def by_permutes(
    incoming, layer_input, pre_gate, mid_gate, long_gate, out_gate, long_filter, mid_filter
):
    sections = lax.axis_size("section")
    devices = lax.axis_size("ctx")
    half = devices // 2
    beta = (2.0 * sections) ** (-0.5)
    tokens, channels = layer_input.shape[1:]
    taps = mid_filter.shape[1]
    seq_len = tokens * devices
    scale = float(seq_len) ** (-0.5)
    owned = channels // devices

    span = tokens + max(tokens, taps)
    fwd = jnp.asarray(forward_table(span, np.arange(span)))
    inv_conv = jnp.asarray(inverse_table(span, tokens + np.arange(tokens)))
    inv_corr = jnp.asarray(inverse_table(span, np.arange(tokens)))
    inv_taps = jnp.asarray(inverse_table(span, tokens - np.arange(taps)))
    size = max(math.gcd(seq_len, 256), seq_len // 8)
    blocks = seq_len // size
    period = 2 * size
    long_fwd = jnp.asarray(forward_table(period, np.arange(-size, size)))
    long_inv = jnp.asarray(inverse_table(period, np.arange(size)))
    tile = math.gcd(owned, 256)
    spectrum = pltpu.VMEM((blocks, period, tile), F32)
    joint = pltpu.VMEM((blocks, period, tile), BF16)
    staged = pltpu.VMEM((seq_len, owned), BF16)

    rows_shape = ((tokens, channels), BF16)
    half_shape = ((tokens, channels // 2), BF16)
    piece = ((tokens, owned), BF16)
    tap_piece = ((taps, owned), BF16)
    mid_flops = 8 * span * tokens * channels
    long_flops = 12 * period * seq_len * owned
    few = 4 * tokens * channels

    me = lax.axis_index("ctx").astype(jnp.int32)[None]
    inputs, gate_pre, gate_mid, gate_long, gate_out = (
        array[0] for array in (layer_input, pre_gate, mid_gate, long_gate, out_gate)
    )
    filter_taps = mid_filter[0]

    far = local(functools.partial(pick_kernel, (4,)), [half_shape], [me, incoming[0]], few, name="far")
    far = passed_along(far, "section", -1)
    mixed_in = local(mix_kernel, [rows_shape], [inputs, gate_pre], few, name="mix")
    earlier = shifted(mixed_in, "ctx", 1)
    sent = after(incoming[0], far)
    near = local(functools.partial(pick_kernel, (0,)), [half_shape], [me, sent], few, name="near")
    near = passed_along(near, "section", -1)
    far_z = local(
        functools.partial(pieces_z_kernel, beta, half), [piece] * half, [me, far, gate_out], few, name="farz"
    )
    signal, filt, *pieces_w = local(
        functools.partial(pieces_branch_kernel, beta),
        [((span, channels), BF16)] * 2 + [piece] * devices,
        [me, fwd, inv_conv, after(earlier, far_z), mixed_in, filter_taps, inputs, gate_mid, gate_long],
        mid_flops, name="branch",
    )
    far_z = in_turn(far_z, far_z, far_z)
    near = after(near, pieces_w)
    near_z = local(
        functools.partial(pieces_z_kernel, beta, 0), [piece] * half, [me, near, gate_out], few, name="nearz"
    )
    far_w = in_turn(pieces_w[half:], far_z[0], far_z[1])
    pieces_z = exchanged(near_z) + far_z
    *pieces_g, channel_z = local(
        functools.partial(pieces_grad_w_kernel, blocks, devices),
        [piece] * devices + [((seq_len, owned), BF16)],
        [me, long_fwd, long_inv, long_filter[0], *pieces_z[::-1]], long_flops,
        [spectrum, spectrum, joint, staged], name="gradw",
    )
    near_w = after(pieces_w[:half], far_w[2], far_w[3], pieces_g)
    pieces_w = exchanged(near_w) + far_w
    far_g = in_turn(pieces_g[half:], far_w[0], far_w[1])
    near_g = exchanged(after(pieces_g[:half], far_g[2], far_g[3]))
    pieces_g = far_g[::-1] + near_g[::-1]
    long_grad = local(
        functools.partial(pieces_long_grad_kernel, blocks, scale, devices), [((owned, seq_len), BF16)],
        [me, long_fwd, long_inv, channel_z, *pieces_w[::-1]], long_flops,
        [spectrum, spectrum, joint, staged], name="longgrad",
    )
    pieces_g, long_grad = lax.optimization_barrier((pieces_g, long_grad))
    grad_u, grad_b = local(
        functools.partial(pieces_grad_b_kernel, beta, devices), [((tokens, channels), F32), rows_shape],
        [me, near, far, gate_long, gate_mid, *pieces_g], few, name="gradb",
    )
    later = shifted(grad_b, "ctx", -1)
    keep, send = local(
        pieces_taps_kernel, [((half, taps, owned), BF16)] * 2, [me, fwd, inv_taps, signal, grad_b],
        mid_flops, name="taps",
    )
    sums = local(pair_kernel, [tap_piece] * half, [keep, swapped(send, 1)], few, name="pair")
    sums = [swapped(sums[m], 2 * m) for m in (3, 2, 1)] + [sums[0]]
    later = after(later, sums[-1])
    input_grad = local(
        functools.partial(pieces_input_grad_kernel, 512), [rows_shape],
        [fwd, inv_corr, grad_b, later, filt, grad_u, gate_pre], mid_flops, name="inputgrad",
    )
    sums, input_grad = lax.optimization_barrier((sums, input_grad))
    mid_grad = local(functools.partial(pieces_total_kernel, scale), [tap_piece], sums, few, name="midgrad")
    return (input_grad[None], long_grad[None], mid_grad[None])


def per_device(*arrays):
    devices = lax.axis_size("ctx")
    owned = arrays[0].shape[2] // devices
    if owned % 128 == 0 and devices == 8:
        return by_permutes(*arrays)
    return by_all_to_all(*arrays)


def solution(mesh):
    placed = (
        P("section", "ctx", None),
        P("section", "ctx", None),
        P("section", "ctx", None),
        P("section", "ctx", None),
        P("section", "ctx", None),
        P("section", "ctx", None),
        P("section", "ctx", None),
        P("section", None, None),
    )
    return jax.shard_map(
        per_device,
        mesh=mesh,
        in_specs=placed,
        out_specs=(P("section", "ctx", None), P("section", "ctx", None), P("section", None, "ctx")),
        check_vma=False,
    )
```

```python
import functools
import math

import jax
import jax.numpy as jnp
import numpy as np
from jax import lax
from jax.experimental import pallas as pl
from jax.experimental.pallas import tpu as pltpu
from jax.sharding import PartitionSpec as P

BF16 = jnp.bfloat16
F32 = jnp.float32
MIB = 1024 * 1024


def passed_along(value, axis, steps):
    count = lax.axis_size(axis)
    pairs = [(source, (source + steps) % count) for source in range(count)]
    return lax.ppermute(value, axis, pairs)


def shifted(array, axis, by):
    devices = lax.axis_size(axis)
    pairs = [(i, i + by) for i in range(devices) if 0 <= i + by < devices]
    return lax.ppermute(array, axis, pairs)


def forward_table(period, positions):
    angle = np.pi * np.outer(2 * np.arange(period // 2) + 1, positions) / period
    return np.concatenate([np.cos(angle), -np.sin(angle)], 0).astype(BF16)


def inverse_table(period, positions):
    angle = np.pi * np.outer(positions, 2 * np.arange(period // 2) + 1) / period
    return (np.concatenate([np.cos(angle), -np.sin(angle)], 1) * (2.0 / period)).astype(BF16)


def dot(left, right):
    return jnp.dot(left, right, preferred_element_type=F32)


def dot_nt(left, right):
    return lax.dot_general(left, right, (((1,), (1,)), ((), ())), preferred_element_type=F32)


def stacked(*rows):
    return jnp.concatenate(rows, 0)


def times(left, right):
    half = left.shape[0] // 2
    l_re, l_im, r_re, r_im = left[:half], left[half:], right[:half], right[half:]
    return jnp.concatenate(
        [(l_re * r_re - l_im * r_im).astype(BF16), (l_re * r_im + l_im * r_re).astype(BF16)], 0
    )


def times_conj(left, right):
    half = left.shape[0] // 2
    l_re, l_im, r_re, r_im = left[:half], left[half:], right[:half], right[half:]
    return jnp.concatenate(
        [(l_re * r_re + l_im * r_im).astype(BF16), (l_im * r_re - l_re * r_im).astype(BF16)], 0
    )


def put_columns(out_ref, value, start):
    owned = out_ref.shape[2]
    width = value.shape[1]
    if owned >= width:
        out_ref[start // owned, :, start % owned : start % owned + width] = value
    else:
        for j in range(width // owned):
            out_ref[start // owned + j] = value[:, j * owned : (j + 1) * owned]


def get_columns(in_ref, start, width):
    owned = in_ref.shape[2]
    if owned >= width:
        return in_ref[start // owned, :, start % owned : start % owned + width]
    return jnp.concatenate([in_ref[start // owned + j] for j in range(width // owned)], 1)


def mix_kernel(inputs_ref, gate_ref, out_ref):
    out_ref[...] = (inputs_ref[...].astype(F32) * gate_ref[...].astype(F32)).astype(BF16)


def grad_z_kernel(beta, adjoint_ref, gate_ref, out_ref):
    value = beta * adjoint_ref[...].astype(F32) * gate_ref[...].astype(F32)
    put_columns(out_ref, value.astype(BF16), 0)


def branch_kernel(
    beta, step, fwd_ref, inv_ref, earlier_ref, mixed_ref, taps_ref, inputs_ref, mid_ref, long_ref, out_ref
):
    tokens = mixed_ref.shape[0]
    taps = taps_ref.shape[0]
    for start in range(0, mixed_ref.shape[1], step):
        cols = slice(start, start + step)
        signal = dot(fwd_ref[...], stacked(earlier_ref[:, cols], mixed_ref[:, cols]))
        filt = dot(fwd_ref[:, :taps], taps_ref[:, cols])
        branch = dot(inv_ref[...], times(signal, filt))
        resid = inputs_ref[:, cols].astype(F32) + beta * branch * mid_ref[:, cols].astype(F32)
        value = (resid * long_ref[:, cols].astype(F32)).astype(BF16)
        put_columns(out_ref, value, start)


def grad_b_kernel(beta, adjoint_ref, grad_w_ref, long_ref, mid_ref, out_ref):
    grad_w = get_columns(grad_w_ref, 0, out_ref.shape[1]).astype(F32)
    grad_u = adjoint_ref[...].astype(F32) + grad_w * long_ref[...].astype(F32)
    out_ref[...] = (beta * grad_u * mid_ref[...].astype(F32)).astype(BF16)


def taps_kernel(
    step, core_ref, fwd_ref, inv_ref, earlier_ref, mixed_ref, grad_b_ref, keep_ref, send_ref
):
    tokens = mixed_ref.shape[0]
    owned = keep_ref.shape[2]
    width = min(owned, step)

    def put(even_ref, odd_ref, owner, at, value):
        ref = even_ref if owner % 2 == 0 else odd_ref
        ref[owner // 2, :, at : at + width] = value

    for start in range(0, mixed_ref.shape[1], step):
        cols = slice(start, start + step)
        signal = dot(fwd_ref[...], stacked(earlier_ref[:, cols], mixed_ref[:, cols]))
        grad = dot(fwd_ref[:, :tokens], grad_b_ref[:, cols])
        part = dot(inv_ref[...], times_conj(signal, grad)).astype(BF16)
        for j in range(0, step, width):
            owner, at = divmod(start + j, owned)
            value = part[:, j : j + width]
            pl.when(core_ref[0] == 0)(functools.partial(put, keep_ref, send_ref, owner, at, value))
            pl.when(core_ref[0] == 1)(functools.partial(put, send_ref, keep_ref, owner, at, value))


def input_grad_kernel(
    step, fwd_ref, inv_ref, grad_b_ref, later_ref, taps_ref, adjoint_ref, grad_w_ref, long_ref, pre_ref,
    out_ref,
):
    tokens = grad_b_ref.shape[0]
    taps = taps_ref.shape[0]
    for start in range(0, grad_b_ref.shape[1], step):
        cols = slice(start, start + step)
        grad_w = get_columns(grad_w_ref, start, step).astype(F32)
        grad_u = adjoint_ref[:, cols].astype(F32) + grad_w * long_ref[:, cols].astype(F32)
        signal = dot(fwd_ref[...], stacked(grad_b_ref[:, cols], later_ref[:, cols]))
        filt = dot(fwd_ref[:, :taps], taps_ref[:, cols])
        act = dot(inv_ref[...], times_conj(signal, filt))
        out_ref[:, cols] = (grad_u + act * pre_ref[:, cols].astype(F32)).astype(BF16)


def correlate(blocks, own_ref, other, joint_ref):
    period, width = joint_ref.shape[1:]
    half = period // 2
    rows, lanes = 16, math.gcd(width, 128) if width % 128 == 0 else width

    def chunk(i, _):
        at = pl.multiple_of(i * rows, rows)
        re, im = pl.ds(at, rows), pl.ds(pl.multiple_of(half + at, rows), rows)
        for start in range(0, width, lanes):
            cols = slice(start, start + lanes)
            own = [(own_ref[q, re, cols], own_ref[q, im, cols]) for q in range(blocks)]
            oth = [(other[d, re, cols], other[d, im, cols]) for d in range(blocks)]
            for p in range(blocks):
                sum_re = sum_im = None
                for q in range(p, blocks):
                    a_re, a_im = own[q]
                    b_re, b_im = oth[q - p]
                    new_re = a_re * b_re + a_im * b_im
                    new_im = a_im * b_re - a_re * b_im
                    sum_re = new_re if sum_re is None else sum_re + new_re
                    sum_im = new_im if sum_im is None else sum_im + new_im
                joint_ref[p, re, cols] = sum_re.astype(BF16)
                joint_ref[p, im, cols] = sum_im.astype(BF16)
        return 0

    lax.fori_loop(0, half // rows, chunk, 0)


def grad_w_kernel(
    blocks, fwd_ref, inv_ref, grad_ref, filt_ref, out_ref, own_ref, other_ref, joint_ref
):
    size = grad_ref.shape[0] // blocks
    for q in range(blocks):
        own_ref[q] = dot(fwd_ref[:, size:], grad_ref[q * size : (q + 1) * size])
        other = dot_nt(fwd_ref[:, size:], filt_ref[:, q * size : (q + 1) * size])
        if q:
            other += dot_nt(fwd_ref[:, :size], filt_ref[:, (q - 1) * size : q * size])
        other_ref[q] = other
    correlate(blocks, own_ref, other_ref, joint_ref)
    for p in range(blocks):
        out_ref[p * size : (p + 1) * size] = dot(inv_ref[...], joint_ref[p]).astype(BF16)


def long_grad_kernel(
    blocks, scale, fwd_ref, inv_ref, grad_ref, long_ref, out_ref, own_ref, other_ref, joint_ref
):
    size = grad_ref.shape[0] // blocks
    for q in range(blocks):
        own_ref[q] = dot(fwd_ref[:, size:], grad_ref[q * size : (q + 1) * size])
        other = dot(fwd_ref[:, size:], long_ref[q * size : (q + 1) * size])
        if q:
            other += dot(fwd_ref[:, :size], long_ref[(q - 1) * size : q * size])
        other_ref[q] = other
    correlate(blocks, own_ref, other_ref, joint_ref)
    for p in range(blocks):
        lags = (dot(inv_ref[...], joint_ref[p]) * scale).T
        out_ref[:, p * size : (p + 1) * size] = lags.astype(BF16)


def total_kernel(scale, parts_ref, out_ref):
    total = parts_ref[0].astype(F32)
    for i in range(1, parts_ref.shape[0]):
        total += parts_ref[i].astype(F32)
    out_ref[...] = (total * scale).astype(BF16)


def call(body, grid, ins, outs, args, flops, scratch=(), vmem=16, name=None):
    moved = sum(a.size * a.dtype.itemsize for a in args)
    moved += sum(math.prod(shape) * jnp.dtype(kind).itemsize for shape, kind, _ in outs)
    result = pl.pallas_call(
        body,
        grid=grid,
        in_specs=ins,
        out_specs=[spec for _, _, spec in outs],
        out_shape=[jax.ShapeDtypeStruct(shape, kind) for shape, kind, _ in outs],
        scratch_shapes=list(scratch),
        compiler_params=pltpu.CompilerParams(vmem_limit_bytes=vmem * MIB),
        cost_estimate=pl.CostEstimate(flops=flops, bytes_accessed=moved, transcendentals=0),
        name=name,
    )(*args)
    return result[0] if len(result) == 1 else result


def whole_spec(array):
    return pl.BlockSpec(array.shape, lambda i: (0,) * array.ndim)


def by_all_to_all(
    incoming, layer_input, pre_gate, mid_gate, long_gate, out_gate, long_filter, mid_filter
):
    sections = lax.axis_size("section")
    devices = lax.axis_size("ctx")
    beta = (2.0 * sections) ** (-0.5)
    tokens, channels = layer_input.shape[1:]
    taps = mid_filter.shape[1]
    seq_len = tokens * devices
    scale = float(seq_len) ** (-0.5)
    owned = channels // devices

    span = tokens + max(tokens, taps)
    fwd = jnp.asarray(forward_table(span, np.arange(span)))
    inv_conv = jnp.asarray(inverse_table(span, tokens + np.arange(tokens)))
    inv_corr = jnp.asarray(inverse_table(span, np.arange(tokens)))
    inv_taps = jnp.asarray(inverse_table(span, tokens - np.arange(taps)))
    size = max(math.gcd(seq_len, 256), seq_len // 8)
    blocks = seq_len // size
    period = 2 * size
    long_fwd = jnp.asarray(forward_table(period, np.arange(-size, size)))
    long_inv = jnp.asarray(inverse_table(period, np.arange(size)))

    wide = max(1024, 2 * owned)
    step = min(256, wide)
    grid = (channels // wide,)
    rows_spec = pl.BlockSpec((tokens, wide), lambda i: (0, i))
    taps_spec = pl.BlockSpec((taps, wide), lambda i: (0, i))
    major_spec = pl.BlockSpec((wide // owned, tokens, owned), lambda i: (i, 0, 0))
    half_major = pl.BlockSpec((wide // owned // 2, taps, owned), lambda i: (i, 0, 0))
    half_shape = (devices // 2, taps, owned)
    rows_shape = (tokens, channels)
    major_shape = (devices, tokens, owned)
    mid_flops = 8 * span * tokens * channels

    tile = math.gcd(owned, 256)
    long_grid = (owned // tile,)
    long_spec = pl.BlockSpec((seq_len, tile), lambda i: (0, i))
    lag_spec = pl.BlockSpec((tile, seq_len), lambda i: (i, 0))
    spectrum = pltpu.VMEM((blocks, period, tile), F32)
    joint = pltpu.VMEM((blocks, period, tile), BF16)
    lanes = -(-tile // 128) * 128
    long_vmem = 2 * (long_fwd.size + long_inv.size) * 2 + 20 * blocks * period * lanes
    long_vmem = -(-long_vmem // MIB) + 6
    long_flops = 4 * period * seq_len * owned

    inputs, gate_pre, gate_mid, gate_long, gate_out = (
        array[0] for array in (layer_input, pre_gate, mid_gate, long_gate, out_gate)
    )
    filter_taps = mid_filter[0]

    adjoint = passed_along(incoming[0], "section", -1)
    mixed_in = call(
        mix_kernel, grid, [rows_spec] * 2, [(rows_shape, BF16, rows_spec)], [inputs, gate_pre],
        2 * tokens * channels, name="mix",
    )
    earlier = shifted(mixed_in, "ctx", 1)
    adjoint, earlier = lax.optimization_barrier((adjoint, earlier))
    grad_z = call(
        functools.partial(grad_z_kernel, beta), grid, [rows_spec] * 2,
        [(major_shape, BF16, major_spec)], [adjoint, gate_out], 2 * tokens * channels, name="gradz",
    )
    grad_z, earlier = lax.optimization_barrier((grad_z, earlier))
    channel_z = lax.all_to_all(grad_z, "ctx", split_axis=0, concat_axis=0, tiled=True)
    long_in = call(
        functools.partial(branch_kernel, beta, step), grid,
        [whole_spec(fwd), whole_spec(inv_conv)] + [rows_spec] * 2 + [taps_spec] + [rows_spec] * 3,
        [(major_shape, BF16, major_spec)],
        [fwd, inv_conv, earlier, mixed_in, filter_taps, inputs, gate_mid, gate_long], mid_flops,
        name="branch",
    )
    channel_z, long_in = lax.optimization_barrier((channel_z, long_in))
    channel_w = lax.all_to_all(long_in, "ctx", split_axis=0, concat_axis=0, tiled=True)
    channel_z = channel_z.reshape(seq_len, owned)
    grad_w = call(
        functools.partial(grad_w_kernel, blocks), long_grid,
        [whole_spec(long_fwd), whole_spec(long_inv), long_spec, lag_spec],
        [((seq_len, owned), BF16, long_spec)], [long_fwd, long_inv, channel_z, long_filter[0]],
        2 * long_flops, [spectrum, spectrum, joint], long_vmem, "gradw",
    )
    grad_w, channel_w = lax.optimization_barrier((grad_w, channel_w))
    returned = lax.all_to_all(
        grad_w.reshape(major_shape), "ctx", split_axis=0, concat_axis=0, tiled=True
    )
    channel_w = channel_w.reshape(seq_len, owned)
    long_grad = call(
        functools.partial(long_grad_kernel, blocks, scale), long_grid,
        [whole_spec(long_fwd), whole_spec(long_inv), long_spec, long_spec],
        [((owned, seq_len), BF16, lag_spec)], [long_fwd, long_inv, channel_z, channel_w],
        2 * long_flops, [spectrum, spectrum, joint], long_vmem, "longgrad",
    )
    returned, long_grad = lax.optimization_barrier((returned, long_grad))
    grad_b = call(
        functools.partial(grad_b_kernel, beta), grid,
        [rows_spec, major_spec] + [rows_spec] * 2, [(rows_shape, BF16, rows_spec)],
        [adjoint, returned, gate_long, gate_mid], 4 * tokens * channels, name="gradb",
    )
    later = shifted(grad_b, "ctx", -1)
    core = (lax.axis_index("ctx") % 2).astype(jnp.int32)[None]
    keep, send = call(
        functools.partial(taps_kernel, step), grid,
        [pl.BlockSpec(memory_space=pltpu.SMEM), whole_spec(fwd), whole_spec(inv_taps)]
        + [rows_spec] * 3,
        [(half_shape, BF16, half_major)] * 2,
        [core, fwd, inv_taps, earlier, mixed_in, grad_b], mid_flops, name="taps",
    )
    partner = lax.ppermute(send, "ctx", [(i, i ^ 1) for i in range(devices)])
    chip_parts = (keep.astype(F32) + partner.astype(F32)).astype(BF16)
    gathered = lax.all_to_all(
        chip_parts, "ctx", split_axis=0, concat_axis=0, tiled=True,
        axis_index_groups=[list(range(c, devices, 2)) for c in range(2)],
    )
    later, _ = lax.optimization_barrier((later, chip_parts))
    input_grad = call(
        functools.partial(input_grad_kernel, step), grid,
        [whole_spec(fwd), whole_spec(inv_corr)] + [rows_spec] * 2 + [taps_spec, rows_spec, major_spec]
        + [rows_spec] * 2,
        [(rows_shape, BF16, rows_spec)],
        [fwd, inv_corr, grad_b, later, filter_taps, adjoint, returned, gate_long, gate_pre],
        mid_flops, name="inputgrad",
    )
    mid_grad = call(
        functools.partial(total_kernel, scale), (1,), [whole_spec(gathered)],
        [((taps, owned), BF16, pl.BlockSpec((taps, owned), lambda i: (0, 0)))], [gathered],
        devices * taps * owned, name="midgrad",
    )
    return (input_grad[None], long_grad[None], mid_grad[None])


def columns(index, width):
    return pl.ds(pl.multiple_of(index * width, width), width)


def pick_kernel(firsts, me_ref, in_ref, *out_refs):
    for first, out_ref in zip(firsts, out_refs):
        width = out_ref.shape[1]
        owned = in_ref.shape[1] // 8
        out_ref[...] = in_ref[:, columns((me_ref[0] ^ first) // (width // owned), width)]


def pieces_z_kernel(beta, first, me_ref, adjoint_ref, gate_ref, *out_refs):
    count = len(out_refs)
    width = out_refs[0].shape[1]
    me = me_ref[0]
    for k in range(count):
        owner = me ^ (first + k)
        part = adjoint_ref[:, columns(owner & (count - 1), width)].astype(F32)
        gate = gate_ref[:, columns(owner, width)].astype(F32)
        out_refs[k][...] = (beta * part * gate).astype(BF16)


def pieces_branch_kernel(
    beta, me_ref, fwd_ref, inv_ref, earlier_ref, mixed_ref, taps_ref, inputs_ref, mid_ref, long_ref,
    signal_ref, filt_ref, *out_refs,
):
    taps = taps_ref.shape[0]
    width = out_refs[0].shape[1]
    me = me_ref[0]
    count = len(out_refs)
    for k in list(range(count // 2, count)) + list(range(count // 2)):
        cols = columns(me ^ k, width)
        signal = dot(fwd_ref[...], stacked(earlier_ref[:, cols], mixed_ref[:, cols]))
        filt = dot(fwd_ref[:, :taps], taps_ref[:, cols])
        signal_ref[:, cols] = signal.astype(BF16)
        filt_ref[:, cols] = filt.astype(BF16)
        branch = dot(inv_ref[...], times(signal, filt))
        resid = inputs_ref[:, cols].astype(F32) + beta * branch * mid_ref[:, cols].astype(F32)
        out_refs[k][...] = (resid * long_ref[:, cols].astype(F32)).astype(BF16)


def spectra(blocks, fwd_ref, array_ref, cols, out_ref):
    size = array_ref.shape[0] // blocks
    for q in range(blocks):
        out_ref[q] = dot(fwd_ref[:, size:], array_ref[q * size : (q + 1) * size, cols])


def extended_spectra(blocks, fwd_ref, array_ref, cols, out_ref):
    size = array_ref.shape[0] // blocks
    out_ref[0] = dot(fwd_ref[:, size:], array_ref[:size, cols])
    for q in range(1, blocks):
        out_ref[q] = dot(fwd_ref[...], array_ref[(q - 1) * size : (q + 1) * size, cols])


def pieces_grad_w_kernel(blocks, count, me_ref, fwd_ref, inv_ref, filt_ref, *refs):
    piece_refs, out_refs = refs[:count][::-1], refs[count : 2 * count]
    whole_ref, own_ref, other_ref, joint_ref, result_ref = refs[2 * count :]
    rows = piece_refs[0].shape[0]
    size = whole_ref.shape[0] // blocks
    tile = joint_ref.shape[2]
    me = me_ref[0]
    for k in range(count):
        whole_ref[columns(me ^ k, rows), :] = piece_refs[k][...]
    for start in range(0, whole_ref.shape[1], tile):
        cols = slice(start, start + tile)
        spectra(blocks, fwd_ref, whole_ref, cols, own_ref)
        other_ref[0] = dot_nt(fwd_ref[:, size:], filt_ref[cols, :size])
        for q in range(1, blocks):
            other_ref[q] = dot_nt(fwd_ref[...], filt_ref[cols, (q - 1) * size : (q + 1) * size])
        correlate(blocks, own_ref, other_ref, joint_ref)
        for p in range(blocks):
            result_ref[p * size : (p + 1) * size, cols] = dot(inv_ref[...], joint_ref[p]).astype(BF16)
    for k in range(count):
        out_refs[k][...] = result_ref[columns(me ^ k, rows), :]


def pieces_long_grad_kernel(blocks, scale, count, me_ref, fwd_ref, inv_ref, grad_ref, *refs):
    piece_refs, out_ref = refs[:count][::-1], refs[count]
    own_ref, other_ref, joint_ref, whole_ref = refs[count + 1 :]
    rows = piece_refs[0].shape[0]
    size = whole_ref.shape[0] // blocks
    tile = joint_ref.shape[2]
    me = me_ref[0]
    for k in range(count):
        whole_ref[columns(me ^ k, rows), :] = piece_refs[k][...]
    for start in range(0, whole_ref.shape[1], tile):
        cols = slice(start, start + tile)
        spectra(blocks, fwd_ref, grad_ref, cols, own_ref)
        extended_spectra(blocks, fwd_ref, whole_ref, cols, other_ref)
        correlate(blocks, own_ref, other_ref, joint_ref)
        for p in range(blocks):
            lags = (dot(inv_ref[...], joint_ref[p]) * scale).T
            out_ref[cols, p * size : (p + 1) * size] = lags.astype(BF16)


def pieces_grad_b_kernel(beta, count, me_ref, near_ref, far_ref, long_ref, gate_ref, *refs):
    piece_refs, (grad_u_ref, grad_b_ref) = refs[:count][::-1], refs[count:]
    width = piece_refs[0].shape[1]
    me = me_ref[0]
    for k in range(count):
        owner = me ^ k
        cols = columns(owner, width)
        adjoint_ref = near_ref if k < count // 2 else far_ref
        adjoint = adjoint_ref[:, columns(owner & (adjoint_ref.shape[1] // width - 1), width)].astype(F32)
        grad_u = adjoint + piece_refs[k][...].astype(F32) * long_ref[:, cols].astype(F32)
        grad_u_ref[:, cols] = grad_u
        grad_b_ref[:, cols] = (beta * grad_u * gate_ref[:, cols].astype(F32)).astype(BF16)


def pieces_taps_kernel(me_ref, fwd_ref, inv_ref, signal_ref, grad_b_ref, keep_ref, send_ref):
    tokens = grad_b_ref.shape[0]
    width = keep_ref.shape[2]
    me = me_ref[0]
    for k in range(2 * keep_ref.shape[0]):
        cols = columns(me ^ k, width)
        grad = dot(fwd_ref[:, :tokens], grad_b_ref[:, cols])
        part = dot(inv_ref[...], times_conj(signal_ref[:, cols].astype(F32), grad)).astype(BF16)
        (send_ref if k % 2 else keep_ref)[k // 2] = part


def pair_kernel(keep_ref, came_ref, *out_refs):
    for m, out_ref in enumerate(out_refs):
        out_ref[...] = (keep_ref[m].astype(F32) + came_ref[m].astype(F32)).astype(BF16)


def pieces_total_kernel(scale, *refs):
    total = refs[0][...].astype(F32)
    for ref in refs[1:-1]:
        total += ref[...].astype(F32)
    refs[-1][...] = (total * scale).astype(BF16)


def pieces_input_grad_kernel(
    step, fwd_ref, inv_ref, grad_b_ref, later_ref, filt_ref, grad_u_ref, pre_ref, out_ref
):
    for start in range(0, grad_b_ref.shape[1], step):
        cols = slice(start, start + step)
        signal = dot(fwd_ref[...], stacked(grad_b_ref[:, cols], later_ref[:, cols]))
        act = dot(inv_ref[...], times_conj(signal, filt_ref[:, cols].astype(F32)))
        value = grad_u_ref[:, cols] + act * pre_ref[:, cols].astype(F32)
        out_ref[:, cols] = value.astype(BF16)


def local(body, outs, args, flops, scratch=(), vmem=24, name=None):
    moved = sum(a.size * a.dtype.itemsize for a in args)
    moved += sum(math.prod(shape) * jnp.dtype(kind).itemsize for shape, kind in outs)
    specs = [
        pl.BlockSpec(memory_space=pltpu.SMEM if a.dtype == jnp.int32 else pltpu.VMEM) for a in args
    ]
    result = pl.pallas_call(
        body,
        in_specs=specs,
        out_specs=[pl.BlockSpec(memory_space=pltpu.VMEM) for _ in outs],
        out_shape=[jax.ShapeDtypeStruct(shape, kind) for shape, kind in outs],
        scratch_shapes=list(scratch),
        compiler_params=pltpu.CompilerParams(vmem_limit_bytes=vmem * MIB),
        cost_estimate=pl.CostEstimate(flops=flops, bytes_accessed=moved, transcendentals=0),
        name=name,
    )(*args)
    return result[0] if len(result) == 1 else result


def swapped(array, k):
    count = lax.axis_size("ctx")
    return lax.ppermute(array, "ctx", [(i, i ^ k) for i in range(count)])


def after(value, *others):
    return lax.optimization_barrier((value, others))[0]


def exchanged(pieces, first=0):
    return [swapped(piece, first + k) if first + k else piece for k, piece in enumerate(pieces)]


def far_pair(pieces, first, *before):
    if before:
        pieces = [after(piece, other) for piece, other in zip(pieces, before)]
    return exchanged(pieces, first)


def by_permutes(
    incoming, layer_input, pre_gate, mid_gate, long_gate, out_gate, long_filter, mid_filter
):
    sections = lax.axis_size("section")
    devices = lax.axis_size("ctx")
    half = devices // 2
    beta = (2.0 * sections) ** (-0.5)
    tokens, channels = layer_input.shape[1:]
    taps = mid_filter.shape[1]
    seq_len = tokens * devices
    scale = float(seq_len) ** (-0.5)
    owned = channels // devices

    span = tokens + max(tokens, taps)
    fwd = jnp.asarray(forward_table(span, np.arange(span)))
    inv_conv = jnp.asarray(inverse_table(span, tokens + np.arange(tokens)))
    inv_corr = jnp.asarray(inverse_table(span, np.arange(tokens)))
    inv_taps = jnp.asarray(inverse_table(span, tokens - np.arange(taps)))
    size = max(math.gcd(seq_len, 256), seq_len // 8)
    blocks = seq_len // size
    period = 2 * size
    long_fwd = jnp.asarray(forward_table(period, np.arange(-size, size)))
    long_inv = jnp.asarray(inverse_table(period, np.arange(size)))
    tile = math.gcd(owned, 256)
    spectrum = pltpu.VMEM((blocks, period, tile), F32)
    joint = pltpu.VMEM((blocks, period, tile), BF16)
    staged = pltpu.VMEM((seq_len, owned), BF16)

    rows_shape = ((tokens, channels), BF16)
    half_shape = ((tokens, channels // 2), BF16)
    piece = ((tokens, owned), BF16)
    tap_piece = ((taps, owned), BF16)
    mid_flops = 8 * span * tokens * channels
    long_flops = 12 * period * seq_len * owned
    few = 4 * tokens * channels

    me = lax.axis_index("ctx").astype(jnp.int32)[None]
    inputs, gate_pre, gate_mid, gate_long, gate_out = (
        array[0] for array in (layer_input, pre_gate, mid_gate, long_gate, out_gate)
    )
    filter_taps = mid_filter[0]

    far = local(functools.partial(pick_kernel, (4,)), [half_shape], [me, incoming[0]], few, name="far")
    far = passed_along(far, "section", -1)
    mixed_in = local(mix_kernel, [rows_shape], [inputs, gate_pre], few, name="mix")
    earlier = shifted(mixed_in, "ctx", 1)
    sent = after(incoming[0], far)
    near = local(functools.partial(pick_kernel, (0,)), [half_shape], [me, sent], few, name="near")
    near = passed_along(near, "section", -1)
    far_z = local(
        functools.partial(pieces_z_kernel, beta, half), [piece] * half, [me, far, gate_out], few, name="farz"
    )
    near_z = local(
        functools.partial(pieces_z_kernel, beta, 0), [piece] * half, [me, near, gate_out], few, name="nearz"
    )
    signal, filt, *pieces_w = local(
        functools.partial(pieces_branch_kernel, beta),
        [((span, channels), BF16)] * 2 + [piece] * devices,
        [me, fwd, inv_conv, after(earlier, near_z), mixed_in, filter_taps, inputs, gate_mid, gate_long],
        mid_flops, name="branch",
    )
    z_6, z_7 = far_pair(far_z[2:], 6)
    z_4, z_5 = far_pair(far_z[:2], 4, z_6, z_7)
    near_z = exchanged(near_z)
    pieces_z = near_z + [z_4, z_5, z_6, z_7]
    w_6, w_7 = far_pair(pieces_w[6:], 6, (z_4, near_z), (z_5, near_z))
    near_w = exchanged(pieces_w[:half])
    *pieces_g, channel_z = local(
        functools.partial(pieces_grad_w_kernel, blocks, devices),
        [piece] * devices + [((seq_len, owned), BF16)],
        [me, long_fwd, long_inv, long_filter[0], *pieces_z[::-1]], long_flops,
        [spectrum, spectrum, joint, staged], name="gradw",
    )
    w_4, w_5 = far_pair(pieces_w[4:6], 4, (w_6, near_w, pieces_g[0]), (w_7, near_w, pieces_g[0]))
    pieces_w = near_w + [w_4, w_5, w_6, w_7]
    near_g = exchanged(pieces_g[:half])
    g_6, g_7 = far_pair(pieces_g[6:], 6, (w_4, near_g), (w_5, near_g))
    g_4, g_5 = far_pair(pieces_g[4:6], 4, g_6, g_7)
    pieces_g = [g_7, g_6, g_5, g_4] + near_g[::-1]
    long_grad = local(
        functools.partial(pieces_long_grad_kernel, blocks, scale, devices), [((owned, seq_len), BF16)],
        [me, long_fwd, long_inv, channel_z, *pieces_w[::-1]], long_flops,
        [spectrum, spectrum, joint, staged], name="longgrad",
    )
    pieces_g, long_grad = lax.optimization_barrier((pieces_g, long_grad))
    grad_u, grad_b = local(
        functools.partial(pieces_grad_b_kernel, beta, devices), [((tokens, channels), F32), rows_shape],
        [me, near, far, gate_long, gate_mid, *pieces_g], few, name="gradb",
    )
    later = shifted(grad_b, "ctx", -1)
    keep, send = local(
        pieces_taps_kernel, [((half, taps, owned), BF16)] * 2, [me, fwd, inv_taps, signal, grad_b],
        mid_flops, name="taps",
    )
    sums = local(pair_kernel, [tap_piece] * half, [keep, swapped(send, 1)], few, name="pair")
    sums = [swapped(sums[m], 2 * m) for m in (3, 2, 1)] + [sums[0]]
    later = after(later, sums[-1])
    input_grad = local(
        functools.partial(pieces_input_grad_kernel, 512), [rows_shape],
        [fwd, inv_corr, grad_b, later, filt, grad_u, gate_pre], mid_flops, name="inputgrad",
    )
    sums, input_grad = lax.optimization_barrier((sums, input_grad))
    mid_grad = local(functools.partial(pieces_total_kernel, scale), [tap_piece], sums, few, name="midgrad")
    return (input_grad[None], long_grad[None], mid_grad[None])


def per_device(*arrays):
    devices = lax.axis_size("ctx")
    owned = arrays[0].shape[2] // devices
    if owned % 128 == 0 and devices == 8:
        return by_permutes(*arrays)
    return by_all_to_all(*arrays)


def solution(mesh):
    placed = (
        P("section", "ctx", None),
        P("section", "ctx", None),
        P("section", "ctx", None),
        P("section", "ctx", None),
        P("section", "ctx", None),
        P("section", "ctx", None),
        P("section", "ctx", None),
        P("section", None, None),
    )
    return jax.shard_map(
        per_device,
        mesh=mesh,
        in_specs=placed,
        out_specs=(P("section", "ctx", None), P("section", "ctx", None), P("section", None, "ctx")),
        check_vma=False,
    )
```

```python
import functools
import math

import jax
import jax.numpy as jnp
import numpy as np
from jax import lax
from jax.experimental import pallas as pl
from jax.experimental.pallas import tpu as pltpu
from jax.sharding import PartitionSpec as P

BF16 = jnp.bfloat16
F32 = jnp.float32
MIB = 1024 * 1024


def passed_along(value, axis, steps):
    count = lax.axis_size(axis)
    pairs = [(source, (source + steps) % count) for source in range(count)]
    return lax.ppermute(value, axis, pairs)


def shifted(array, axis, by):
    devices = lax.axis_size(axis)
    pairs = [(i, i + by) for i in range(devices) if 0 <= i + by < devices]
    return lax.ppermute(array, axis, pairs)


def forward_table(period, positions):
    angle = np.pi * np.outer(2 * np.arange(period // 2) + 1, positions) / period
    return np.concatenate([np.cos(angle), -np.sin(angle)], 0).astype(BF16)


def inverse_table(period, positions):
    angle = np.pi * np.outer(positions, 2 * np.arange(period // 2) + 1) / period
    return (np.concatenate([np.cos(angle), -np.sin(angle)], 1) * (2.0 / period)).astype(BF16)


def dot(left, right):
    return jnp.dot(left, right, preferred_element_type=F32)


def dot_nt(left, right):
    return lax.dot_general(left, right, (((1,), (1,)), ((), ())), preferred_element_type=F32)


def stacked(*rows):
    return jnp.concatenate(rows, 0)


def times(left, right):
    half = left.shape[0] // 2
    l_re, l_im, r_re, r_im = left[:half], left[half:], right[:half], right[half:]
    return jnp.concatenate(
        [(l_re * r_re - l_im * r_im).astype(BF16), (l_re * r_im + l_im * r_re).astype(BF16)], 0
    )


def times_conj(left, right):
    half = left.shape[0] // 2
    l_re, l_im, r_re, r_im = left[:half], left[half:], right[:half], right[half:]
    return jnp.concatenate(
        [(l_re * r_re + l_im * r_im).astype(BF16), (l_im * r_re - l_re * r_im).astype(BF16)], 0
    )


def put_columns(out_ref, value, start):
    owned = out_ref.shape[2]
    width = value.shape[1]
    if owned >= width:
        out_ref[start // owned, :, start % owned : start % owned + width] = value
    else:
        for j in range(width // owned):
            out_ref[start // owned + j] = value[:, j * owned : (j + 1) * owned]


def get_columns(in_ref, start, width):
    owned = in_ref.shape[2]
    if owned >= width:
        return in_ref[start // owned, :, start % owned : start % owned + width]
    return jnp.concatenate([in_ref[start // owned + j] for j in range(width // owned)], 1)


def mix_kernel(inputs_ref, gate_ref, out_ref):
    out_ref[...] = (inputs_ref[...].astype(F32) * gate_ref[...].astype(F32)).astype(BF16)


def grad_z_kernel(beta, adjoint_ref, gate_ref, out_ref):
    value = beta * adjoint_ref[...].astype(F32) * gate_ref[...].astype(F32)
    put_columns(out_ref, value.astype(BF16), 0)


def branch_kernel(
    beta, step, fwd_ref, inv_ref, earlier_ref, mixed_ref, taps_ref, inputs_ref, mid_ref, long_ref, out_ref
):
    tokens = mixed_ref.shape[0]
    taps = taps_ref.shape[0]
    for start in range(0, mixed_ref.shape[1], step):
        cols = slice(start, start + step)
        signal = dot(fwd_ref[...], stacked(earlier_ref[:, cols], mixed_ref[:, cols]))
        filt = dot(fwd_ref[:, :taps], taps_ref[:, cols])
        branch = dot(inv_ref[...], times(signal, filt))
        resid = inputs_ref[:, cols].astype(F32) + beta * branch * mid_ref[:, cols].astype(F32)
        value = (resid * long_ref[:, cols].astype(F32)).astype(BF16)
        put_columns(out_ref, value, start)


def grad_b_kernel(beta, adjoint_ref, grad_w_ref, long_ref, mid_ref, out_ref):
    grad_w = get_columns(grad_w_ref, 0, out_ref.shape[1]).astype(F32)
    grad_u = adjoint_ref[...].astype(F32) + grad_w * long_ref[...].astype(F32)
    out_ref[...] = (beta * grad_u * mid_ref[...].astype(F32)).astype(BF16)


def taps_kernel(
    step, core_ref, fwd_ref, inv_ref, earlier_ref, mixed_ref, grad_b_ref, keep_ref, send_ref
):
    tokens = mixed_ref.shape[0]
    owned = keep_ref.shape[2]
    width = min(owned, step)

    def put(even_ref, odd_ref, owner, at, value):
        ref = even_ref if owner % 2 == 0 else odd_ref
        ref[owner // 2, :, at : at + width] = value

    for start in range(0, mixed_ref.shape[1], step):
        cols = slice(start, start + step)
        signal = dot(fwd_ref[...], stacked(earlier_ref[:, cols], mixed_ref[:, cols]))
        grad = dot(fwd_ref[:, :tokens], grad_b_ref[:, cols])
        part = dot(inv_ref[...], times_conj(signal, grad)).astype(BF16)
        for j in range(0, step, width):
            owner, at = divmod(start + j, owned)
            value = part[:, j : j + width]
            pl.when(core_ref[0] == 0)(functools.partial(put, keep_ref, send_ref, owner, at, value))
            pl.when(core_ref[0] == 1)(functools.partial(put, send_ref, keep_ref, owner, at, value))


def input_grad_kernel(
    step, fwd_ref, inv_ref, grad_b_ref, later_ref, taps_ref, adjoint_ref, grad_w_ref, long_ref, pre_ref,
    out_ref,
):
    tokens = grad_b_ref.shape[0]
    taps = taps_ref.shape[0]
    for start in range(0, grad_b_ref.shape[1], step):
        cols = slice(start, start + step)
        grad_w = get_columns(grad_w_ref, start, step).astype(F32)
        grad_u = adjoint_ref[:, cols].astype(F32) + grad_w * long_ref[:, cols].astype(F32)
        signal = dot(fwd_ref[...], stacked(grad_b_ref[:, cols], later_ref[:, cols]))
        filt = dot(fwd_ref[:, :taps], taps_ref[:, cols])
        act = dot(inv_ref[...], times_conj(signal, filt))
        out_ref[:, cols] = (grad_u + act * pre_ref[:, cols].astype(F32)).astype(BF16)


def correlate(blocks, own_ref, other, joint_ref):
    period, width = joint_ref.shape[1:]
    half = period // 2
    rows, lanes = 16, math.gcd(width, 128) if width % 128 == 0 else width

    def chunk(i, _):
        at = pl.multiple_of(i * rows, rows)
        re, im = pl.ds(at, rows), pl.ds(pl.multiple_of(half + at, rows), rows)
        for start in range(0, width, lanes):
            cols = slice(start, start + lanes)
            own = [(own_ref[q, re, cols], own_ref[q, im, cols]) for q in range(blocks)]
            oth = [(other[d, re, cols], other[d, im, cols]) for d in range(blocks)]
            for p in range(blocks):
                sum_re = sum_im = None
                for q in range(p, blocks):
                    a_re, a_im = own[q]
                    b_re, b_im = oth[q - p]
                    new_re = a_re * b_re + a_im * b_im
                    new_im = a_im * b_re - a_re * b_im
                    sum_re = new_re if sum_re is None else sum_re + new_re
                    sum_im = new_im if sum_im is None else sum_im + new_im
                joint_ref[p, re, cols] = sum_re.astype(BF16)
                joint_ref[p, im, cols] = sum_im.astype(BF16)
        return 0

    lax.fori_loop(0, half // rows, chunk, 0)


def grad_w_kernel(
    blocks, fwd_ref, inv_ref, grad_ref, filt_ref, out_ref, own_ref, other_ref, joint_ref
):
    size = grad_ref.shape[0] // blocks
    for q in range(blocks):
        own_ref[q] = dot(fwd_ref[:, size:], grad_ref[q * size : (q + 1) * size])
        other = dot_nt(fwd_ref[:, size:], filt_ref[:, q * size : (q + 1) * size])
        if q:
            other += dot_nt(fwd_ref[:, :size], filt_ref[:, (q - 1) * size : q * size])
        other_ref[q] = other
    correlate(blocks, own_ref, other_ref, joint_ref)
    for p in range(blocks):
        out_ref[p * size : (p + 1) * size] = dot(inv_ref[...], joint_ref[p]).astype(BF16)


def long_grad_kernel(
    blocks, scale, fwd_ref, inv_ref, grad_ref, long_ref, out_ref, own_ref, other_ref, joint_ref
):
    size = grad_ref.shape[0] // blocks
    for q in range(blocks):
        own_ref[q] = dot(fwd_ref[:, size:], grad_ref[q * size : (q + 1) * size])
        other = dot(fwd_ref[:, size:], long_ref[q * size : (q + 1) * size])
        if q:
            other += dot(fwd_ref[:, :size], long_ref[(q - 1) * size : q * size])
        other_ref[q] = other
    correlate(blocks, own_ref, other_ref, joint_ref)
    for p in range(blocks):
        lags = (dot(inv_ref[...], joint_ref[p]) * scale).T
        out_ref[:, p * size : (p + 1) * size] = lags.astype(BF16)


def total_kernel(scale, parts_ref, out_ref):
    total = parts_ref[0].astype(F32)
    for i in range(1, parts_ref.shape[0]):
        total += parts_ref[i].astype(F32)
    out_ref[...] = (total * scale).astype(BF16)


def call(body, grid, ins, outs, args, flops, scratch=(), vmem=16, name=None):
    moved = sum(a.size * a.dtype.itemsize for a in args)
    moved += sum(math.prod(shape) * jnp.dtype(kind).itemsize for shape, kind, _ in outs)
    result = pl.pallas_call(
        body,
        grid=grid,
        in_specs=ins,
        out_specs=[spec for _, _, spec in outs],
        out_shape=[jax.ShapeDtypeStruct(shape, kind) for shape, kind, _ in outs],
        scratch_shapes=list(scratch),
        compiler_params=pltpu.CompilerParams(vmem_limit_bytes=vmem * MIB),
        cost_estimate=pl.CostEstimate(flops=flops, bytes_accessed=moved, transcendentals=0),
        name=name,
    )(*args)
    return result[0] if len(result) == 1 else result


def whole_spec(array):
    return pl.BlockSpec(array.shape, lambda i: (0,) * array.ndim)


def by_all_to_all(
    incoming, layer_input, pre_gate, mid_gate, long_gate, out_gate, long_filter, mid_filter
):
    sections = lax.axis_size("section")
    devices = lax.axis_size("ctx")
    beta = (2.0 * sections) ** (-0.5)
    tokens, channels = layer_input.shape[1:]
    taps = mid_filter.shape[1]
    seq_len = tokens * devices
    scale = float(seq_len) ** (-0.5)
    owned = channels // devices

    span = tokens + max(tokens, taps)
    fwd = jnp.asarray(forward_table(span, np.arange(span)))
    inv_conv = jnp.asarray(inverse_table(span, tokens + np.arange(tokens)))
    inv_corr = jnp.asarray(inverse_table(span, np.arange(tokens)))
    inv_taps = jnp.asarray(inverse_table(span, tokens - np.arange(taps)))
    size = max(math.gcd(seq_len, 256), seq_len // 8)
    blocks = seq_len // size
    period = 2 * size
    long_fwd = jnp.asarray(forward_table(period, np.arange(-size, size)))
    long_inv = jnp.asarray(inverse_table(period, np.arange(size)))

    wide = max(1024, 2 * owned)
    step = min(256, wide)
    grid = (channels // wide,)
    rows_spec = pl.BlockSpec((tokens, wide), lambda i: (0, i))
    taps_spec = pl.BlockSpec((taps, wide), lambda i: (0, i))
    major_spec = pl.BlockSpec((wide // owned, tokens, owned), lambda i: (i, 0, 0))
    half_major = pl.BlockSpec((wide // owned // 2, taps, owned), lambda i: (i, 0, 0))
    half_shape = (devices // 2, taps, owned)
    rows_shape = (tokens, channels)
    major_shape = (devices, tokens, owned)
    mid_flops = 8 * span * tokens * channels

    tile = math.gcd(owned, 256)
    long_grid = (owned // tile,)
    long_spec = pl.BlockSpec((seq_len, tile), lambda i: (0, i))
    lag_spec = pl.BlockSpec((tile, seq_len), lambda i: (i, 0))
    spectrum = pltpu.VMEM((blocks, period, tile), F32)
    joint = pltpu.VMEM((blocks, period, tile), BF16)
    lanes = -(-tile // 128) * 128
    long_vmem = 2 * (long_fwd.size + long_inv.size) * 2 + 20 * blocks * period * lanes
    long_vmem = -(-long_vmem // MIB) + 6
    long_flops = 4 * period * seq_len * owned

    inputs, gate_pre, gate_mid, gate_long, gate_out = (
        array[0] for array in (layer_input, pre_gate, mid_gate, long_gate, out_gate)
    )
    filter_taps = mid_filter[0]

    adjoint = passed_along(incoming[0], "section", -1)
    mixed_in = call(
        mix_kernel, grid, [rows_spec] * 2, [(rows_shape, BF16, rows_spec)], [inputs, gate_pre],
        2 * tokens * channels, name="mix",
    )
    earlier = shifted(mixed_in, "ctx", 1)
    adjoint, earlier = lax.optimization_barrier((adjoint, earlier))
    grad_z = call(
        functools.partial(grad_z_kernel, beta), grid, [rows_spec] * 2,
        [(major_shape, BF16, major_spec)], [adjoint, gate_out], 2 * tokens * channels, name="gradz",
    )
    grad_z, earlier = lax.optimization_barrier((grad_z, earlier))
    channel_z = lax.all_to_all(grad_z, "ctx", split_axis=0, concat_axis=0, tiled=True)
    long_in = call(
        functools.partial(branch_kernel, beta, step), grid,
        [whole_spec(fwd), whole_spec(inv_conv)] + [rows_spec] * 2 + [taps_spec] + [rows_spec] * 3,
        [(major_shape, BF16, major_spec)],
        [fwd, inv_conv, earlier, mixed_in, filter_taps, inputs, gate_mid, gate_long], mid_flops,
        name="branch",
    )
    channel_z, long_in = lax.optimization_barrier((channel_z, long_in))
    channel_w = lax.all_to_all(long_in, "ctx", split_axis=0, concat_axis=0, tiled=True)
    channel_z = channel_z.reshape(seq_len, owned)
    grad_w = call(
        functools.partial(grad_w_kernel, blocks), long_grid,
        [whole_spec(long_fwd), whole_spec(long_inv), long_spec, lag_spec],
        [((seq_len, owned), BF16, long_spec)], [long_fwd, long_inv, channel_z, long_filter[0]],
        2 * long_flops, [spectrum, spectrum, joint], long_vmem, "gradw",
    )
    grad_w, channel_w = lax.optimization_barrier((grad_w, channel_w))
    returned = lax.all_to_all(
        grad_w.reshape(major_shape), "ctx", split_axis=0, concat_axis=0, tiled=True
    )
    channel_w = channel_w.reshape(seq_len, owned)
    long_grad = call(
        functools.partial(long_grad_kernel, blocks, scale), long_grid,
        [whole_spec(long_fwd), whole_spec(long_inv), long_spec, long_spec],
        [((owned, seq_len), BF16, lag_spec)], [long_fwd, long_inv, channel_z, channel_w],
        2 * long_flops, [spectrum, spectrum, joint], long_vmem, "longgrad",
    )
    returned, long_grad = lax.optimization_barrier((returned, long_grad))
    grad_b = call(
        functools.partial(grad_b_kernel, beta), grid,
        [rows_spec, major_spec] + [rows_spec] * 2, [(rows_shape, BF16, rows_spec)],
        [adjoint, returned, gate_long, gate_mid], 4 * tokens * channels, name="gradb",
    )
    later = shifted(grad_b, "ctx", -1)
    core = (lax.axis_index("ctx") % 2).astype(jnp.int32)[None]
    keep, send = call(
        functools.partial(taps_kernel, step), grid,
        [pl.BlockSpec(memory_space=pltpu.SMEM), whole_spec(fwd), whole_spec(inv_taps)]
        + [rows_spec] * 3,
        [(half_shape, BF16, half_major)] * 2,
        [core, fwd, inv_taps, earlier, mixed_in, grad_b], mid_flops, name="taps",
    )
    partner = lax.ppermute(send, "ctx", [(i, i ^ 1) for i in range(devices)])
    chip_parts = (keep.astype(F32) + partner.astype(F32)).astype(BF16)
    gathered = lax.all_to_all(
        chip_parts, "ctx", split_axis=0, concat_axis=0, tiled=True,
        axis_index_groups=[list(range(c, devices, 2)) for c in range(2)],
    )
    later, _ = lax.optimization_barrier((later, chip_parts))
    input_grad = call(
        functools.partial(input_grad_kernel, step), grid,
        [whole_spec(fwd), whole_spec(inv_corr)] + [rows_spec] * 2 + [taps_spec, rows_spec, major_spec]
        + [rows_spec] * 2,
        [(rows_shape, BF16, rows_spec)],
        [fwd, inv_corr, grad_b, later, filter_taps, adjoint, returned, gate_long, gate_pre],
        mid_flops, name="inputgrad",
    )
    mid_grad = call(
        functools.partial(total_kernel, scale), (1,), [whole_spec(gathered)],
        [((taps, owned), BF16, pl.BlockSpec((taps, owned), lambda i: (0, 0)))], [gathered],
        devices * taps * owned, name="midgrad",
    )
    return (input_grad[None], long_grad[None], mid_grad[None])


def columns(index, width):
    return pl.ds(pl.multiple_of(index * width, width), width)


def pick_kernel(firsts, me_ref, in_ref, *out_refs):
    for first, out_ref in zip(firsts, out_refs):
        width = out_ref.shape[1]
        owned = in_ref.shape[1] // 8
        out_ref[...] = in_ref[:, columns((me_ref[0] ^ first) // (width // owned), width)]


def pieces_z_kernel(beta, first, me_ref, adjoint_ref, gate_ref, *out_refs):
    count = len(out_refs)
    width = out_refs[0].shape[1]
    me = me_ref[0]
    for k in range(count):
        owner = me ^ (first + k)
        part = adjoint_ref[:, columns(owner & (count - 1), width)].astype(F32)
        gate = gate_ref[:, columns(owner, width)].astype(F32)
        out_refs[k][...] = (beta * part * gate).astype(BF16)


def pieces_branch_kernel(
    beta, me_ref, fwd_ref, inv_ref, earlier_ref, mixed_ref, taps_ref, inputs_ref, mid_ref, long_ref,
    signal_ref, filt_ref, *out_refs,
):
    taps = taps_ref.shape[0]
    width = out_refs[0].shape[1]
    me = me_ref[0]
    count = len(out_refs)
    for k in list(range(count // 2, count)) + list(range(count // 2)):
        cols = columns(me ^ k, width)
        signal = dot(fwd_ref[...], stacked(earlier_ref[:, cols], mixed_ref[:, cols]))
        filt = dot(fwd_ref[:, :taps], taps_ref[:, cols])
        signal_ref[:, cols] = signal.astype(BF16)
        filt_ref[:, cols] = filt.astype(BF16)
        branch = dot(inv_ref[...], times(signal, filt))
        resid = inputs_ref[:, cols].astype(F32) + beta * branch * mid_ref[:, cols].astype(F32)
        out_refs[k][...] = (resid * long_ref[:, cols].astype(F32)).astype(BF16)


def spectra(blocks, fwd_ref, array_ref, cols, out_ref):
    size = array_ref.shape[0] // blocks
    for q in range(blocks):
        out_ref[q] = dot(fwd_ref[:, size:], array_ref[q * size : (q + 1) * size, cols])


def extended_spectra(blocks, fwd_ref, array_ref, cols, out_ref):
    size = array_ref.shape[0] // blocks
    out_ref[0] = dot(fwd_ref[:, size:], array_ref[:size, cols])
    for q in range(1, blocks):
        out_ref[q] = dot(fwd_ref[...], array_ref[(q - 1) * size : (q + 1) * size, cols])


def pieces_grad_w_kernel(blocks, count, me_ref, fwd_ref, inv_ref, filt_ref, *refs):
    piece_refs, out_refs = refs[:count][::-1], refs[count : 2 * count]
    whole_ref, own_ref, other_ref, joint_ref, result_ref = refs[2 * count :]
    rows = piece_refs[0].shape[0]
    size = whole_ref.shape[0] // blocks
    tile = joint_ref.shape[2]
    me = me_ref[0]
    for k in range(count):
        whole_ref[columns(me ^ k, rows), :] = piece_refs[k][...]
    for start in range(0, whole_ref.shape[1], tile):
        cols = slice(start, start + tile)
        spectra(blocks, fwd_ref, whole_ref, cols, own_ref)
        other_ref[0] = dot_nt(fwd_ref[:, size:], filt_ref[cols, :size])
        for q in range(1, blocks):
            other_ref[q] = dot_nt(fwd_ref[...], filt_ref[cols, (q - 1) * size : (q + 1) * size])
        correlate(blocks, own_ref, other_ref, joint_ref)
        for p in range(blocks):
            result_ref[p * size : (p + 1) * size, cols] = dot(inv_ref[...], joint_ref[p]).astype(BF16)
    for k in range(count):
        out_refs[k][...] = result_ref[columns(me ^ k, rows), :]


def pieces_long_grad_kernel(blocks, scale, count, me_ref, fwd_ref, inv_ref, grad_ref, *refs):
    piece_refs, out_ref = refs[:count][::-1], refs[count]
    own_ref, other_ref, joint_ref, whole_ref = refs[count + 1 :]
    rows = piece_refs[0].shape[0]
    size = whole_ref.shape[0] // blocks
    tile = joint_ref.shape[2]
    me = me_ref[0]
    for k in range(count):
        whole_ref[columns(me ^ k, rows), :] = piece_refs[k][...]
    for start in range(0, whole_ref.shape[1], tile):
        cols = slice(start, start + tile)
        spectra(blocks, fwd_ref, grad_ref, cols, own_ref)
        extended_spectra(blocks, fwd_ref, whole_ref, cols, other_ref)
        correlate(blocks, own_ref, other_ref, joint_ref)
        for p in range(blocks):
            lags = (dot(inv_ref[...], joint_ref[p]) * scale).T
            out_ref[cols, p * size : (p + 1) * size] = lags.astype(BF16)


def pieces_grad_b_kernel(beta, count, me_ref, near_ref, far_ref, long_ref, gate_ref, *refs):
    piece_refs, (grad_u_ref, grad_b_ref) = refs[:count][::-1], refs[count:]
    width = piece_refs[0].shape[1]
    me = me_ref[0]
    for k in range(count):
        owner = me ^ k
        cols = columns(owner, width)
        adjoint_ref = near_ref if k < count // 2 else far_ref
        adjoint = adjoint_ref[:, columns(owner & (adjoint_ref.shape[1] // width - 1), width)].astype(F32)
        grad_u = adjoint + piece_refs[k][...].astype(F32) * long_ref[:, cols].astype(F32)
        grad_u_ref[:, cols] = grad_u
        grad_b_ref[:, cols] = (beta * grad_u * gate_ref[:, cols].astype(F32)).astype(BF16)


def pieces_taps_kernel(me_ref, fwd_ref, inv_ref, signal_ref, grad_b_ref, keep_ref, send_ref):
    tokens = grad_b_ref.shape[0]
    width = keep_ref.shape[2]
    me = me_ref[0]
    for k in range(2 * keep_ref.shape[0]):
        cols = columns(me ^ k, width)
        grad = dot(fwd_ref[:, :tokens], grad_b_ref[:, cols])
        part = dot(inv_ref[...], times_conj(signal_ref[:, cols].astype(F32), grad)).astype(BF16)
        (send_ref if k % 2 else keep_ref)[k // 2] = part


def pair_kernel(keep_ref, came_ref, *out_refs):
    for m, out_ref in enumerate(out_refs):
        out_ref[...] = (keep_ref[m].astype(F32) + came_ref[m].astype(F32)).astype(BF16)


def pieces_total_kernel(scale, *refs):
    total = refs[0][...].astype(F32)
    for ref in refs[1:-1]:
        total += ref[...].astype(F32)
    refs[-1][...] = (total * scale).astype(BF16)


def pieces_input_grad_kernel(
    step, fwd_ref, inv_ref, grad_b_ref, later_ref, filt_ref, grad_u_ref, pre_ref, out_ref
):
    for start in range(0, grad_b_ref.shape[1], step):
        cols = slice(start, start + step)
        signal = dot(fwd_ref[...], stacked(grad_b_ref[:, cols], later_ref[:, cols]))
        act = dot(inv_ref[...], times_conj(signal, filt_ref[:, cols].astype(F32)))
        value = grad_u_ref[:, cols] + act * pre_ref[:, cols].astype(F32)
        out_ref[:, cols] = value.astype(BF16)


def local(body, outs, args, flops, scratch=(), vmem=24, name=None):
    moved = sum(a.size * a.dtype.itemsize for a in args)
    moved += sum(math.prod(shape) * jnp.dtype(kind).itemsize for shape, kind in outs)
    specs = [
        pl.BlockSpec(memory_space=pltpu.SMEM if a.dtype == jnp.int32 else pltpu.VMEM) for a in args
    ]
    result = pl.pallas_call(
        body,
        in_specs=specs,
        out_specs=[pl.BlockSpec(memory_space=pltpu.VMEM) for _ in outs],
        out_shape=[jax.ShapeDtypeStruct(shape, kind) for shape, kind in outs],
        scratch_shapes=list(scratch),
        compiler_params=pltpu.CompilerParams(vmem_limit_bytes=vmem * MIB),
        cost_estimate=pl.CostEstimate(flops=flops, bytes_accessed=moved, transcendentals=0),
        name=name,
    )(*args)
    return result[0] if len(result) == 1 else result


def swapped(array, k):
    count = lax.axis_size("ctx")
    return lax.ppermute(array, "ctx", [(i, i ^ k) for i in range(count)])


def after(value, *others):
    return lax.optimization_barrier((value, others))[0]


def exchanged(pieces, first=0):
    return [swapped(piece, first + k) if first + k else piece for k, piece in enumerate(pieces)]


def far_pair(pieces, first, *before):
    if before:
        pieces = [after(piece, other) for piece, other in zip(pieces, before)]
    return exchanged(pieces, first)


def by_permutes(
    incoming, layer_input, pre_gate, mid_gate, long_gate, out_gate, long_filter, mid_filter
):
    sections = lax.axis_size("section")
    devices = lax.axis_size("ctx")
    half = devices // 2
    beta = (2.0 * sections) ** (-0.5)
    tokens, channels = layer_input.shape[1:]
    taps = mid_filter.shape[1]
    seq_len = tokens * devices
    scale = float(seq_len) ** (-0.5)
    owned = channels // devices

    span = tokens + max(tokens, taps)
    fwd = jnp.asarray(forward_table(span, np.arange(span)))
    inv_conv = jnp.asarray(inverse_table(span, tokens + np.arange(tokens)))
    inv_corr = jnp.asarray(inverse_table(span, np.arange(tokens)))
    inv_taps = jnp.asarray(inverse_table(span, tokens - np.arange(taps)))
    size = max(math.gcd(seq_len, 256), seq_len // 8)
    blocks = seq_len // size
    period = 2 * size
    long_fwd = jnp.asarray(forward_table(period, np.arange(-size, size)))
    long_inv = jnp.asarray(inverse_table(period, np.arange(size)))
    tile = math.gcd(owned, 256)
    spectrum = pltpu.VMEM((blocks, period, tile), F32)
    joint = pltpu.VMEM((blocks, period, tile), BF16)
    staged = pltpu.VMEM((seq_len, owned), BF16)

    rows_shape = ((tokens, channels), BF16)
    half_shape = ((tokens, channels // 2), BF16)
    piece = ((tokens, owned), BF16)
    tap_piece = ((taps, owned), BF16)
    mid_flops = 8 * span * tokens * channels
    long_flops = 12 * period * seq_len * owned
    few = 4 * tokens * channels

    me = lax.axis_index("ctx").astype(jnp.int32)[None]
    inputs, gate_pre, gate_mid, gate_long, gate_out = (
        array[0] for array in (layer_input, pre_gate, mid_gate, long_gate, out_gate)
    )
    filter_taps = mid_filter[0]

    far = local(functools.partial(pick_kernel, (4,)), [half_shape], [me, incoming[0]], few, name="far")
    far = passed_along(far, "section", -1)
    mixed_in = local(mix_kernel, [rows_shape], [inputs, gate_pre], few, name="mix")
    earlier = shifted(mixed_in, "ctx", 1)
    sent = after(incoming[0], far)
    near = local(functools.partial(pick_kernel, (0,)), [half_shape], [me, sent], few, name="near")
    near = passed_along(near, "section", -1)
    far_z = local(
        functools.partial(pieces_z_kernel, beta, half), [piece] * half, [me, far, gate_out], few, name="farz"
    )
    signal, filt, *pieces_w = local(
        functools.partial(pieces_branch_kernel, beta),
        [((span, channels), BF16)] * 2 + [piece] * devices,
        [me, fwd, inv_conv, after(earlier, far_z), mixed_in, filter_taps, inputs, gate_mid, gate_long],
        mid_flops, name="branch",
    )
    z_6, z_7 = far_pair(far_z[2:], 6)
    z_4, z_5 = far_pair(far_z[:2], 4, z_6, z_7)
    near_w = exchanged(pieces_w[:half])
    near_z = local(
        functools.partial(pieces_z_kernel, beta, 0), [piece] * half,
        [me, after(near, near_w, z_7), gate_out], few, name="nearz",
    )
    near_z = exchanged(near_z)
    pieces_z = near_z + [z_4, z_5, z_6, z_7]
    w_6, w_7 = far_pair(pieces_w[6:], 6, (z_4, near_z), (z_5, near_z))
    *pieces_g, channel_z = local(
        functools.partial(pieces_grad_w_kernel, blocks, devices),
        [piece] * devices + [((seq_len, owned), BF16)],
        [me, long_fwd, long_inv, long_filter[0], *pieces_z[::-1]], long_flops,
        [spectrum, spectrum, joint, staged], name="gradw",
    )
    w_4, w_5 = far_pair(pieces_w[4:6], 4, (w_6, pieces_g[0]), (w_7, pieces_g[0]))
    pieces_w = near_w + [w_4, w_5, w_6, w_7]
    near_g = exchanged(pieces_g[:half])
    g_6, g_7 = far_pair(pieces_g[6:], 6, (w_4, near_g), (w_5, near_g))
    g_4, g_5 = far_pair(pieces_g[4:6], 4, g_6, g_7)
    pieces_g = [g_7, g_6, g_5, g_4] + near_g[::-1]
    long_grad = local(
        functools.partial(pieces_long_grad_kernel, blocks, scale, devices), [((owned, seq_len), BF16)],
        [me, long_fwd, long_inv, channel_z, *pieces_w[::-1]], long_flops,
        [spectrum, spectrum, joint, staged], name="longgrad",
    )
    pieces_g, long_grad = lax.optimization_barrier((pieces_g, long_grad))
    grad_u, grad_b = local(
        functools.partial(pieces_grad_b_kernel, beta, devices), [((tokens, channels), F32), rows_shape],
        [me, near, far, gate_long, gate_mid, *pieces_g], few, name="gradb",
    )
    later = shifted(grad_b, "ctx", -1)
    keep, send = local(
        pieces_taps_kernel, [((half, taps, owned), BF16)] * 2, [me, fwd, inv_taps, signal, grad_b],
        mid_flops, name="taps",
    )
    sums = local(pair_kernel, [tap_piece] * half, [keep, swapped(send, 1)], few, name="pair")
    sums = [swapped(sums[m], 2 * m) for m in (3, 2, 1)] + [sums[0]]
    later = after(later, sums[-1])
    wide = channels // 4
    rows_spec = pl.BlockSpec((tokens, wide), lambda i: (0, i))
    filt_spec = pl.BlockSpec((span, wide), lambda i: (0, i))
    input_grad = call(
        functools.partial(pieces_input_grad_kernel, 512), (4,),
        [whole_spec(fwd), whole_spec(inv_corr), rows_spec, rows_spec, filt_spec, rows_spec, rows_spec],
        [(*rows_shape, rows_spec)], [fwd, inv_corr, grad_b, later, filt, grad_u, gate_pre], mid_flops,
        name="inputgrad",
    )
    sums, input_grad = lax.optimization_barrier((sums, input_grad))
    mid_grad = local(functools.partial(pieces_total_kernel, scale), [tap_piece], sums, few, name="midgrad")
    return (input_grad[None], long_grad[None], mid_grad[None])


def per_device(*arrays):
    devices = lax.axis_size("ctx")
    owned = arrays[0].shape[2] // devices
    if owned % 128 == 0 and devices == 8:
        return by_permutes(*arrays)
    return by_all_to_all(*arrays)


def solution(mesh):
    placed = (
        P("section", "ctx", None),
        P("section", "ctx", None),
        P("section", "ctx", None),
        P("section", "ctx", None),
        P("section", "ctx", None),
        P("section", "ctx", None),
        P("section", "ctx", None),
        P("section", None, None),
    )
    return jax.shard_map(
        per_device,
        mesh=mesh,
        in_specs=placed,
        out_specs=(P("section", "ctx", None), P("section", "ctx", None), P("section", None, "ctx")),
        check_vma=False,
    )
```

```python
import functools
import math

import jax
import jax.numpy as jnp
import numpy as np
from jax import lax
from jax.experimental import pallas as pl
from jax.experimental.pallas import tpu as pltpu
from jax.sharding import PartitionSpec as P

BF16 = jnp.bfloat16
F32 = jnp.float32
MIB = 1024 * 1024


def passed_along(value, axis, steps):
    count = lax.axis_size(axis)
    pairs = [(source, (source + steps) % count) for source in range(count)]
    return lax.ppermute(value, axis, pairs)


def shifted(array, axis, by):
    devices = lax.axis_size(axis)
    pairs = [(i, i + by) for i in range(devices) if 0 <= i + by < devices]
    return lax.ppermute(array, axis, pairs)


def forward_table(period, positions):
    angle = np.pi * np.outer(2 * np.arange(period // 2) + 1, positions) / period
    return np.concatenate([np.cos(angle), -np.sin(angle)], 0).astype(BF16)


def inverse_table(period, positions):
    angle = np.pi * np.outer(positions, 2 * np.arange(period // 2) + 1) / period
    return (np.concatenate([np.cos(angle), -np.sin(angle)], 1) * (2.0 / period)).astype(BF16)


def dot(left, right):
    return jnp.dot(left, right, preferred_element_type=F32)


def dot_nt(left, right):
    return lax.dot_general(left, right, (((1,), (1,)), ((), ())), preferred_element_type=F32)


def stacked(*rows):
    return jnp.concatenate(rows, 0)


def times(left, right):
    half = left.shape[0] // 2
    l_re, l_im, r_re, r_im = left[:half], left[half:], right[:half], right[half:]
    return jnp.concatenate(
        [(l_re * r_re - l_im * r_im).astype(BF16), (l_re * r_im + l_im * r_re).astype(BF16)], 0
    )


def times_conj(left, right):
    half = left.shape[0] // 2
    l_re, l_im, r_re, r_im = left[:half], left[half:], right[:half], right[half:]
    return jnp.concatenate(
        [(l_re * r_re + l_im * r_im).astype(BF16), (l_im * r_re - l_re * r_im).astype(BF16)], 0
    )


def put_columns(out_ref, value, start):
    owned = out_ref.shape[2]
    width = value.shape[1]
    if owned >= width:
        out_ref[start // owned, :, start % owned : start % owned + width] = value
    else:
        for j in range(width // owned):
            out_ref[start // owned + j] = value[:, j * owned : (j + 1) * owned]


def get_columns(in_ref, start, width):
    owned = in_ref.shape[2]
    if owned >= width:
        return in_ref[start // owned, :, start % owned : start % owned + width]
    return jnp.concatenate([in_ref[start // owned + j] for j in range(width // owned)], 1)


def mix_kernel(inputs_ref, gate_ref, out_ref):
    out_ref[...] = (inputs_ref[...].astype(F32) * gate_ref[...].astype(F32)).astype(BF16)


def grad_z_kernel(beta, adjoint_ref, gate_ref, out_ref):
    value = beta * adjoint_ref[...].astype(F32) * gate_ref[...].astype(F32)
    put_columns(out_ref, value.astype(BF16), 0)


def branch_kernel(
    beta, step, fwd_ref, inv_ref, earlier_ref, mixed_ref, taps_ref, inputs_ref, mid_ref, long_ref, out_ref
):
    tokens = mixed_ref.shape[0]
    taps = taps_ref.shape[0]
    for start in range(0, mixed_ref.shape[1], step):
        cols = slice(start, start + step)
        signal = dot(fwd_ref[...], stacked(earlier_ref[:, cols], mixed_ref[:, cols]))
        filt = dot(fwd_ref[:, :taps], taps_ref[:, cols])
        branch = dot(inv_ref[...], times(signal, filt))
        resid = inputs_ref[:, cols].astype(F32) + beta * branch * mid_ref[:, cols].astype(F32)
        value = (resid * long_ref[:, cols].astype(F32)).astype(BF16)
        put_columns(out_ref, value, start)


def grad_b_kernel(beta, adjoint_ref, grad_w_ref, long_ref, mid_ref, out_ref):
    grad_w = get_columns(grad_w_ref, 0, out_ref.shape[1]).astype(F32)
    grad_u = adjoint_ref[...].astype(F32) + grad_w * long_ref[...].astype(F32)
    out_ref[...] = (beta * grad_u * mid_ref[...].astype(F32)).astype(BF16)


def taps_kernel(
    step, core_ref, fwd_ref, inv_ref, earlier_ref, mixed_ref, grad_b_ref, keep_ref, send_ref
):
    tokens = mixed_ref.shape[0]
    owned = keep_ref.shape[2]
    width = min(owned, step)

    def put(even_ref, odd_ref, owner, at, value):
        ref = even_ref if owner % 2 == 0 else odd_ref
        ref[owner // 2, :, at : at + width] = value

    for start in range(0, mixed_ref.shape[1], step):
        cols = slice(start, start + step)
        signal = dot(fwd_ref[...], stacked(earlier_ref[:, cols], mixed_ref[:, cols]))
        grad = dot(fwd_ref[:, :tokens], grad_b_ref[:, cols])
        part = dot(inv_ref[...], times_conj(signal, grad)).astype(BF16)
        for j in range(0, step, width):
            owner, at = divmod(start + j, owned)
            value = part[:, j : j + width]
            pl.when(core_ref[0] == 0)(functools.partial(put, keep_ref, send_ref, owner, at, value))
            pl.when(core_ref[0] == 1)(functools.partial(put, send_ref, keep_ref, owner, at, value))


def input_grad_kernel(
    step, fwd_ref, inv_ref, grad_b_ref, later_ref, taps_ref, adjoint_ref, grad_w_ref, long_ref, pre_ref,
    out_ref,
):
    tokens = grad_b_ref.shape[0]
    taps = taps_ref.shape[0]
    for start in range(0, grad_b_ref.shape[1], step):
        cols = slice(start, start + step)
        grad_w = get_columns(grad_w_ref, start, step).astype(F32)
        grad_u = adjoint_ref[:, cols].astype(F32) + grad_w * long_ref[:, cols].astype(F32)
        signal = dot(fwd_ref[...], stacked(grad_b_ref[:, cols], later_ref[:, cols]))
        filt = dot(fwd_ref[:, :taps], taps_ref[:, cols])
        act = dot(inv_ref[...], times_conj(signal, filt))
        out_ref[:, cols] = (grad_u + act * pre_ref[:, cols].astype(F32)).astype(BF16)


def correlate(blocks, own_ref, other, joint_ref):
    period, width = joint_ref.shape[1:]
    half = period // 2
    rows, lanes = 16, math.gcd(width, 128) if width % 128 == 0 else width

    def chunk(i, _):
        at = pl.multiple_of(i * rows, rows)
        re, im = pl.ds(at, rows), pl.ds(pl.multiple_of(half + at, rows), rows)
        for start in range(0, width, lanes):
            cols = slice(start, start + lanes)
            own = [(own_ref[q, re, cols], own_ref[q, im, cols]) for q in range(blocks)]
            oth = [(other[d, re, cols], other[d, im, cols]) for d in range(blocks)]
            for p in range(blocks):
                sum_re = sum_im = None
                for q in range(p, blocks):
                    a_re, a_im = own[q]
                    b_re, b_im = oth[q - p]
                    new_re = a_re * b_re + a_im * b_im
                    new_im = a_im * b_re - a_re * b_im
                    sum_re = new_re if sum_re is None else sum_re + new_re
                    sum_im = new_im if sum_im is None else sum_im + new_im
                joint_ref[p, re, cols] = sum_re.astype(BF16)
                joint_ref[p, im, cols] = sum_im.astype(BF16)
        return 0

    lax.fori_loop(0, half // rows, chunk, 0)


def grad_w_kernel(
    blocks, fwd_ref, inv_ref, grad_ref, filt_ref, out_ref, own_ref, other_ref, joint_ref
):
    size = grad_ref.shape[0] // blocks
    for q in range(blocks):
        own_ref[q] = dot(fwd_ref[:, size:], grad_ref[q * size : (q + 1) * size])
        other = dot_nt(fwd_ref[:, size:], filt_ref[:, q * size : (q + 1) * size])
        if q:
            other += dot_nt(fwd_ref[:, :size], filt_ref[:, (q - 1) * size : q * size])
        other_ref[q] = other
    correlate(blocks, own_ref, other_ref, joint_ref)
    for p in range(blocks):
        out_ref[p * size : (p + 1) * size] = dot(inv_ref[...], joint_ref[p]).astype(BF16)


def long_grad_kernel(
    blocks, scale, fwd_ref, inv_ref, grad_ref, long_ref, out_ref, own_ref, other_ref, joint_ref
):
    size = grad_ref.shape[0] // blocks
    for q in range(blocks):
        own_ref[q] = dot(fwd_ref[:, size:], grad_ref[q * size : (q + 1) * size])
        other = dot(fwd_ref[:, size:], long_ref[q * size : (q + 1) * size])
        if q:
            other += dot(fwd_ref[:, :size], long_ref[(q - 1) * size : q * size])
        other_ref[q] = other
    correlate(blocks, own_ref, other_ref, joint_ref)
    for p in range(blocks):
        lags = (dot(inv_ref[...], joint_ref[p]) * scale).T
        out_ref[:, p * size : (p + 1) * size] = lags.astype(BF16)


def total_kernel(scale, parts_ref, out_ref):
    total = parts_ref[0].astype(F32)
    for i in range(1, parts_ref.shape[0]):
        total += parts_ref[i].astype(F32)
    out_ref[...] = (total * scale).astype(BF16)


def call(body, grid, ins, outs, args, flops, scratch=(), vmem=16, name=None):
    moved = sum(a.size * a.dtype.itemsize for a in args)
    moved += sum(math.prod(shape) * jnp.dtype(kind).itemsize for shape, kind, _ in outs)
    result = pl.pallas_call(
        body,
        grid=grid,
        in_specs=ins,
        out_specs=[spec for _, _, spec in outs],
        out_shape=[jax.ShapeDtypeStruct(shape, kind) for shape, kind, _ in outs],
        scratch_shapes=list(scratch),
        compiler_params=pltpu.CompilerParams(vmem_limit_bytes=vmem * MIB),
        cost_estimate=pl.CostEstimate(flops=flops, bytes_accessed=moved, transcendentals=0),
        name=name,
    )(*args)
    return result[0] if len(result) == 1 else result


def whole_spec(array):
    return pl.BlockSpec(array.shape, lambda i: (0,) * array.ndim)


def by_all_to_all(
    incoming, layer_input, pre_gate, mid_gate, long_gate, out_gate, long_filter, mid_filter
):
    sections = lax.axis_size("section")
    devices = lax.axis_size("ctx")
    beta = (2.0 * sections) ** (-0.5)
    tokens, channels = layer_input.shape[1:]
    taps = mid_filter.shape[1]
    seq_len = tokens * devices
    scale = float(seq_len) ** (-0.5)
    owned = channels // devices

    span = tokens + max(tokens, taps)
    fwd = jnp.asarray(forward_table(span, np.arange(span)))
    inv_conv = jnp.asarray(inverse_table(span, tokens + np.arange(tokens)))
    inv_corr = jnp.asarray(inverse_table(span, np.arange(tokens)))
    inv_taps = jnp.asarray(inverse_table(span, tokens - np.arange(taps)))
    size = max(math.gcd(seq_len, 256), seq_len // 8)
    blocks = seq_len // size
    period = 2 * size
    long_fwd = jnp.asarray(forward_table(period, np.arange(-size, size)))
    long_inv = jnp.asarray(inverse_table(period, np.arange(size)))

    wide = max(1024, 2 * owned)
    step = min(256, wide)
    grid = (channels // wide,)
    rows_spec = pl.BlockSpec((tokens, wide), lambda i: (0, i))
    taps_spec = pl.BlockSpec((taps, wide), lambda i: (0, i))
    major_spec = pl.BlockSpec((wide // owned, tokens, owned), lambda i: (i, 0, 0))
    half_major = pl.BlockSpec((wide // owned // 2, taps, owned), lambda i: (i, 0, 0))
    half_shape = (devices // 2, taps, owned)
    rows_shape = (tokens, channels)
    major_shape = (devices, tokens, owned)
    mid_flops = 8 * span * tokens * channels

    tile = math.gcd(owned, 256)
    long_grid = (owned // tile,)
    long_spec = pl.BlockSpec((seq_len, tile), lambda i: (0, i))
    lag_spec = pl.BlockSpec((tile, seq_len), lambda i: (i, 0))
    spectrum = pltpu.VMEM((blocks, period, tile), F32)
    joint = pltpu.VMEM((blocks, period, tile), BF16)
    lanes = -(-tile // 128) * 128
    long_vmem = 2 * (long_fwd.size + long_inv.size) * 2 + 20 * blocks * period * lanes
    long_vmem = -(-long_vmem // MIB) + 6
    long_flops = 4 * period * seq_len * owned

    inputs, gate_pre, gate_mid, gate_long, gate_out = (
        array[0] for array in (layer_input, pre_gate, mid_gate, long_gate, out_gate)
    )
    filter_taps = mid_filter[0]

    adjoint = passed_along(incoming[0], "section", -1)
    mixed_in = call(
        mix_kernel, grid, [rows_spec] * 2, [(rows_shape, BF16, rows_spec)], [inputs, gate_pre],
        2 * tokens * channels, name="mix",
    )
    earlier = shifted(mixed_in, "ctx", 1)
    adjoint, earlier = lax.optimization_barrier((adjoint, earlier))
    grad_z = call(
        functools.partial(grad_z_kernel, beta), grid, [rows_spec] * 2,
        [(major_shape, BF16, major_spec)], [adjoint, gate_out], 2 * tokens * channels, name="gradz",
    )
    grad_z, earlier = lax.optimization_barrier((grad_z, earlier))
    channel_z = lax.all_to_all(grad_z, "ctx", split_axis=0, concat_axis=0, tiled=True)
    long_in = call(
        functools.partial(branch_kernel, beta, step), grid,
        [whole_spec(fwd), whole_spec(inv_conv)] + [rows_spec] * 2 + [taps_spec] + [rows_spec] * 3,
        [(major_shape, BF16, major_spec)],
        [fwd, inv_conv, earlier, mixed_in, filter_taps, inputs, gate_mid, gate_long], mid_flops,
        name="branch",
    )
    channel_z, long_in = lax.optimization_barrier((channel_z, long_in))
    channel_w = lax.all_to_all(long_in, "ctx", split_axis=0, concat_axis=0, tiled=True)
    channel_z = channel_z.reshape(seq_len, owned)
    grad_w = call(
        functools.partial(grad_w_kernel, blocks), long_grid,
        [whole_spec(long_fwd), whole_spec(long_inv), long_spec, lag_spec],
        [((seq_len, owned), BF16, long_spec)], [long_fwd, long_inv, channel_z, long_filter[0]],
        2 * long_flops, [spectrum, spectrum, joint], long_vmem, "gradw",
    )
    grad_w, channel_w = lax.optimization_barrier((grad_w, channel_w))
    returned = lax.all_to_all(
        grad_w.reshape(major_shape), "ctx", split_axis=0, concat_axis=0, tiled=True
    )
    channel_w = channel_w.reshape(seq_len, owned)
    long_grad = call(
        functools.partial(long_grad_kernel, blocks, scale), long_grid,
        [whole_spec(long_fwd), whole_spec(long_inv), long_spec, long_spec],
        [((owned, seq_len), BF16, lag_spec)], [long_fwd, long_inv, channel_z, channel_w],
        2 * long_flops, [spectrum, spectrum, joint], long_vmem, "longgrad",
    )
    returned, long_grad = lax.optimization_barrier((returned, long_grad))
    grad_b = call(
        functools.partial(grad_b_kernel, beta), grid,
        [rows_spec, major_spec] + [rows_spec] * 2, [(rows_shape, BF16, rows_spec)],
        [adjoint, returned, gate_long, gate_mid], 4 * tokens * channels, name="gradb",
    )
    later = shifted(grad_b, "ctx", -1)
    core = (lax.axis_index("ctx") % 2).astype(jnp.int32)[None]
    keep, send = call(
        functools.partial(taps_kernel, step), grid,
        [pl.BlockSpec(memory_space=pltpu.SMEM), whole_spec(fwd), whole_spec(inv_taps)]
        + [rows_spec] * 3,
        [(half_shape, BF16, half_major)] * 2,
        [core, fwd, inv_taps, earlier, mixed_in, grad_b], mid_flops, name="taps",
    )
    partner = lax.ppermute(send, "ctx", [(i, i ^ 1) for i in range(devices)])
    chip_parts = (keep.astype(F32) + partner.astype(F32)).astype(BF16)
    gathered = lax.all_to_all(
        chip_parts, "ctx", split_axis=0, concat_axis=0, tiled=True,
        axis_index_groups=[list(range(c, devices, 2)) for c in range(2)],
    )
    later, _ = lax.optimization_barrier((later, chip_parts))
    input_grad = call(
        functools.partial(input_grad_kernel, step), grid,
        [whole_spec(fwd), whole_spec(inv_corr)] + [rows_spec] * 2 + [taps_spec, rows_spec, major_spec]
        + [rows_spec] * 2,
        [(rows_shape, BF16, rows_spec)],
        [fwd, inv_corr, grad_b, later, filter_taps, adjoint, returned, gate_long, gate_pre],
        mid_flops, name="inputgrad",
    )
    mid_grad = call(
        functools.partial(total_kernel, scale), (1,), [whole_spec(gathered)],
        [((taps, owned), BF16, pl.BlockSpec((taps, owned), lambda i: (0, 0)))], [gathered],
        devices * taps * owned, name="midgrad",
    )
    return (input_grad[None], long_grad[None], mid_grad[None])


def columns(index, width):
    return pl.ds(pl.multiple_of(index * width, width), width)


def pick_kernel(firsts, me_ref, in_ref, *out_refs):
    for first, out_ref in zip(firsts, out_refs):
        width = out_ref.shape[1]
        owned = in_ref.shape[1] // 8
        out_ref[...] = in_ref[:, columns((me_ref[0] ^ first) // (width // owned), width)]


def pieces_z_kernel(beta, first, me_ref, adjoint_ref, gate_ref, *out_refs):
    count = len(out_refs)
    width = out_refs[0].shape[1]
    me = me_ref[0]
    for k in range(count):
        owner = me ^ (first + k)
        part = adjoint_ref[:, columns(owner & (count - 1), width)].astype(F32)
        gate = gate_ref[:, columns(owner, width)].astype(F32)
        out_refs[k][...] = (beta * part * gate).astype(BF16)


def pieces_branch_kernel(
    beta, me_ref, fwd_ref, inv_ref, earlier_ref, mixed_ref, taps_ref, inputs_ref, mid_ref, long_ref,
    signal_ref, filt_ref, *out_refs,
):
    taps = taps_ref.shape[0]
    width = out_refs[0].shape[1]
    me = me_ref[0]
    count = len(out_refs)
    for k in list(range(count // 2, count)) + list(range(count // 2)):
        cols = columns(me ^ k, width)
        signal = dot(fwd_ref[...], stacked(earlier_ref[:, cols], mixed_ref[:, cols]))
        filt = dot(fwd_ref[:, :taps], taps_ref[:, cols])
        signal_ref[:, cols] = signal.astype(BF16)
        filt_ref[:, cols] = filt.astype(BF16)
        branch = dot(inv_ref[...], times(signal, filt))
        resid = inputs_ref[:, cols].astype(F32) + beta * branch * mid_ref[:, cols].astype(F32)
        out_refs[k][...] = (resid * long_ref[:, cols].astype(F32)).astype(BF16)


def spectra(blocks, fwd_ref, array_ref, cols, out_ref):
    size = array_ref.shape[0] // blocks
    for q in range(blocks):
        out_ref[q] = dot(fwd_ref[:, size:], array_ref[q * size : (q + 1) * size, cols])


def extended_spectra(blocks, fwd_ref, array_ref, cols, out_ref):
    size = array_ref.shape[0] // blocks
    out_ref[0] = dot(fwd_ref[:, size:], array_ref[:size, cols])
    for q in range(1, blocks):
        out_ref[q] = dot(fwd_ref[...], array_ref[(q - 1) * size : (q + 1) * size, cols])


def pieces_grad_w_kernel(blocks, count, me_ref, fwd_ref, inv_ref, filt_ref, *refs):
    piece_refs, out_refs = refs[:count][::-1], refs[count : 2 * count]
    whole_ref, own_ref, other_ref, joint_ref, result_ref = refs[2 * count :]
    rows = piece_refs[0].shape[0]
    size = whole_ref.shape[0] // blocks
    tile = joint_ref.shape[2]
    me = me_ref[0]
    for k in range(count):
        whole_ref[columns(me ^ k, rows), :] = piece_refs[k][...]
    for start in range(0, whole_ref.shape[1], tile):
        cols = slice(start, start + tile)
        spectra(blocks, fwd_ref, whole_ref, cols, own_ref)
        other_ref[0] = dot_nt(fwd_ref[:, size:], filt_ref[cols, :size])
        for q in range(1, blocks):
            other_ref[q] = dot_nt(fwd_ref[...], filt_ref[cols, (q - 1) * size : (q + 1) * size])
        correlate(blocks, own_ref, other_ref, joint_ref)
        for p in range(blocks):
            result_ref[p * size : (p + 1) * size, cols] = dot(inv_ref[...], joint_ref[p]).astype(BF16)
    for k in range(count):
        out_refs[k][...] = result_ref[columns(me ^ k, rows), :]


def pieces_long_grad_kernel(blocks, scale, count, me_ref, fwd_ref, inv_ref, grad_ref, *refs):
    piece_refs, out_ref = refs[:count][::-1], refs[count]
    own_ref, other_ref, joint_ref, whole_ref = refs[count + 1 :]
    rows = piece_refs[0].shape[0]
    size = whole_ref.shape[0] // blocks
    tile = joint_ref.shape[2]
    me = me_ref[0]
    for k in range(count):
        whole_ref[columns(me ^ k, rows), :] = piece_refs[k][...]
    for start in range(0, whole_ref.shape[1], tile):
        cols = slice(start, start + tile)
        spectra(blocks, fwd_ref, grad_ref, cols, own_ref)
        extended_spectra(blocks, fwd_ref, whole_ref, cols, other_ref)
        correlate(blocks, own_ref, other_ref, joint_ref)
        for p in range(blocks):
            lags = (dot(inv_ref[...], joint_ref[p]) * scale).T
            out_ref[cols, p * size : (p + 1) * size] = lags.astype(BF16)


def pieces_grad_b_kernel(beta, count, me_ref, near_ref, far_ref, long_ref, gate_ref, *refs):
    piece_refs, (grad_u_ref, grad_b_ref) = refs[:count][::-1], refs[count:]
    width = piece_refs[0].shape[1]
    me = me_ref[0]
    for k in range(count):
        owner = me ^ k
        cols = columns(owner, width)
        adjoint_ref = near_ref if k < count // 2 else far_ref
        adjoint = adjoint_ref[:, columns(owner & (adjoint_ref.shape[1] // width - 1), width)].astype(F32)
        grad_u = adjoint + piece_refs[k][...].astype(F32) * long_ref[:, cols].astype(F32)
        grad_u_ref[:, cols] = grad_u
        grad_b_ref[:, cols] = (beta * grad_u * gate_ref[:, cols].astype(F32)).astype(BF16)


def pieces_taps_kernel(me_ref, fwd_ref, inv_ref, signal_ref, grad_b_ref, keep_ref, send_ref):
    tokens = grad_b_ref.shape[0]
    width = keep_ref.shape[2]
    me = me_ref[0]
    for k in range(2 * keep_ref.shape[0]):
        cols = columns(me ^ k, width)
        grad = dot(fwd_ref[:, :tokens], grad_b_ref[:, cols])
        part = dot(inv_ref[...], times_conj(signal_ref[:, cols].astype(F32), grad)).astype(BF16)
        (send_ref if k % 2 else keep_ref)[k // 2] = part


def pair_kernel(keep_ref, came_ref, *out_refs):
    for m, out_ref in enumerate(out_refs):
        out_ref[...] = (keep_ref[m].astype(F32) + came_ref[m].astype(F32)).astype(BF16)


def pieces_total_kernel(scale, *refs):
    total = refs[0][...].astype(F32)
    for ref in refs[1:-1]:
        total += ref[...].astype(F32)
    refs[-1][...] = (total * scale).astype(BF16)


def pieces_input_grad_kernel(
    step, fwd_ref, inv_ref, grad_b_ref, later_ref, filt_ref, grad_u_ref, pre_ref, out_ref
):
    for start in range(0, grad_b_ref.shape[1], step):
        cols = slice(start, start + step)
        signal = dot(fwd_ref[...], stacked(grad_b_ref[:, cols], later_ref[:, cols]))
        act = dot(inv_ref[...], times_conj(signal, filt_ref[:, cols].astype(F32)))
        value = grad_u_ref[:, cols] + act * pre_ref[:, cols].astype(F32)
        out_ref[:, cols] = value.astype(BF16)


def local(body, outs, args, flops, scratch=(), vmem=24, name=None):
    moved = sum(a.size * a.dtype.itemsize for a in args)
    moved += sum(math.prod(shape) * jnp.dtype(kind).itemsize for shape, kind in outs)
    specs = [
        pl.BlockSpec(memory_space=pltpu.SMEM if a.dtype == jnp.int32 else pltpu.VMEM) for a in args
    ]
    result = pl.pallas_call(
        body,
        in_specs=specs,
        out_specs=[pl.BlockSpec(memory_space=pltpu.VMEM) for _ in outs],
        out_shape=[jax.ShapeDtypeStruct(shape, kind) for shape, kind in outs],
        scratch_shapes=list(scratch),
        compiler_params=pltpu.CompilerParams(vmem_limit_bytes=vmem * MIB),
        cost_estimate=pl.CostEstimate(flops=flops, bytes_accessed=moved, transcendentals=0),
        name=name,
    )(*args)
    return result[0] if len(result) == 1 else result


def swapped(array, k):
    count = lax.axis_size("ctx")
    return lax.ppermute(array, "ctx", [(i, i ^ k) for i in range(count)])


def after(value, *others):
    return lax.optimization_barrier((value, others))[0]


def exchanged(pieces, first=0):
    return [swapped(piece, first + k) if first + k else piece for k, piece in enumerate(pieces)]


def far_pair(pieces, first, *before):
    if before:
        pieces = [after(piece, other) for piece, other in zip(pieces, before)]
    return exchanged(pieces, first)


def by_permutes(
    incoming, layer_input, pre_gate, mid_gate, long_gate, out_gate, long_filter, mid_filter
):
    sections = lax.axis_size("section")
    devices = lax.axis_size("ctx")
    half = devices // 2
    beta = (2.0 * sections) ** (-0.5)
    tokens, channels = layer_input.shape[1:]
    taps = mid_filter.shape[1]
    seq_len = tokens * devices
    scale = float(seq_len) ** (-0.5)
    owned = channels // devices

    span = tokens + max(tokens, taps)
    fwd = jnp.asarray(forward_table(span, np.arange(span)))
    inv_conv = jnp.asarray(inverse_table(span, tokens + np.arange(tokens)))
    inv_corr = jnp.asarray(inverse_table(span, np.arange(tokens)))
    inv_taps = jnp.asarray(inverse_table(span, tokens - np.arange(taps)))
    size = max(math.gcd(seq_len, 256), seq_len // 8)
    blocks = seq_len // size
    period = 2 * size
    long_fwd = jnp.asarray(forward_table(period, np.arange(-size, size)))
    long_inv = jnp.asarray(inverse_table(period, np.arange(size)))
    tile = math.gcd(owned, 256)
    spectrum = pltpu.VMEM((blocks, period, tile), F32)
    joint = pltpu.VMEM((blocks, period, tile), BF16)
    staged = pltpu.VMEM((seq_len, owned), BF16)

    rows_shape = ((tokens, channels), BF16)
    half_shape = ((tokens, channels // 2), BF16)
    piece = ((tokens, owned), BF16)
    tap_piece = ((taps, owned), BF16)
    mid_flops = 8 * span * tokens * channels
    long_flops = 12 * period * seq_len * owned
    few = 4 * tokens * channels

    me = lax.axis_index("ctx").astype(jnp.int32)[None]
    inputs, gate_pre, gate_mid, gate_long, gate_out = (
        array[0] for array in (layer_input, pre_gate, mid_gate, long_gate, out_gate)
    )
    filter_taps = mid_filter[0]

    far = local(functools.partial(pick_kernel, (4,)), [half_shape], [me, incoming[0]], few, name="far")
    far = passed_along(far, "section", -1)
    mixed_in = local(mix_kernel, [rows_shape], [inputs, gate_pre], few, name="mix")
    earlier = shifted(mixed_in, "ctx", 1)
    sent = after(incoming[0], far)
    near = local(functools.partial(pick_kernel, (0,)), [half_shape], [me, sent], few, name="near")
    near = passed_along(near, "section", -1)
    far_z = local(
        functools.partial(pieces_z_kernel, beta, half), [piece] * half, [me, far, gate_out], few, name="farz"
    )
    z_6, z_7 = far_pair(far_z[2:], 6)
    z_5 = swapped(far_z[1], 5)
    z_4 = swapped(after(far_z[0], z_6), 4)
    near = after(near, z_5, z_6, z_7)
    near_z = local(
        functools.partial(pieces_z_kernel, beta, 0), [piece] * half, [me, near, gate_out], few, name="nearz"
    )
    signal, filt, *pieces_w = local(
        functools.partial(pieces_branch_kernel, beta),
        [((span, channels), BF16)] * 2 + [piece] * devices,
        [me, fwd, inv_conv, after(earlier, near_z), mixed_in, filter_taps, inputs, gate_mid, gate_long],
        mid_flops, name="branch",
    )
    near_z = exchanged(near_z)
    pieces_z = near_z + [z_4, z_5, z_6, z_7]
    w_6, w_7 = far_pair(pieces_w[6:], 6, (z_4, near_z), (z_5, near_z))
    near_w = exchanged(pieces_w[:half])
    *pieces_g, channel_z = local(
        functools.partial(pieces_grad_w_kernel, blocks, devices),
        [piece] * devices + [((seq_len, owned), BF16)],
        [me, long_fwd, long_inv, long_filter[0], *pieces_z[::-1]], long_flops,
        [spectrum, spectrum, joint, staged], name="gradw",
    )
    w_4, w_5 = far_pair(pieces_w[4:6], 4, (w_6, near_w, pieces_g[0]), (w_7, near_w, pieces_g[0]))
    pieces_w = near_w + [w_4, w_5, w_6, w_7]
    near_g = exchanged(pieces_g[:half])
    g_6, g_7 = far_pair(pieces_g[6:], 6, (w_4, near_g), (w_5, near_g))
    g_4, g_5 = far_pair(pieces_g[4:6], 4, g_6, g_7)
    pieces_g = [g_7, g_6, g_5, g_4] + near_g[::-1]
    long_grad = local(
        functools.partial(pieces_long_grad_kernel, blocks, scale, devices), [((owned, seq_len), BF16)],
        [me, long_fwd, long_inv, channel_z, *pieces_w[::-1]], long_flops,
        [spectrum, spectrum, joint, staged], name="longgrad",
    )
    pieces_g, long_grad = lax.optimization_barrier((pieces_g, long_grad))
    grad_u, grad_b = local(
        functools.partial(pieces_grad_b_kernel, beta, devices), [((tokens, channels), F32), rows_shape],
        [me, near, far, gate_long, gate_mid, *pieces_g], few, name="gradb",
    )
    later = shifted(grad_b, "ctx", -1)
    keep, send = local(
        pieces_taps_kernel, [((half, taps, owned), BF16)] * 2, [me, fwd, inv_taps, signal, grad_b],
        mid_flops, name="taps",
    )
    sums = local(pair_kernel, [tap_piece] * half, [keep, swapped(send, 1)], few, name="pair")
    sums = [swapped(sums[m], 2 * m) for m in (3, 2, 1)] + [sums[0]]
    later = after(later, sums[-1])
    input_grad = local(
        functools.partial(pieces_input_grad_kernel, 512), [rows_shape],
        [fwd, inv_corr, grad_b, later, filt, grad_u, gate_pre], mid_flops, name="inputgrad",
    )
    sums, input_grad = lax.optimization_barrier((sums, input_grad))
    mid_grad = local(functools.partial(pieces_total_kernel, scale), [tap_piece], sums, few, name="midgrad")
    return (input_grad[None], long_grad[None], mid_grad[None])


def per_device(*arrays):
    devices = lax.axis_size("ctx")
    owned = arrays[0].shape[2] // devices
    if owned % 128 == 0 and devices == 8:
        return by_permutes(*arrays)
    return by_all_to_all(*arrays)


def solution(mesh):
    placed = (
        P("section", "ctx", None),
        P("section", "ctx", None),
        P("section", "ctx", None),
        P("section", "ctx", None),
        P("section", "ctx", None),
        P("section", "ctx", None),
        P("section", "ctx", None),
        P("section", None, None),
    )
    return jax.shard_map(
        per_device,
        mesh=mesh,
        in_specs=placed,
        out_specs=(P("section", "ctx", None), P("section", "ctx", None), P("section", None, "ctx")),
        check_vma=False,
    )
```

```python
import functools
import math

import jax
import jax.numpy as jnp
import numpy as np
from jax import lax
from jax.experimental import pallas as pl
from jax.experimental.pallas import tpu as pltpu
from jax.sharding import PartitionSpec as P

BF16 = jnp.bfloat16
F32 = jnp.float32
MIB = 1024 * 1024


def passed_along(value, axis, steps):
    count = lax.axis_size(axis)
    pairs = [(source, (source + steps) % count) for source in range(count)]
    return lax.ppermute(value, axis, pairs)


def shifted(array, axis, by):
    devices = lax.axis_size(axis)
    pairs = [(i, i + by) for i in range(devices) if 0 <= i + by < devices]
    return lax.ppermute(array, axis, pairs)


def forward_table(period, positions):
    angle = np.pi * np.outer(2 * np.arange(period // 2) + 1, positions) / period
    return np.concatenate([np.cos(angle), -np.sin(angle)], 0).astype(BF16)


def inverse_table(period, positions):
    angle = np.pi * np.outer(positions, 2 * np.arange(period // 2) + 1) / period
    return (np.concatenate([np.cos(angle), -np.sin(angle)], 1) * (2.0 / period)).astype(BF16)


def dot(left, right):
    return jnp.dot(left, right, preferred_element_type=F32)


def dot_nt(left, right):
    return lax.dot_general(left, right, (((1,), (1,)), ((), ())), preferred_element_type=F32)


def stacked(*rows):
    return jnp.concatenate(rows, 0)


def times(left, right):
    half = left.shape[0] // 2
    l_re, l_im, r_re, r_im = left[:half], left[half:], right[:half], right[half:]
    return jnp.concatenate(
        [(l_re * r_re - l_im * r_im).astype(BF16), (l_re * r_im + l_im * r_re).astype(BF16)], 0
    )


def times_conj(left, right):
    half = left.shape[0] // 2
    l_re, l_im, r_re, r_im = left[:half], left[half:], right[:half], right[half:]
    return jnp.concatenate(
        [(l_re * r_re + l_im * r_im).astype(BF16), (l_im * r_re - l_re * r_im).astype(BF16)], 0
    )


def put_columns(out_ref, value, start):
    owned = out_ref.shape[2]
    width = value.shape[1]
    if owned >= width:
        out_ref[start // owned, :, start % owned : start % owned + width] = value
    else:
        for j in range(width // owned):
            out_ref[start // owned + j] = value[:, j * owned : (j + 1) * owned]


def get_columns(in_ref, start, width):
    owned = in_ref.shape[2]
    if owned >= width:
        return in_ref[start // owned, :, start % owned : start % owned + width]
    return jnp.concatenate([in_ref[start // owned + j] for j in range(width // owned)], 1)


def mix_kernel(inputs_ref, gate_ref, out_ref):
    out_ref[...] = (inputs_ref[...].astype(F32) * gate_ref[...].astype(F32)).astype(BF16)


def grad_z_kernel(beta, adjoint_ref, gate_ref, out_ref):
    value = beta * adjoint_ref[...].astype(F32) * gate_ref[...].astype(F32)
    put_columns(out_ref, value.astype(BF16), 0)


def branch_kernel(
    beta, step, fwd_ref, inv_ref, earlier_ref, mixed_ref, taps_ref, inputs_ref, mid_ref, long_ref, out_ref
):
    tokens = mixed_ref.shape[0]
    taps = taps_ref.shape[0]
    for start in range(0, mixed_ref.shape[1], step):
        cols = slice(start, start + step)
        signal = dot(fwd_ref[...], stacked(earlier_ref[:, cols], mixed_ref[:, cols]))
        filt = dot(fwd_ref[:, :taps], taps_ref[:, cols])
        branch = dot(inv_ref[...], times(signal, filt))
        resid = inputs_ref[:, cols].astype(F32) + beta * branch * mid_ref[:, cols].astype(F32)
        value = (resid * long_ref[:, cols].astype(F32)).astype(BF16)
        put_columns(out_ref, value, start)


def grad_b_kernel(beta, adjoint_ref, grad_w_ref, long_ref, mid_ref, out_ref):
    grad_w = get_columns(grad_w_ref, 0, out_ref.shape[1]).astype(F32)
    grad_u = adjoint_ref[...].astype(F32) + grad_w * long_ref[...].astype(F32)
    out_ref[...] = (beta * grad_u * mid_ref[...].astype(F32)).astype(BF16)


def taps_kernel(
    step, core_ref, fwd_ref, inv_ref, earlier_ref, mixed_ref, grad_b_ref, keep_ref, send_ref
):
    tokens = mixed_ref.shape[0]
    owned = keep_ref.shape[2]
    width = min(owned, step)

    def put(even_ref, odd_ref, owner, at, value):
        ref = even_ref if owner % 2 == 0 else odd_ref
        ref[owner // 2, :, at : at + width] = value

    for start in range(0, mixed_ref.shape[1], step):
        cols = slice(start, start + step)
        signal = dot(fwd_ref[...], stacked(earlier_ref[:, cols], mixed_ref[:, cols]))
        grad = dot(fwd_ref[:, :tokens], grad_b_ref[:, cols])
        part = dot(inv_ref[...], times_conj(signal, grad)).astype(BF16)
        for j in range(0, step, width):
            owner, at = divmod(start + j, owned)
            value = part[:, j : j + width]
            pl.when(core_ref[0] == 0)(functools.partial(put, keep_ref, send_ref, owner, at, value))
            pl.when(core_ref[0] == 1)(functools.partial(put, send_ref, keep_ref, owner, at, value))


def input_grad_kernel(
    step, fwd_ref, inv_ref, grad_b_ref, later_ref, taps_ref, adjoint_ref, grad_w_ref, long_ref, pre_ref,
    out_ref,
):
    tokens = grad_b_ref.shape[0]
    taps = taps_ref.shape[0]
    for start in range(0, grad_b_ref.shape[1], step):
        cols = slice(start, start + step)
        grad_w = get_columns(grad_w_ref, start, step).astype(F32)
        grad_u = adjoint_ref[:, cols].astype(F32) + grad_w * long_ref[:, cols].astype(F32)
        signal = dot(fwd_ref[...], stacked(grad_b_ref[:, cols], later_ref[:, cols]))
        filt = dot(fwd_ref[:, :taps], taps_ref[:, cols])
        act = dot(inv_ref[...], times_conj(signal, filt))
        out_ref[:, cols] = (grad_u + act * pre_ref[:, cols].astype(F32)).astype(BF16)


def correlate(blocks, own_ref, other, joint_ref):
    period, width = joint_ref.shape[1:]
    half = period // 2
    rows, lanes = 16, math.gcd(width, 128) if width % 128 == 0 else width

    def chunk(i, _):
        at = pl.multiple_of(i * rows, rows)
        re, im = pl.ds(at, rows), pl.ds(pl.multiple_of(half + at, rows), rows)
        for start in range(0, width, lanes):
            cols = slice(start, start + lanes)
            own = [(own_ref[q, re, cols], own_ref[q, im, cols]) for q in range(blocks)]
            oth = [(other[d, re, cols], other[d, im, cols]) for d in range(blocks)]
            for p in range(blocks):
                sum_re = sum_im = None
                for q in range(p, blocks):
                    a_re, a_im = own[q]
                    b_re, b_im = oth[q - p]
                    new_re = a_re * b_re + a_im * b_im
                    new_im = a_im * b_re - a_re * b_im
                    sum_re = new_re if sum_re is None else sum_re + new_re
                    sum_im = new_im if sum_im is None else sum_im + new_im
                joint_ref[p, re, cols] = sum_re.astype(BF16)
                joint_ref[p, im, cols] = sum_im.astype(BF16)
        return 0

    lax.fori_loop(0, half // rows, chunk, 0)


def grad_w_kernel(
    blocks, fwd_ref, inv_ref, grad_ref, filt_ref, out_ref, own_ref, other_ref, joint_ref
):
    size = grad_ref.shape[0] // blocks
    for q in range(blocks):
        own_ref[q] = dot(fwd_ref[:, size:], grad_ref[q * size : (q + 1) * size])
        other = dot_nt(fwd_ref[:, size:], filt_ref[:, q * size : (q + 1) * size])
        if q:
            other += dot_nt(fwd_ref[:, :size], filt_ref[:, (q - 1) * size : q * size])
        other_ref[q] = other
    correlate(blocks, own_ref, other_ref, joint_ref)
    for p in range(blocks):
        out_ref[p * size : (p + 1) * size] = dot(inv_ref[...], joint_ref[p]).astype(BF16)


def long_grad_kernel(
    blocks, scale, fwd_ref, inv_ref, grad_ref, long_ref, out_ref, own_ref, other_ref, joint_ref
):
    size = grad_ref.shape[0] // blocks
    for q in range(blocks):
        own_ref[q] = dot(fwd_ref[:, size:], grad_ref[q * size : (q + 1) * size])
        other = dot(fwd_ref[:, size:], long_ref[q * size : (q + 1) * size])
        if q:
            other += dot(fwd_ref[:, :size], long_ref[(q - 1) * size : q * size])
        other_ref[q] = other
    correlate(blocks, own_ref, other_ref, joint_ref)
    for p in range(blocks):
        lags = (dot(inv_ref[...], joint_ref[p]) * scale).T
        out_ref[:, p * size : (p + 1) * size] = lags.astype(BF16)


def total_kernel(scale, parts_ref, out_ref):
    total = parts_ref[0].astype(F32)
    for i in range(1, parts_ref.shape[0]):
        total += parts_ref[i].astype(F32)
    out_ref[...] = (total * scale).astype(BF16)


def call(body, grid, ins, outs, args, flops, scratch=(), vmem=16, name=None):
    moved = sum(a.size * a.dtype.itemsize for a in args)
    moved += sum(math.prod(shape) * jnp.dtype(kind).itemsize for shape, kind, _ in outs)
    result = pl.pallas_call(
        body,
        grid=grid,
        in_specs=ins,
        out_specs=[spec for _, _, spec in outs],
        out_shape=[jax.ShapeDtypeStruct(shape, kind) for shape, kind, _ in outs],
        scratch_shapes=list(scratch),
        compiler_params=pltpu.CompilerParams(vmem_limit_bytes=vmem * MIB),
        cost_estimate=pl.CostEstimate(flops=flops, bytes_accessed=moved, transcendentals=0),
        name=name,
    )(*args)
    return result[0] if len(result) == 1 else result


def whole_spec(array):
    return pl.BlockSpec(array.shape, lambda i: (0,) * array.ndim)


def by_all_to_all(
    incoming, layer_input, pre_gate, mid_gate, long_gate, out_gate, long_filter, mid_filter
):
    sections = lax.axis_size("section")
    devices = lax.axis_size("ctx")
    beta = (2.0 * sections) ** (-0.5)
    tokens, channels = layer_input.shape[1:]
    taps = mid_filter.shape[1]
    seq_len = tokens * devices
    scale = float(seq_len) ** (-0.5)
    owned = channels // devices

    span = tokens + max(tokens, taps)
    fwd = jnp.asarray(forward_table(span, np.arange(span)))
    inv_conv = jnp.asarray(inverse_table(span, tokens + np.arange(tokens)))
    inv_corr = jnp.asarray(inverse_table(span, np.arange(tokens)))
    inv_taps = jnp.asarray(inverse_table(span, tokens - np.arange(taps)))
    size = max(math.gcd(seq_len, 256), seq_len // 8)
    blocks = seq_len // size
    period = 2 * size
    long_fwd = jnp.asarray(forward_table(period, np.arange(-size, size)))
    long_inv = jnp.asarray(inverse_table(period, np.arange(size)))

    wide = max(1024, 2 * owned)
    step = min(256, wide)
    grid = (channels // wide,)
    rows_spec = pl.BlockSpec((tokens, wide), lambda i: (0, i))
    taps_spec = pl.BlockSpec((taps, wide), lambda i: (0, i))
    major_spec = pl.BlockSpec((wide // owned, tokens, owned), lambda i: (i, 0, 0))
    half_major = pl.BlockSpec((wide // owned // 2, taps, owned), lambda i: (i, 0, 0))
    half_shape = (devices // 2, taps, owned)
    rows_shape = (tokens, channels)
    major_shape = (devices, tokens, owned)
    mid_flops = 8 * span * tokens * channels

    tile = math.gcd(owned, 256)
    long_grid = (owned // tile,)
    long_spec = pl.BlockSpec((seq_len, tile), lambda i: (0, i))
    lag_spec = pl.BlockSpec((tile, seq_len), lambda i: (i, 0))
    spectrum = pltpu.VMEM((blocks, period, tile), F32)
    joint = pltpu.VMEM((blocks, period, tile), BF16)
    lanes = -(-tile // 128) * 128
    long_vmem = 2 * (long_fwd.size + long_inv.size) * 2 + 20 * blocks * period * lanes
    long_vmem = -(-long_vmem // MIB) + 6
    long_flops = 4 * period * seq_len * owned

    inputs, gate_pre, gate_mid, gate_long, gate_out = (
        array[0] for array in (layer_input, pre_gate, mid_gate, long_gate, out_gate)
    )
    filter_taps = mid_filter[0]

    adjoint = passed_along(incoming[0], "section", -1)
    mixed_in = call(
        mix_kernel, grid, [rows_spec] * 2, [(rows_shape, BF16, rows_spec)], [inputs, gate_pre],
        2 * tokens * channels, name="mix",
    )
    earlier = shifted(mixed_in, "ctx", 1)
    adjoint, earlier = lax.optimization_barrier((adjoint, earlier))
    grad_z = call(
        functools.partial(grad_z_kernel, beta), grid, [rows_spec] * 2,
        [(major_shape, BF16, major_spec)], [adjoint, gate_out], 2 * tokens * channels, name="gradz",
    )
    grad_z, earlier = lax.optimization_barrier((grad_z, earlier))
    channel_z = lax.all_to_all(grad_z, "ctx", split_axis=0, concat_axis=0, tiled=True)
    long_in = call(
        functools.partial(branch_kernel, beta, step), grid,
        [whole_spec(fwd), whole_spec(inv_conv)] + [rows_spec] * 2 + [taps_spec] + [rows_spec] * 3,
        [(major_shape, BF16, major_spec)],
        [fwd, inv_conv, earlier, mixed_in, filter_taps, inputs, gate_mid, gate_long], mid_flops,
        name="branch",
    )
    channel_z, long_in = lax.optimization_barrier((channel_z, long_in))
    channel_w = lax.all_to_all(long_in, "ctx", split_axis=0, concat_axis=0, tiled=True)
    channel_z = channel_z.reshape(seq_len, owned)
    grad_w = call(
        functools.partial(grad_w_kernel, blocks), long_grid,
        [whole_spec(long_fwd), whole_spec(long_inv), long_spec, lag_spec],
        [((seq_len, owned), BF16, long_spec)], [long_fwd, long_inv, channel_z, long_filter[0]],
        2 * long_flops, [spectrum, spectrum, joint], long_vmem, "gradw",
    )
    grad_w, channel_w = lax.optimization_barrier((grad_w, channel_w))
    returned = lax.all_to_all(
        grad_w.reshape(major_shape), "ctx", split_axis=0, concat_axis=0, tiled=True
    )
    channel_w = channel_w.reshape(seq_len, owned)
    long_grad = call(
        functools.partial(long_grad_kernel, blocks, scale), long_grid,
        [whole_spec(long_fwd), whole_spec(long_inv), long_spec, long_spec],
        [((owned, seq_len), BF16, lag_spec)], [long_fwd, long_inv, channel_z, channel_w],
        2 * long_flops, [spectrum, spectrum, joint], long_vmem, "longgrad",
    )
    returned, long_grad = lax.optimization_barrier((returned, long_grad))
    grad_b = call(
        functools.partial(grad_b_kernel, beta), grid,
        [rows_spec, major_spec] + [rows_spec] * 2, [(rows_shape, BF16, rows_spec)],
        [adjoint, returned, gate_long, gate_mid], 4 * tokens * channels, name="gradb",
    )
    later = shifted(grad_b, "ctx", -1)
    core = (lax.axis_index("ctx") % 2).astype(jnp.int32)[None]
    keep, send = call(
        functools.partial(taps_kernel, step), grid,
        [pl.BlockSpec(memory_space=pltpu.SMEM), whole_spec(fwd), whole_spec(inv_taps)]
        + [rows_spec] * 3,
        [(half_shape, BF16, half_major)] * 2,
        [core, fwd, inv_taps, earlier, mixed_in, grad_b], mid_flops, name="taps",
    )
    partner = lax.ppermute(send, "ctx", [(i, i ^ 1) for i in range(devices)])
    chip_parts = (keep.astype(F32) + partner.astype(F32)).astype(BF16)
    gathered = lax.all_to_all(
        chip_parts, "ctx", split_axis=0, concat_axis=0, tiled=True,
        axis_index_groups=[list(range(c, devices, 2)) for c in range(2)],
    )
    later, _ = lax.optimization_barrier((later, chip_parts))
    input_grad = call(
        functools.partial(input_grad_kernel, step), grid,
        [whole_spec(fwd), whole_spec(inv_corr)] + [rows_spec] * 2 + [taps_spec, rows_spec, major_spec]
        + [rows_spec] * 2,
        [(rows_shape, BF16, rows_spec)],
        [fwd, inv_corr, grad_b, later, filter_taps, adjoint, returned, gate_long, gate_pre],
        mid_flops, name="inputgrad",
    )
    mid_grad = call(
        functools.partial(total_kernel, scale), (1,), [whole_spec(gathered)],
        [((taps, owned), BF16, pl.BlockSpec((taps, owned), lambda i: (0, 0)))], [gathered],
        devices * taps * owned, name="midgrad",
    )
    return (input_grad[None], long_grad[None], mid_grad[None])


def columns(index, width):
    return pl.ds(pl.multiple_of(index * width, width), width)


def pick_kernel(firsts, me_ref, in_ref, *out_refs):
    for first, out_ref in zip(firsts, out_refs):
        width = out_ref.shape[1]
        owned = in_ref.shape[1] // 8
        out_ref[...] = in_ref[:, columns((me_ref[0] ^ first) // (width // owned), width)]


def pieces_z_kernel(beta, first, me_ref, adjoint_ref, gate_ref, *out_refs):
    count = len(out_refs)
    width = out_refs[0].shape[1]
    me = me_ref[0]
    for k in range(count):
        owner = me ^ (first + k)
        part = adjoint_ref[:, columns(owner & (count - 1), width)].astype(F32)
        gate = gate_ref[:, columns(owner, width)].astype(F32)
        out_refs[k][...] = (beta * part * gate).astype(BF16)


def pieces_branch_kernel(
    beta, me_ref, fwd_ref, inv_ref, earlier_ref, mixed_ref, taps_ref, inputs_ref, mid_ref, long_ref,
    signal_ref, filt_ref, *out_refs,
):
    taps = taps_ref.shape[0]
    width = out_refs[0].shape[1]
    me = me_ref[0]
    count = len(out_refs)
    for k in list(range(count // 2, count)) + list(range(count // 2)):
        cols = columns(me ^ k, width)
        signal = dot(fwd_ref[...], stacked(earlier_ref[:, cols], mixed_ref[:, cols]))
        filt = dot(fwd_ref[:, :taps], taps_ref[:, cols])
        signal_ref[:, cols] = signal.astype(BF16)
        filt_ref[:, cols] = filt.astype(BF16)
        branch = dot(inv_ref[...], times(signal, filt))
        resid = inputs_ref[:, cols].astype(F32) + beta * branch * mid_ref[:, cols].astype(F32)
        out_refs[k][...] = (resid * long_ref[:, cols].astype(F32)).astype(BF16)


def spectra(blocks, fwd_ref, array_ref, cols, out_ref):
    size = array_ref.shape[0] // blocks
    for q in range(blocks):
        out_ref[q] = dot(fwd_ref[:, size:], array_ref[q * size : (q + 1) * size, cols])


def extended_spectra(blocks, fwd_ref, array_ref, cols, out_ref):
    size = array_ref.shape[0] // blocks
    out_ref[0] = dot(fwd_ref[:, size:], array_ref[:size, cols])
    for q in range(1, blocks):
        out_ref[q] = dot(fwd_ref[...], array_ref[(q - 1) * size : (q + 1) * size, cols])


def pieces_grad_w_kernel(blocks, count, me_ref, fwd_ref, inv_ref, filt_ref, *refs):
    piece_refs, out_refs = refs[:count][::-1], refs[count : 2 * count]
    whole_ref, own_ref, other_ref, joint_ref, result_ref = refs[2 * count :]
    rows = piece_refs[0].shape[0]
    size = whole_ref.shape[0] // blocks
    tile = joint_ref.shape[2]
    me = me_ref[0]
    for k in range(count):
        whole_ref[columns(me ^ k, rows), :] = piece_refs[k][...]
    for start in range(0, whole_ref.shape[1], tile):
        cols = slice(start, start + tile)
        spectra(blocks, fwd_ref, whole_ref, cols, own_ref)
        other_ref[0] = dot_nt(fwd_ref[:, size:], filt_ref[cols, :size])
        for q in range(1, blocks):
            other_ref[q] = dot_nt(fwd_ref[...], filt_ref[cols, (q - 1) * size : (q + 1) * size])
        correlate(blocks, own_ref, other_ref, joint_ref)
        for p in range(blocks):
            result_ref[p * size : (p + 1) * size, cols] = dot(inv_ref[...], joint_ref[p]).astype(BF16)
    for k in range(count):
        out_refs[k][...] = result_ref[columns(me ^ k, rows), :]


def pieces_long_grad_kernel(blocks, scale, count, me_ref, fwd_ref, inv_ref, grad_ref, *refs):
    piece_refs, out_ref = refs[:count][::-1], refs[count]
    own_ref, other_ref, joint_ref, whole_ref = refs[count + 1 :]
    rows = piece_refs[0].shape[0]
    size = whole_ref.shape[0] // blocks
    tile = joint_ref.shape[2]
    me = me_ref[0]
    for k in range(count):
        whole_ref[columns(me ^ k, rows), :] = piece_refs[k][...]
    for start in range(0, whole_ref.shape[1], tile):
        cols = slice(start, start + tile)
        spectra(blocks, fwd_ref, grad_ref, cols, own_ref)
        extended_spectra(blocks, fwd_ref, whole_ref, cols, other_ref)
        correlate(blocks, own_ref, other_ref, joint_ref)
        for p in range(blocks):
            lags = (dot(inv_ref[...], joint_ref[p]) * scale).T
            out_ref[cols, p * size : (p + 1) * size] = lags.astype(BF16)


def pieces_grad_b_kernel(beta, count, me_ref, near_ref, far_ref, long_ref, gate_ref, *refs):
    piece_refs, (grad_u_ref, grad_b_ref) = refs[:count][::-1], refs[count:]
    width = piece_refs[0].shape[1]
    me = me_ref[0]
    for k in range(count):
        owner = me ^ k
        cols = columns(owner, width)
        adjoint_ref = near_ref if k < count // 2 else far_ref
        adjoint = adjoint_ref[:, columns(owner & (adjoint_ref.shape[1] // width - 1), width)].astype(F32)
        grad_u = adjoint + piece_refs[k][...].astype(F32) * long_ref[:, cols].astype(F32)
        grad_u_ref[:, cols] = grad_u
        grad_b_ref[:, cols] = (beta * grad_u * gate_ref[:, cols].astype(F32)).astype(BF16)


def pieces_taps_kernel(me_ref, fwd_ref, inv_ref, signal_ref, grad_b_ref, keep_ref, send_ref):
    tokens = grad_b_ref.shape[0]
    width = keep_ref.shape[2]
    me = me_ref[0]
    for k in range(2 * keep_ref.shape[0]):
        cols = columns(me ^ k, width)
        grad = dot(fwd_ref[:, :tokens], grad_b_ref[:, cols])
        part = dot(inv_ref[...], times_conj(signal_ref[:, cols].astype(F32), grad)).astype(BF16)
        (send_ref if k % 2 else keep_ref)[k // 2] = part


def pair_kernel(keep_ref, came_ref, *out_refs):
    for m, out_ref in enumerate(out_refs):
        out_ref[...] = (keep_ref[m].astype(F32) + came_ref[m].astype(F32)).astype(BF16)


def pieces_total_kernel(scale, *refs):
    total = refs[0][...].astype(F32)
    for ref in refs[1:-1]:
        total += ref[...].astype(F32)
    refs[-1][...] = (total * scale).astype(BF16)


def pieces_input_grad_kernel(
    step, fwd_ref, inv_ref, grad_b_ref, later_ref, filt_ref, grad_u_ref, pre_ref, out_ref
):
    for start in range(0, grad_b_ref.shape[1], step):
        cols = slice(start, start + step)
        signal = dot(fwd_ref[...], stacked(grad_b_ref[:, cols], later_ref[:, cols]))
        act = dot(inv_ref[...], times_conj(signal, filt_ref[:, cols].astype(F32)))
        value = grad_u_ref[:, cols] + act * pre_ref[:, cols].astype(F32)
        out_ref[:, cols] = value.astype(BF16)


def local(body, outs, args, flops, scratch=(), vmem=24, name=None):
    moved = sum(a.size * a.dtype.itemsize for a in args)
    moved += sum(math.prod(shape) * jnp.dtype(kind).itemsize for shape, kind in outs)
    specs = [
        pl.BlockSpec(memory_space=pltpu.SMEM if a.dtype == jnp.int32 else pltpu.VMEM) for a in args
    ]
    result = pl.pallas_call(
        body,
        in_specs=specs,
        out_specs=[pl.BlockSpec(memory_space=pltpu.VMEM) for _ in outs],
        out_shape=[jax.ShapeDtypeStruct(shape, kind) for shape, kind in outs],
        scratch_shapes=list(scratch),
        compiler_params=pltpu.CompilerParams(vmem_limit_bytes=vmem * MIB),
        cost_estimate=pl.CostEstimate(flops=flops, bytes_accessed=moved, transcendentals=0),
        name=name,
    )(*args)
    return result[0] if len(result) == 1 else result


def swapped(array, k):
    count = lax.axis_size("ctx")
    return lax.ppermute(array, "ctx", [(i, i ^ k) for i in range(count)])


def after(value, *others):
    return lax.optimization_barrier((value, others))[0]


def exchanged(pieces, first=0):
    return [swapped(piece, first + k) if first + k else piece for k, piece in enumerate(pieces)]


def far_pair(pieces, first, *before):
    if before:
        pieces = [after(piece, other) for piece, other in zip(pieces, before)]
    return exchanged(pieces, first)


def by_permutes(
    incoming, layer_input, pre_gate, mid_gate, long_gate, out_gate, long_filter, mid_filter
):
    sections = lax.axis_size("section")
    devices = lax.axis_size("ctx")
    half = devices // 2
    beta = (2.0 * sections) ** (-0.5)
    tokens, channels = layer_input.shape[1:]
    taps = mid_filter.shape[1]
    seq_len = tokens * devices
    scale = float(seq_len) ** (-0.5)
    owned = channels // devices

    span = tokens + max(tokens, taps)
    fwd = jnp.asarray(forward_table(span, np.arange(span)))
    inv_conv = jnp.asarray(inverse_table(span, tokens + np.arange(tokens)))
    inv_corr = jnp.asarray(inverse_table(span, np.arange(tokens)))
    inv_taps = jnp.asarray(inverse_table(span, tokens - np.arange(taps)))
    size = max(math.gcd(seq_len, 256), seq_len // 8)
    blocks = seq_len // size
    period = 2 * size
    long_fwd = jnp.asarray(forward_table(period, np.arange(-size, size)))
    long_inv = jnp.asarray(inverse_table(period, np.arange(size)))
    tile = math.gcd(owned, 256)
    spectrum = pltpu.VMEM((blocks, period, tile), F32)
    joint = pltpu.VMEM((blocks, period, tile), BF16)
    staged = pltpu.VMEM((seq_len, owned), BF16)

    rows_shape = ((tokens, channels), BF16)
    half_shape = ((tokens, channels // 2), BF16)
    piece = ((tokens, owned), BF16)
    tap_piece = ((taps, owned), BF16)
    mid_flops = 8 * span * tokens * channels
    long_flops = 12 * period * seq_len * owned
    few = 4 * tokens * channels

    me = lax.axis_index("ctx").astype(jnp.int32)[None]
    inputs, gate_pre, gate_mid, gate_long, gate_out = (
        array[0] for array in (layer_input, pre_gate, mid_gate, long_gate, out_gate)
    )
    filter_taps = mid_filter[0]

    far = local(functools.partial(pick_kernel, (4,)), [half_shape], [me, incoming[0]], few, name="far")
    far = passed_along(far, "section", -1)
    mixed_in = local(mix_kernel, [rows_shape], [inputs, gate_pre], few, name="mix")
    earlier = shifted(mixed_in, "ctx", 1)
    sent = after(incoming[0], far)
    near = local(functools.partial(pick_kernel, (0,)), [half_shape], [me, sent], few, name="near")
    near = passed_along(near, "section", -1)
    far_z = local(
        functools.partial(pieces_z_kernel, beta, half), [piece] * half, [me, far, gate_out], few, name="farz"
    )
    near_z = local(
        functools.partial(pieces_z_kernel, beta, 0), [piece] * half, [me, near, gate_out], few, name="nearz"
    )
    signal, filt, *pieces_w = local(
        functools.partial(pieces_branch_kernel, beta),
        [((span, channels), BF16)] * 2 + [piece] * devices,
        [me, fwd, inv_conv, after(earlier, near_z), mixed_in, filter_taps, inputs, gate_mid, gate_long],
        mid_flops, name="branch",
    )
    z_6, z_7 = far_pair(far_z[2:], 6)
    z_4, z_5 = far_pair(far_z[:2], 4, z_6, z_7)
    near_z = exchanged(near_z)
    pieces_z = near_z + [z_4, z_5, z_6, z_7]
    w_6, w_7 = far_pair(pieces_w[6:], 6, z_4, z_5)
    near_w = exchanged(pieces_w[:half])
    *pieces_g, channel_z = local(
        functools.partial(pieces_grad_w_kernel, blocks, devices),
        [piece] * devices + [((seq_len, owned), BF16)],
        [me, long_fwd, long_inv, long_filter[0], *pieces_z[::-1]], long_flops,
        [spectrum, spectrum, joint, staged], name="gradw",
    )
    w_4, w_5 = far_pair(pieces_w[4:6], 4, (w_6, near_w, pieces_g[0]), (w_7, near_w, pieces_g[0]))
    pieces_w = near_w + [w_4, w_5, w_6, w_7]
    near_g = exchanged(pieces_g[:half])
    g_6, g_7 = far_pair(pieces_g[6:], 6, (w_4, near_g), (w_5, near_g))
    g_4, g_5 = far_pair(pieces_g[4:6], 4, g_6, g_7)
    pieces_g = [g_7, g_6, g_5, g_4] + near_g[::-1]
    long_grad = local(
        functools.partial(pieces_long_grad_kernel, blocks, scale, devices), [((owned, seq_len), BF16)],
        [me, long_fwd, long_inv, channel_z, *pieces_w[::-1]], long_flops,
        [spectrum, spectrum, joint, staged], name="longgrad",
    )
    pieces_g, long_grad = lax.optimization_barrier((pieces_g, long_grad))
    grad_u, grad_b = local(
        functools.partial(pieces_grad_b_kernel, beta, devices), [((tokens, channels), F32), rows_shape],
        [me, near, far, gate_long, gate_mid, *pieces_g], few, name="gradb",
    )
    later = shifted(grad_b, "ctx", -1)
    keep, send = local(
        pieces_taps_kernel, [((half, taps, owned), BF16)] * 2, [me, fwd, inv_taps, signal, grad_b],
        mid_flops, name="taps",
    )
    sums = local(pair_kernel, [tap_piece] * half, [keep, swapped(send, 1)], few, name="pair")
    sums = [swapped(sums[m], 2 * m) for m in (3, 2, 1)] + [sums[0]]
    later = after(later, sums[-1])
    input_grad = local(
        functools.partial(pieces_input_grad_kernel, 512), [rows_shape],
        [fwd, inv_corr, grad_b, later, filt, grad_u, gate_pre], mid_flops, name="inputgrad",
    )
    sums, input_grad = lax.optimization_barrier((sums, input_grad))
    mid_grad = local(functools.partial(pieces_total_kernel, scale), [tap_piece], sums, few, name="midgrad")
    return (input_grad[None], long_grad[None], mid_grad[None])


def per_device(*arrays):
    devices = lax.axis_size("ctx")
    owned = arrays[0].shape[2] // devices
    if owned % 128 == 0 and devices == 8:
        return by_permutes(*arrays)
    return by_all_to_all(*arrays)


def solution(mesh):
    placed = (
        P("section", "ctx", None),
        P("section", "ctx", None),
        P("section", "ctx", None),
        P("section", "ctx", None),
        P("section", "ctx", None),
        P("section", "ctx", None),
        P("section", "ctx", None),
        P("section", None, None),
    )
    return jax.shard_map(
        per_device,
        mesh=mesh,
        in_specs=placed,
        out_specs=(P("section", "ctx", None), P("section", "ctx", None), P("section", None, "ctx")),
        check_vma=False,
    )
```

```python
import functools
import math

import jax
import jax.numpy as jnp
import numpy as np
from jax import lax
from jax.experimental import pallas as pl
from jax.experimental.pallas import tpu as pltpu
from jax.sharding import PartitionSpec as P

BF16 = jnp.bfloat16
F32 = jnp.float32
MIB = 1024 * 1024


def passed_along(value, axis, steps):
    count = lax.axis_size(axis)
    pairs = [(source, (source + steps) % count) for source in range(count)]
    return lax.ppermute(value, axis, pairs)


def shifted(array, axis, by):
    devices = lax.axis_size(axis)
    pairs = [(i, i + by) for i in range(devices) if 0 <= i + by < devices]
    return lax.ppermute(array, axis, pairs)


def forward_table(period, positions):
    angle = np.pi * np.outer(2 * np.arange(period // 2) + 1, positions) / period
    return np.concatenate([np.cos(angle), -np.sin(angle)], 0).astype(BF16)


def inverse_table(period, positions):
    angle = np.pi * np.outer(positions, 2 * np.arange(period // 2) + 1) / period
    return (np.concatenate([np.cos(angle), -np.sin(angle)], 1) * (2.0 / period)).astype(BF16)


def dot(left, right):
    return jnp.dot(left, right, preferred_element_type=F32)


def dot_nt(left, right):
    return lax.dot_general(left, right, (((1,), (1,)), ((), ())), preferred_element_type=F32)


def stacked(*rows):
    return jnp.concatenate(rows, 0)


def times(left, right):
    half = left.shape[0] // 2
    l_re, l_im, r_re, r_im = left[:half], left[half:], right[:half], right[half:]
    return jnp.concatenate(
        [(l_re * r_re - l_im * r_im).astype(BF16), (l_re * r_im + l_im * r_re).astype(BF16)], 0
    )


def times_conj(left, right):
    half = left.shape[0] // 2
    l_re, l_im, r_re, r_im = left[:half], left[half:], right[:half], right[half:]
    return jnp.concatenate(
        [(l_re * r_re + l_im * r_im).astype(BF16), (l_im * r_re - l_re * r_im).astype(BF16)], 0
    )


def put_columns(out_ref, value, start):
    owned = out_ref.shape[2]
    width = value.shape[1]
    if owned >= width:
        out_ref[start // owned, :, start % owned : start % owned + width] = value
    else:
        for j in range(width // owned):
            out_ref[start // owned + j] = value[:, j * owned : (j + 1) * owned]


def get_columns(in_ref, start, width):
    owned = in_ref.shape[2]
    if owned >= width:
        return in_ref[start // owned, :, start % owned : start % owned + width]
    return jnp.concatenate([in_ref[start // owned + j] for j in range(width // owned)], 1)


def mix_kernel(inputs_ref, gate_ref, out_ref):
    out_ref[...] = (inputs_ref[...].astype(F32) * gate_ref[...].astype(F32)).astype(BF16)


def grad_z_kernel(beta, adjoint_ref, gate_ref, out_ref):
    value = beta * adjoint_ref[...].astype(F32) * gate_ref[...].astype(F32)
    put_columns(out_ref, value.astype(BF16), 0)


def branch_kernel(
    beta, step, fwd_ref, inv_ref, earlier_ref, mixed_ref, taps_ref, inputs_ref, mid_ref, long_ref, out_ref
):
    tokens = mixed_ref.shape[0]
    taps = taps_ref.shape[0]
    for start in range(0, mixed_ref.shape[1], step):
        cols = slice(start, start + step)
        signal = dot(fwd_ref[...], stacked(earlier_ref[:, cols], mixed_ref[:, cols]))
        filt = dot(fwd_ref[:, :taps], taps_ref[:, cols])
        branch = dot(inv_ref[...], times(signal, filt))
        resid = inputs_ref[:, cols].astype(F32) + beta * branch * mid_ref[:, cols].astype(F32)
        value = (resid * long_ref[:, cols].astype(F32)).astype(BF16)
        put_columns(out_ref, value, start)


def grad_b_kernel(beta, adjoint_ref, grad_w_ref, long_ref, mid_ref, out_ref):
    grad_w = get_columns(grad_w_ref, 0, out_ref.shape[1]).astype(F32)
    grad_u = adjoint_ref[...].astype(F32) + grad_w * long_ref[...].astype(F32)
    out_ref[...] = (beta * grad_u * mid_ref[...].astype(F32)).astype(BF16)


def taps_kernel(
    step, core_ref, fwd_ref, inv_ref, earlier_ref, mixed_ref, grad_b_ref, keep_ref, send_ref
):
    tokens = mixed_ref.shape[0]
    owned = keep_ref.shape[2]
    width = min(owned, step)

    def put(even_ref, odd_ref, owner, at, value):
        ref = even_ref if owner % 2 == 0 else odd_ref
        ref[owner // 2, :, at : at + width] = value

    for start in range(0, mixed_ref.shape[1], step):
        cols = slice(start, start + step)
        signal = dot(fwd_ref[...], stacked(earlier_ref[:, cols], mixed_ref[:, cols]))
        grad = dot(fwd_ref[:, :tokens], grad_b_ref[:, cols])
        part = dot(inv_ref[...], times_conj(signal, grad)).astype(BF16)
        for j in range(0, step, width):
            owner, at = divmod(start + j, owned)
            value = part[:, j : j + width]
            pl.when(core_ref[0] == 0)(functools.partial(put, keep_ref, send_ref, owner, at, value))
            pl.when(core_ref[0] == 1)(functools.partial(put, send_ref, keep_ref, owner, at, value))


def input_grad_kernel(
    step, fwd_ref, inv_ref, grad_b_ref, later_ref, taps_ref, adjoint_ref, grad_w_ref, long_ref, pre_ref,
    out_ref,
):
    tokens = grad_b_ref.shape[0]
    taps = taps_ref.shape[0]
    for start in range(0, grad_b_ref.shape[1], step):
        cols = slice(start, start + step)
        grad_w = get_columns(grad_w_ref, start, step).astype(F32)
        grad_u = adjoint_ref[:, cols].astype(F32) + grad_w * long_ref[:, cols].astype(F32)
        signal = dot(fwd_ref[...], stacked(grad_b_ref[:, cols], later_ref[:, cols]))
        filt = dot(fwd_ref[:, :taps], taps_ref[:, cols])
        act = dot(inv_ref[...], times_conj(signal, filt))
        out_ref[:, cols] = (grad_u + act * pre_ref[:, cols].astype(F32)).astype(BF16)


def correlate(blocks, own_ref, other, joint_ref):
    period, width = joint_ref.shape[1:]
    half = period // 2
    rows, lanes = 16, math.gcd(width, 128) if width % 128 == 0 else width

    def chunk(i, _):
        at = pl.multiple_of(i * rows, rows)
        re, im = pl.ds(at, rows), pl.ds(pl.multiple_of(half + at, rows), rows)
        for start in range(0, width, lanes):
            cols = slice(start, start + lanes)
            own = [(own_ref[q, re, cols], own_ref[q, im, cols]) for q in range(blocks)]
            oth = [(other[d, re, cols], other[d, im, cols]) for d in range(blocks)]
            for p in range(blocks):
                sum_re = sum_im = None
                for q in range(p, blocks):
                    a_re, a_im = own[q]
                    b_re, b_im = oth[q - p]
                    new_re = a_re * b_re + a_im * b_im
                    new_im = a_im * b_re - a_re * b_im
                    sum_re = new_re if sum_re is None else sum_re + new_re
                    sum_im = new_im if sum_im is None else sum_im + new_im
                joint_ref[p, re, cols] = sum_re.astype(BF16)
                joint_ref[p, im, cols] = sum_im.astype(BF16)
        return 0

    lax.fori_loop(0, half // rows, chunk, 0)


def grad_w_kernel(
    blocks, fwd_ref, inv_ref, grad_ref, filt_ref, out_ref, own_ref, other_ref, joint_ref
):
    size = grad_ref.shape[0] // blocks
    for q in range(blocks):
        own_ref[q] = dot(fwd_ref[:, size:], grad_ref[q * size : (q + 1) * size])
        other = dot_nt(fwd_ref[:, size:], filt_ref[:, q * size : (q + 1) * size])
        if q:
            other += dot_nt(fwd_ref[:, :size], filt_ref[:, (q - 1) * size : q * size])
        other_ref[q] = other
    correlate(blocks, own_ref, other_ref, joint_ref)
    for p in range(blocks):
        out_ref[p * size : (p + 1) * size] = dot(inv_ref[...], joint_ref[p]).astype(BF16)


def long_grad_kernel(
    blocks, scale, fwd_ref, inv_ref, grad_ref, long_ref, out_ref, own_ref, other_ref, joint_ref
):
    size = grad_ref.shape[0] // blocks
    for q in range(blocks):
        own_ref[q] = dot(fwd_ref[:, size:], grad_ref[q * size : (q + 1) * size])
        other = dot(fwd_ref[:, size:], long_ref[q * size : (q + 1) * size])
        if q:
            other += dot(fwd_ref[:, :size], long_ref[(q - 1) * size : q * size])
        other_ref[q] = other
    correlate(blocks, own_ref, other_ref, joint_ref)
    for p in range(blocks):
        lags = (dot(inv_ref[...], joint_ref[p]) * scale).T
        out_ref[:, p * size : (p + 1) * size] = lags.astype(BF16)


def total_kernel(scale, parts_ref, out_ref):
    total = parts_ref[0].astype(F32)
    for i in range(1, parts_ref.shape[0]):
        total += parts_ref[i].astype(F32)
    out_ref[...] = (total * scale).astype(BF16)


def call(body, grid, ins, outs, args, flops, scratch=(), vmem=16, name=None):
    moved = sum(a.size * a.dtype.itemsize for a in args)
    moved += sum(math.prod(shape) * jnp.dtype(kind).itemsize for shape, kind, _ in outs)
    result = pl.pallas_call(
        body,
        grid=grid,
        in_specs=ins,
        out_specs=[spec for _, _, spec in outs],
        out_shape=[jax.ShapeDtypeStruct(shape, kind) for shape, kind, _ in outs],
        scratch_shapes=list(scratch),
        compiler_params=pltpu.CompilerParams(vmem_limit_bytes=vmem * MIB),
        cost_estimate=pl.CostEstimate(flops=flops, bytes_accessed=moved, transcendentals=0),
        name=name,
    )(*args)
    return result[0] if len(result) == 1 else result


def whole_spec(array):
    return pl.BlockSpec(array.shape, lambda i: (0,) * array.ndim)


def by_all_to_all(
    incoming, layer_input, pre_gate, mid_gate, long_gate, out_gate, long_filter, mid_filter
):
    sections = lax.axis_size("section")
    devices = lax.axis_size("ctx")
    beta = (2.0 * sections) ** (-0.5)
    tokens, channels = layer_input.shape[1:]
    taps = mid_filter.shape[1]
    seq_len = tokens * devices
    scale = float(seq_len) ** (-0.5)
    owned = channels // devices

    span = tokens + max(tokens, taps)
    fwd = jnp.asarray(forward_table(span, np.arange(span)))
    inv_conv = jnp.asarray(inverse_table(span, tokens + np.arange(tokens)))
    inv_corr = jnp.asarray(inverse_table(span, np.arange(tokens)))
    inv_taps = jnp.asarray(inverse_table(span, tokens - np.arange(taps)))
    size = max(math.gcd(seq_len, 256), seq_len // 8)
    blocks = seq_len // size
    period = 2 * size
    long_fwd = jnp.asarray(forward_table(period, np.arange(-size, size)))
    long_inv = jnp.asarray(inverse_table(period, np.arange(size)))

    wide = max(1024, 2 * owned)
    step = min(256, wide)
    grid = (channels // wide,)
    rows_spec = pl.BlockSpec((tokens, wide), lambda i: (0, i))
    taps_spec = pl.BlockSpec((taps, wide), lambda i: (0, i))
    major_spec = pl.BlockSpec((wide // owned, tokens, owned), lambda i: (i, 0, 0))
    half_major = pl.BlockSpec((wide // owned // 2, taps, owned), lambda i: (i, 0, 0))
    half_shape = (devices // 2, taps, owned)
    rows_shape = (tokens, channels)
    major_shape = (devices, tokens, owned)
    mid_flops = 8 * span * tokens * channels

    tile = math.gcd(owned, 256)
    long_grid = (owned // tile,)
    long_spec = pl.BlockSpec((seq_len, tile), lambda i: (0, i))
    lag_spec = pl.BlockSpec((tile, seq_len), lambda i: (i, 0))
    spectrum = pltpu.VMEM((blocks, period, tile), F32)
    joint = pltpu.VMEM((blocks, period, tile), BF16)
    lanes = -(-tile // 128) * 128
    long_vmem = 2 * (long_fwd.size + long_inv.size) * 2 + 20 * blocks * period * lanes
    long_vmem = -(-long_vmem // MIB) + 6
    long_flops = 4 * period * seq_len * owned

    inputs, gate_pre, gate_mid, gate_long, gate_out = (
        array[0] for array in (layer_input, pre_gate, mid_gate, long_gate, out_gate)
    )
    filter_taps = mid_filter[0]

    adjoint = passed_along(incoming[0], "section", -1)
    mixed_in = call(
        mix_kernel, grid, [rows_spec] * 2, [(rows_shape, BF16, rows_spec)], [inputs, gate_pre],
        2 * tokens * channels, name="mix",
    )
    earlier = shifted(mixed_in, "ctx", 1)
    adjoint, earlier = lax.optimization_barrier((adjoint, earlier))
    grad_z = call(
        functools.partial(grad_z_kernel, beta), grid, [rows_spec] * 2,
        [(major_shape, BF16, major_spec)], [adjoint, gate_out], 2 * tokens * channels, name="gradz",
    )
    grad_z, earlier = lax.optimization_barrier((grad_z, earlier))
    channel_z = lax.all_to_all(grad_z, "ctx", split_axis=0, concat_axis=0, tiled=True)
    long_in = call(
        functools.partial(branch_kernel, beta, step), grid,
        [whole_spec(fwd), whole_spec(inv_conv)] + [rows_spec] * 2 + [taps_spec] + [rows_spec] * 3,
        [(major_shape, BF16, major_spec)],
        [fwd, inv_conv, earlier, mixed_in, filter_taps, inputs, gate_mid, gate_long], mid_flops,
        name="branch",
    )
    channel_z, long_in = lax.optimization_barrier((channel_z, long_in))
    channel_w = lax.all_to_all(long_in, "ctx", split_axis=0, concat_axis=0, tiled=True)
    channel_z = channel_z.reshape(seq_len, owned)
    grad_w = call(
        functools.partial(grad_w_kernel, blocks), long_grid,
        [whole_spec(long_fwd), whole_spec(long_inv), long_spec, lag_spec],
        [((seq_len, owned), BF16, long_spec)], [long_fwd, long_inv, channel_z, long_filter[0]],
        2 * long_flops, [spectrum, spectrum, joint], long_vmem, "gradw",
    )
    grad_w, channel_w = lax.optimization_barrier((grad_w, channel_w))
    returned = lax.all_to_all(
        grad_w.reshape(major_shape), "ctx", split_axis=0, concat_axis=0, tiled=True
    )
    channel_w = channel_w.reshape(seq_len, owned)
    long_grad = call(
        functools.partial(long_grad_kernel, blocks, scale), long_grid,
        [whole_spec(long_fwd), whole_spec(long_inv), long_spec, long_spec],
        [((owned, seq_len), BF16, lag_spec)], [long_fwd, long_inv, channel_z, channel_w],
        2 * long_flops, [spectrum, spectrum, joint], long_vmem, "longgrad",
    )
    returned, long_grad = lax.optimization_barrier((returned, long_grad))
    grad_b = call(
        functools.partial(grad_b_kernel, beta), grid,
        [rows_spec, major_spec] + [rows_spec] * 2, [(rows_shape, BF16, rows_spec)],
        [adjoint, returned, gate_long, gate_mid], 4 * tokens * channels, name="gradb",
    )
    later = shifted(grad_b, "ctx", -1)
    core = (lax.axis_index("ctx") % 2).astype(jnp.int32)[None]
    keep, send = call(
        functools.partial(taps_kernel, step), grid,
        [pl.BlockSpec(memory_space=pltpu.SMEM), whole_spec(fwd), whole_spec(inv_taps)]
        + [rows_spec] * 3,
        [(half_shape, BF16, half_major)] * 2,
        [core, fwd, inv_taps, earlier, mixed_in, grad_b], mid_flops, name="taps",
    )
    partner = lax.ppermute(send, "ctx", [(i, i ^ 1) for i in range(devices)])
    chip_parts = (keep.astype(F32) + partner.astype(F32)).astype(BF16)
    gathered = lax.all_to_all(
        chip_parts, "ctx", split_axis=0, concat_axis=0, tiled=True,
        axis_index_groups=[list(range(c, devices, 2)) for c in range(2)],
    )
    later, _ = lax.optimization_barrier((later, chip_parts))
    input_grad = call(
        functools.partial(input_grad_kernel, step), grid,
        [whole_spec(fwd), whole_spec(inv_corr)] + [rows_spec] * 2 + [taps_spec, rows_spec, major_spec]
        + [rows_spec] * 2,
        [(rows_shape, BF16, rows_spec)],
        [fwd, inv_corr, grad_b, later, filter_taps, adjoint, returned, gate_long, gate_pre],
        mid_flops, name="inputgrad",
    )
    mid_grad = call(
        functools.partial(total_kernel, scale), (1,), [whole_spec(gathered)],
        [((taps, owned), BF16, pl.BlockSpec((taps, owned), lambda i: (0, 0)))], [gathered],
        devices * taps * owned, name="midgrad",
    )
    return (input_grad[None], long_grad[None], mid_grad[None])


def columns(index, width):
    return pl.ds(pl.multiple_of(index * width, width), width)


def pick_kernel(firsts, me_ref, in_ref, *out_refs):
    for first, out_ref in zip(firsts, out_refs):
        width = out_ref.shape[1]
        owned = in_ref.shape[1] // 8
        out_ref[...] = in_ref[:, columns((me_ref[0] ^ first) // (width // owned), width)]


def pieces_z_kernel(beta, first, me_ref, adjoint_ref, gate_ref, *out_refs):
    count = len(out_refs)
    width = out_refs[0].shape[1]
    me = me_ref[0]
    for k in range(count):
        owner = me ^ (first + k)
        part = adjoint_ref[:, columns(owner & (count - 1), width)].astype(F32)
        gate = gate_ref[:, columns(owner, width)].astype(F32)
        out_refs[k][...] = (beta * part * gate).astype(BF16)


def pieces_branch_kernel(
    beta, me_ref, fwd_ref, inv_ref, earlier_ref, mixed_ref, taps_ref, inputs_ref, mid_ref, long_ref,
    signal_ref, filt_ref, *out_refs,
):
    taps = taps_ref.shape[0]
    width = out_refs[0].shape[1]
    me = me_ref[0]
    count = len(out_refs)
    for k in list(range(count // 2, count)) + list(range(count // 2)):
        cols = columns(me ^ k, width)
        signal = dot(fwd_ref[...], stacked(earlier_ref[:, cols], mixed_ref[:, cols]))
        filt = dot(fwd_ref[:, :taps], taps_ref[:, cols])
        signal_ref[:, cols] = signal.astype(BF16)
        filt_ref[:, cols] = filt.astype(BF16)
        branch = dot(inv_ref[...], times(signal, filt))
        resid = inputs_ref[:, cols].astype(F32) + beta * branch * mid_ref[:, cols].astype(F32)
        out_refs[k][...] = (resid * long_ref[:, cols].astype(F32)).astype(BF16)


def spectra(blocks, fwd_ref, array_ref, cols, out_ref):
    size = array_ref.shape[0] // blocks
    for q in range(blocks):
        out_ref[q] = dot(fwd_ref[:, size:], array_ref[q * size : (q + 1) * size, cols])


def extended_spectra(blocks, fwd_ref, array_ref, cols, out_ref):
    size = array_ref.shape[0] // blocks
    out_ref[0] = dot(fwd_ref[:, size:], array_ref[:size, cols])
    for q in range(1, blocks):
        out_ref[q] = dot(fwd_ref[...], array_ref[(q - 1) * size : (q + 1) * size, cols])


def pieces_grad_w_kernel(blocks, count, me_ref, fwd_ref, inv_ref, filt_ref, *refs):
    piece_refs, out_refs = refs[:count][::-1], refs[count : 2 * count]
    whole_ref, own_ref, other_ref, joint_ref, result_ref = refs[2 * count :]
    rows = piece_refs[0].shape[0]
    size = whole_ref.shape[0] // blocks
    tile = joint_ref.shape[2]
    me = me_ref[0]
    for k in range(count):
        whole_ref[columns(me ^ k, rows), :] = piece_refs[k][...]
    for start in range(0, whole_ref.shape[1], tile):
        cols = slice(start, start + tile)
        spectra(blocks, fwd_ref, whole_ref, cols, own_ref)
        other_ref[0] = dot_nt(fwd_ref[:, size:], filt_ref[cols, :size])
        for q in range(1, blocks):
            other_ref[q] = dot_nt(fwd_ref[...], filt_ref[cols, (q - 1) * size : (q + 1) * size])
        correlate(blocks, own_ref, other_ref, joint_ref)
        for p in range(blocks):
            result_ref[p * size : (p + 1) * size, cols] = dot(inv_ref[...], joint_ref[p]).astype(BF16)
    for k in range(count):
        out_refs[k][...] = result_ref[columns(me ^ k, rows), :]


def pieces_long_grad_kernel(blocks, scale, count, me_ref, fwd_ref, inv_ref, grad_ref, *refs):
    piece_refs, out_ref = refs[:count][::-1], refs[count]
    own_ref, other_ref, joint_ref, whole_ref = refs[count + 1 :]
    rows = piece_refs[0].shape[0]
    size = whole_ref.shape[0] // blocks
    tile = joint_ref.shape[2]
    me = me_ref[0]
    for k in range(count):
        whole_ref[columns(me ^ k, rows), :] = piece_refs[k][...]
    for start in range(0, whole_ref.shape[1], tile):
        cols = slice(start, start + tile)
        spectra(blocks, fwd_ref, grad_ref, cols, own_ref)
        extended_spectra(blocks, fwd_ref, whole_ref, cols, other_ref)
        correlate(blocks, own_ref, other_ref, joint_ref)
        for p in range(blocks):
            lags = (dot(inv_ref[...], joint_ref[p]) * scale).T
            out_ref[cols, p * size : (p + 1) * size] = lags.astype(BF16)


def pieces_grad_b_kernel(beta, count, me_ref, near_ref, far_ref, long_ref, gate_ref, *refs):
    piece_refs, (grad_u_ref, grad_b_ref) = refs[:count][::-1], refs[count:]
    width = piece_refs[0].shape[1]
    me = me_ref[0]
    for k in range(count):
        owner = me ^ k
        cols = columns(owner, width)
        adjoint_ref = near_ref if k < count // 2 else far_ref
        adjoint = adjoint_ref[:, columns(owner & (adjoint_ref.shape[1] // width - 1), width)].astype(F32)
        grad_u = adjoint + piece_refs[k][...].astype(F32) * long_ref[:, cols].astype(F32)
        grad_u_ref[:, cols] = grad_u
        grad_b_ref[:, cols] = (beta * grad_u * gate_ref[:, cols].astype(F32)).astype(BF16)


def pieces_taps_kernel(me_ref, fwd_ref, inv_ref, signal_ref, grad_b_ref, keep_ref, send_ref):
    tokens = grad_b_ref.shape[0]
    width = keep_ref.shape[2]
    me = me_ref[0]
    for k in range(2 * keep_ref.shape[0]):
        cols = columns(me ^ k, width)
        grad = dot(fwd_ref[:, :tokens], grad_b_ref[:, cols])
        part = dot(inv_ref[...], times_conj(signal_ref[:, cols].astype(F32), grad)).astype(BF16)
        (send_ref if k % 2 else keep_ref)[k // 2] = part


def pair_kernel(keep_ref, came_ref, *out_refs):
    for m, out_ref in enumerate(out_refs):
        out_ref[...] = (keep_ref[m].astype(F32) + came_ref[m].astype(F32)).astype(BF16)


def pieces_total_kernel(scale, *refs):
    total = refs[0][...].astype(F32)
    for ref in refs[1:-1]:
        total += ref[...].astype(F32)
    refs[-1][...] = (total * scale).astype(BF16)


def pieces_input_grad_kernel(
    step, fwd_ref, inv_ref, grad_b_ref, later_ref, filt_ref, grad_u_ref, pre_ref, out_ref
):
    for start in range(0, grad_b_ref.shape[1], step):
        cols = slice(start, start + step)
        signal = dot(fwd_ref[...], stacked(grad_b_ref[:, cols], later_ref[:, cols]))
        act = dot(inv_ref[...], times_conj(signal, filt_ref[:, cols].astype(F32)))
        value = grad_u_ref[:, cols] + act * pre_ref[:, cols].astype(F32)
        out_ref[:, cols] = value.astype(BF16)


def local(body, outs, args, flops, scratch=(), vmem=24, name=None):
    moved = sum(a.size * a.dtype.itemsize for a in args)
    moved += sum(math.prod(shape) * jnp.dtype(kind).itemsize for shape, kind in outs)
    specs = [
        pl.BlockSpec(memory_space=pltpu.SMEM if a.dtype == jnp.int32 else pltpu.VMEM) for a in args
    ]
    result = pl.pallas_call(
        body,
        in_specs=specs,
        out_specs=[pl.BlockSpec(memory_space=pltpu.VMEM) for _ in outs],
        out_shape=[jax.ShapeDtypeStruct(shape, kind) for shape, kind in outs],
        scratch_shapes=list(scratch),
        compiler_params=pltpu.CompilerParams(vmem_limit_bytes=vmem * MIB),
        cost_estimate=pl.CostEstimate(flops=flops, bytes_accessed=moved, transcendentals=0),
        name=name,
    )(*args)
    return result[0] if len(result) == 1 else result


def swapped(array, k):
    count = lax.axis_size("ctx")
    return lax.ppermute(array, "ctx", [(i, i ^ k) for i in range(count)])


def after(value, *others):
    return lax.optimization_barrier((value, others))[0]


def exchanged(pieces, first=0):
    return [swapped(piece, first + k) if first + k else piece for k, piece in enumerate(pieces)]


def far_pair(pieces, first, *before):
    if before:
        pieces = [after(piece, other) for piece, other in zip(pieces, before)]
    return exchanged(pieces, first)


def by_permutes(
    incoming, layer_input, pre_gate, mid_gate, long_gate, out_gate, long_filter, mid_filter
):
    sections = lax.axis_size("section")
    devices = lax.axis_size("ctx")
    half = devices // 2
    beta = (2.0 * sections) ** (-0.5)
    tokens, channels = layer_input.shape[1:]
    taps = mid_filter.shape[1]
    seq_len = tokens * devices
    scale = float(seq_len) ** (-0.5)
    owned = channels // devices

    span = tokens + max(tokens, taps)
    fwd = jnp.asarray(forward_table(span, np.arange(span)))
    inv_conv = jnp.asarray(inverse_table(span, tokens + np.arange(tokens)))
    inv_corr = jnp.asarray(inverse_table(span, np.arange(tokens)))
    inv_taps = jnp.asarray(inverse_table(span, tokens - np.arange(taps)))
    size = max(math.gcd(seq_len, 256), seq_len // 8)
    blocks = seq_len // size
    period = 2 * size
    long_fwd = jnp.asarray(forward_table(period, np.arange(-size, size)))
    long_inv = jnp.asarray(inverse_table(period, np.arange(size)))
    tile = math.gcd(owned, 256)
    spectrum = pltpu.VMEM((blocks, period, tile), F32)
    joint = pltpu.VMEM((blocks, period, tile), BF16)
    staged = pltpu.VMEM((seq_len, owned), BF16)

    rows_shape = ((tokens, channels), BF16)
    half_shape = ((tokens, channels // 2), BF16)
    piece = ((tokens, owned), BF16)
    tap_piece = ((taps, owned), BF16)
    mid_flops = 8 * span * tokens * channels
    long_flops = 12 * period * seq_len * owned
    few = 4 * tokens * channels

    me = lax.axis_index("ctx").astype(jnp.int32)[None]
    inputs, gate_pre, gate_mid, gate_long, gate_out = (
        array[0] for array in (layer_input, pre_gate, mid_gate, long_gate, out_gate)
    )
    filter_taps = mid_filter[0]

    far = local(functools.partial(pick_kernel, (4,)), [half_shape], [me, incoming[0]], few, name="far")
    far = passed_along(far, "section", -1)
    mixed_in = local(mix_kernel, [rows_shape], [inputs, gate_pre], few, name="mix")
    earlier = shifted(mixed_in, "ctx", 1)
    sent = after(incoming[0], far)
    near = local(functools.partial(pick_kernel, (0,)), [half_shape], [me, sent], few, name="near")
    near = passed_along(near, "section", -1)
    far_z = local(
        functools.partial(pieces_z_kernel, beta, half), [piece] * half, [me, far, gate_out], few, name="farz"
    )
    near_z = local(
        functools.partial(pieces_z_kernel, beta, 0), [piece] * half, [me, near, gate_out], few, name="nearz"
    )
    signal, filt, *pieces_w = local(
        functools.partial(pieces_branch_kernel, beta),
        [((span, channels), BF16)] * 2 + [piece] * devices,
        [me, fwd, inv_conv, after(earlier, near_z), mixed_in, filter_taps, inputs, gate_mid, gate_long],
        mid_flops, name="branch",
    )
    z_6, z_7 = far_pair(far_z[2:], 6)
    z_4, z_5 = far_pair(far_z[:2], 4, z_6, z_7)
    near_z = exchanged(near_z)
    pieces_z = near_z + [z_4, z_5, z_6, z_7]
    w_6, w_7 = far_pair(pieces_w[6:], 6, z_4, (z_5, near_z))
    near_w = exchanged(pieces_w[:half])
    *pieces_g, channel_z = local(
        functools.partial(pieces_grad_w_kernel, blocks, devices),
        [piece] * devices + [((seq_len, owned), BF16)],
        [me, long_fwd, long_inv, long_filter[0], *pieces_z[::-1]], long_flops,
        [spectrum, spectrum, joint, staged], name="gradw",
    )
    w_4, w_5 = far_pair(pieces_w[4:6], 4, (w_6, near_w, pieces_g[0]), (w_7, near_w, pieces_g[0]))
    pieces_w = near_w + [w_4, w_5, w_6, w_7]
    near_g = exchanged(pieces_g[:half])
    g_6, g_7 = far_pair(pieces_g[6:], 6, (w_4, near_g), (w_5, near_g))
    g_4, g_5 = far_pair(pieces_g[4:6], 4, g_6, g_7)
    pieces_g = [g_7, g_6, g_5, g_4] + near_g[::-1]
    long_grad = local(
        functools.partial(pieces_long_grad_kernel, blocks, scale, devices), [((owned, seq_len), BF16)],
        [me, long_fwd, long_inv, channel_z, *pieces_w[::-1]], long_flops,
        [spectrum, spectrum, joint, staged], name="longgrad",
    )
    pieces_g, long_grad = lax.optimization_barrier((pieces_g, long_grad))
    grad_u, grad_b = local(
        functools.partial(pieces_grad_b_kernel, beta, devices), [((tokens, channels), F32), rows_shape],
        [me, near, far, gate_long, gate_mid, *pieces_g], few, name="gradb",
    )
    later = shifted(grad_b, "ctx", -1)
    keep, send = local(
        pieces_taps_kernel, [((half, taps, owned), BF16)] * 2, [me, fwd, inv_taps, signal, grad_b],
        mid_flops, name="taps",
    )
    sums = local(pair_kernel, [tap_piece] * half, [keep, swapped(send, 1)], few, name="pair")
    sums = [swapped(sums[m], 2 * m) for m in (3, 2, 1)] + [sums[0]]
    later = after(later, sums[-1])
    input_grad = local(
        functools.partial(pieces_input_grad_kernel, 512), [rows_shape],
        [fwd, inv_corr, grad_b, later, filt, grad_u, gate_pre], mid_flops, name="inputgrad",
    )
    sums, input_grad = lax.optimization_barrier((sums, input_grad))
    mid_grad = local(functools.partial(pieces_total_kernel, scale), [tap_piece], sums, few, name="midgrad")
    return (input_grad[None], long_grad[None], mid_grad[None])


def per_device(*arrays):
    devices = lax.axis_size("ctx")
    owned = arrays[0].shape[2] // devices
    if owned % 128 == 0 and devices == 8:
        return by_permutes(*arrays)
    return by_all_to_all(*arrays)


def solution(mesh):
    placed = (
        P("section", "ctx", None),
        P("section", "ctx", None),
        P("section", "ctx", None),
        P("section", "ctx", None),
        P("section", "ctx", None),
        P("section", "ctx", None),
        P("section", "ctx", None),
        P("section", None, None),
    )
    return jax.shard_map(
        per_device,
        mesh=mesh,
        in_specs=placed,
        out_specs=(P("section", "ctx", None), P("section", "ctx", None), P("section", None, "ctx")),
        check_vma=False,
    )
```
